32 devices in a mesh: member: 8 (over y, x, core), tile: 4 (over z).
Axes of the slice: x: 2, y: 2, z: 4, core: 2. Of those that a mesh axis runs over, the one named last changes fastest.
Arguments:
- perturbations: bfloat16 [64, 2, 5, 8, 8, 512], P('member', None, None, None, None, 'tile'), may hold values from -6 to 6
- gradient_store: float32 [2, 5, 8, 8, 512], P(None, None, None, 'member', 'tile'), may hold values from -6 to 6
- diffusivity: float32 [8, 8, 512], P(None, None, 'tile'), may hold values from 0.2 to 0.4
- slab_owner: int32 [8], replicated, may hold values from 0 to 7, each once
Outputs:
- increment_store: float32 [2, 5, 8, 8, 512], P(None, None, None, 'member', 'tile')
The draws below stay inside these ranges and needn't reach their ends.
Inputs may be any that keep to these rules, and one draw needn't show every extreme that they name: `slab_owner`: each member index holds exactly one slab.
All inputs are finite; a program needn't handle non-finite values.
Results may differ from the reference program's by a relative error of at most 0.0003.
Values sent between devices are 32-bit elements; how exact they have to be, the bound alone decides.
No kernel may reach another device: no remote copies, remote signals or barrier semaphores. Data moves between devices by JAX's collectives and lax.ppermute only.
A program may use at most 128 MiB of HBM per device.

```python
import math
import jax
import jax.numpy as jnp
from jax import lax

SLOTS = 2
VARS = 5
NZ = 8
SWEEPS = 10
YSLAB = 1
MEMBERS = 64
NX = 512
NY = 8
N_MEMBER = 8


def strengthened(array, own_key, source, target, parts, factor):
    owner, partner = [(jnp.arange(array.shape[dim]) // (array.shape[dim] // parts)).reshape([-1 if axis == dim else 1 for axis in range(array.ndim)]) for dim in (source, target)]
    chosen = jax.random.permutation(own_key, parts)[partner]
    strong = (owner == chosen) | (owner == (partner + parts // 2) % parts)
    return jnp.where(strong, factor * array, array)


def level_of(own_key, extent, split, smallest, largest):
    gain, own = 1.0, jax.random.fold_in(own_key, 6)
    for position, blocks in split:
        heights = jnp.exp(jax.random.uniform(jax.random.fold_in(own, position), (blocks,), jnp.float32, smallest / len(split), largest / len(split)))
        gain = gain * jnp.repeat(heights, extent[position] // blocks).reshape([-1 if axis == position else 1 for axis in range(len(extent))])
    return gain


def normal_values(stream_key, extent, spread, most, pieces=(), kind=jnp.bfloat16):
    entries = jax.random.normal(stream_key, extent, jnp.float32) * spread
    if len(pieces) > 0:
        entries = level_of(stream_key, extent, pieces, -0.22, 0.18) * entries
    return jnp.clip(entries, min=-most, max=most).astype(kind)


def bell_draw_with(key, extent, scale, reach, cuts, heavy, kind=jnp.bfloat16):
    drawn = scale * jax.random.normal(key, extent, jnp.float32)
    if cuts:
        drawn = drawn * level_of(key, extent, cuts, -0.22, 0.18)
    return jnp.clip(strengthened(drawn, jax.random.fold_in(key, 3), *heavy), -reach, reach).astype(kind)


def setup_inputs(seed: int = 0) -> dict:
    key_of = jax.random.split(jax.random.key(seed), 5)
    return {
        "perturbations": bell_draw_with(key_of[0], (MEMBERS, SLOTS, VARS, NZ, NY, NX), 1.0, 6.0, ((0, 8), (5, 4)), (0, 4, 8, 2.0)),
        "gradient_store": normal_values(key_of[1], (SLOTS, VARS, NZ, NY, NX), 1.0, 6.0, ((3, 8), (4, 4)), jnp.float32),
        "diffusivity": jnp.clip(jnp.exp(math.log(0.4) - 0.6931472 * jax.random.uniform(key_of[2], (NZ, NY, NX), jnp.float32) ** level_of(key_of[2], (NZ, NY, NX), ((2, 4),), -0.2, 0.2)), 0.2, 0.4),
        "slab_owner": jax.random.permutation(key_of[3], N_MEMBER).astype(jnp.int32),
    }


def neighbours(grid_field):
    count = grid_field.ndim
    widths_y = [(0, 0)] * (count - 2) + [(1, 1), (0, 0)]
    widths_z = [(0, 0)] * (count - 3) + [(1, 1), (0, 0), (0, 0)]
    padded_y = jnp.pad(grid_field, widths_y)
    padded_z = jnp.pad(grid_field, widths_z)
    return padded_y[..., :-2, :] + padded_y[..., 2:, :] + padded_z[..., :-2, :, :] + padded_z[..., 2:, :, :]


def diffuse(values, coefficient):
    scaled = coefficient * values
    centre = values[..., 1:-1]
    coeff_mid = coefficient[..., 1:-1]
    scaled_mid = scaled[..., 1:-1]
    inflow = scaled[..., :-2] + scaled[..., 2:] + neighbours(scaled_mid)
    outflow = coefficient[..., :-2] + coefficient[..., 2:] + neighbours(coeff_mid)
    return centre + coeff_mid * (inflow - outflow * centre)


def block_rows(slab_owner, slab_rows):
    offsets = jnp.arange(slab_rows, dtype=jnp.int32)
    return (slab_owner.astype(jnp.int32)[:, None] * slab_rows + offsets[None, :]).reshape(-1)


def reference(perturbations, gradient_store, diffusivity, slab_owner):
    true_rows = block_rows(slab_owner, YSLAB)
    gradient = jnp.take(gradient_store, true_rows, axis=3)
    coeff_ext = jnp.pad(diffusivity, ((0, 0), (0, 0), (1, 1)))

    def one_sweep(sweep_index, field_state):
        return diffuse(jnp.pad(field_state, ((0, 0), (0, 0), (1, 1))), coeff_ext)

    def member_step(running, member):
        member_float = member.astype(jnp.float32)
        weighted = jnp.sum(member_float * gradient, axis=(0, 1))
        local_field = lax.fori_loop(0, SWEEPS, one_sweep, weighted)
        return running + member_float * local_field[None, None], None

    start_sum = jnp.zeros((SLOTS, VARS, NZ, NY, NX), jnp.float32)
    running, unused = lax.scan(member_step, start_sum, perturbations)
    increment = running * (1.0 / (MEMBERS - 1))
    store_rows = block_rows(jnp.argsort(slab_owner).astype(jnp.int32), YSLAB)
    return jnp.take(increment, store_rows, axis=3)
```

```python
import functools

import jax
import jax.numpy as jnp
from jax import lax
from jax.experimental import pallas as pl
from jax.experimental.pallas import tpu as pltpu
from jax.sharding import PartitionSpec as P

SWEEPS = 10
GROUPS = 4
VMEM_LIMIT = 48 * 1024 * 1024


def lane_roll(value, shift):
    shift = shift % value.shape[-1]
    return value if shift == 0 else pltpu.roll(value, shift, 1)


def lane_index(shape):
    return lax.broadcasted_iota(jnp.int32, shape, 1)


def pick(values, which):
    result = values[0]
    for index in range(1, len(values)):
        result = jnp.where(which == index, values[index], result)
    return result


def spread(row, rows):
    return jnp.broadcast_to(row, (rows, row.shape[-1]))


def own_strip(near, far):
    lanes = near.shape[-1]
    part = lanes // GROUPS
    group = lane_index(near.shape) // part
    return pick(
        [
            lane_roll(near, SWEEPS),
            lane_roll(near, 2 * part - SWEEPS),
            lane_roll(far, 2 * part + SWEEPS),
            lane_roll(far, lanes - SWEEPS),
        ],
        group,
    )


def packed_edges(strips):
    lanes = strips[0].shape[-1]
    half = lanes // 2
    block = half // len(strips)
    slot = (lane_index(strips[0].shape) % half) // block
    to_right = pick([lane_roll(s, i * block) for i, s in enumerate(strips)], slot)
    to_left = pick([lane_roll(s, (i + 1) * block - half) for i, s in enumerate(strips)], slot)
    return to_right, to_left


def joined_strip(own, from_left, from_right, slot, block):
    lanes = own.shape[-1]
    half = lanes // 2
    place = lane_index(own.shape) % half
    left = lane_roll(from_left, -slot * block)
    right = lane_roll(from_right, half - (slot + 1) * block)
    return jnp.where(place < SWEEPS, left, jnp.where(place >= half - SWEEPS, right, own))


def total(terms):
    terms = list(terms)
    while len(terms) > 1:
        terms = [
            terms[i] + terms[i + 1] if i + 1 < len(terms) else terms[i]
            for i in range(0, len(terms), 2)
        ]
    return terms[0]


def neighbour_total(read, level, row, levels, rows, folded):
    here = read(level, row)
    terms = [lane_roll(here, 1), lane_roll(here, -1)]
    if row > 0:
        terms.append(read(level, row - 1))
    if row < rows - 1:
        terms.append(read(level, row + 1))
    elif folded:
        terms.append(lane_roll(here, here.shape[-1] // 2))
    if level > 0:
        terms.append(read(level - 1, row))
    if level < levels - 1:
        terms.append(read(level + 1, row))
    return here, total(terms)


def sweep(source, target, keep_ref, square_ref, levels, rows, members, folded):
    def read(level, row):
        return source[level, row]

    for level in range(levels):
        for row in range(rows):
            here, around = neighbour_total(read, level, row, levels, rows, folded)
            keep = keep_ref[level, pl.ds(row, 1), :]
            square = square_ref[level, pl.ds(row, 1), :]
            target[level, row] = keep * here + square * around


def all_sweeps(first, second, keep_ref, square_ref, levels, rows, members, folded):
    def pair(index, carry):
        sweep(first, second, keep_ref, square_ref, levels, rows, members, folded)
        sweep(second, first, keep_ref, square_ref, levels, rows, members, folded)
        return carry

    lax.fori_loop(0, SWEEPS // 2, pair, 0)


def weigh_kernel(
    owner_ref, gathered_ref, pert_ref, coeff_ref, field_ref, strip_ref, right_ref, left_ref, grad_ref
):
    members, terms, levels, rows, lanes = pert_ref.shape
    slab_rows = gathered_ref.shape[2]
    folded_rows = rows // 2
    slots = min(4, folded_rows)
    packs = folded_rows // slots
    for slab in range(rows // slab_rows):
        owner = owner_ref[slab]
        for term in range(terms):
            for inner in range(slab_rows):
                row = slab * slab_rows + inner
                grad_ref[pl.ds(term * levels * rows + row, levels, stride=rows), :] = gathered_ref[
                    owner, term, inner
                ]

    def weigh_level(level, carry):
        base = level * rows
        coeff = coeff_ref[level]
        for member in range(members):
            weighted = None
            for term in range(terms):
                start = pl.multiple_of(term * levels * rows + base, rows)
                piece = pert_ref[member, term, level].astype(jnp.float32) * grad_ref[
                    pl.ds(start, rows), :
                ]
                weighted = piece if weighted is None else weighted + piece
            field_ref[pl.ds(base * members + member, rows, stride=members), :] = coeff * weighted
        return carry

    lax.fori_loop(0, levels, weigh_level, 0)

    def field_at(level, row):
        return field_ref[pl.ds((level * rows + row) * members, members), :]

    for level in range(levels):
        for pack in range(packs):
            strips, coeffs = [], []
            for slot in range(slots):
                row = pack * slots + slot
                strip = own_strip(field_at(level, row), field_at(level, rows - 1 - row))
                strip_ref[level, row] = strip
                strips.append(strip)
                coeffs.append(
                    own_strip(
                        spread(coeff_ref[level, pl.ds(row, 1), :], 8),
                        spread(coeff_ref[level, pl.ds(rows - 1 - row, 1), :], 8),
                    )
                )
            place = level * packs + pack
            for ref, packed, coeff_packed in zip(
                (right_ref, left_ref), packed_edges(strips), packed_edges(coeffs)
            ):
                ref[pl.ds(place * members, members), :] = packed
                ref[pl.ds(levels * packs * members + place, 1), :] = coeff_packed[0:1]


def interior_kernel(field_ref, coeff_ref, out_ref, other_ref, keep_ref, square_ref, inverse_ref):
    levels, rows, members, lanes = field_ref.shape
    row_index = lax.broadcasted_iota(jnp.int32, (rows, lanes), 0)
    for level in range(levels):
        here = coeff_ref[level]
        terms = [
            lane_roll(here, 1),
            lane_roll(here, -1),
            jnp.where(row_index > 0, pltpu.roll(here, 1, 0), 0.0),
            jnp.where(row_index < rows - 1, pltpu.roll(here, rows - 1, 0), 0.0),
        ]
        if level > 0:
            terms.append(coeff_ref[level - 1])
        if level < levels - 1:
            terms.append(coeff_ref[level + 1])
        keep_ref[level] = 1.0 - here * total(terms)
        square_ref[level] = here * here
        inverse_ref[level] = 1.0 / here
    sweep(field_ref, other_ref, keep_ref, square_ref, levels, rows, members, False)
    sweep(other_ref, out_ref, keep_ref, square_ref, levels, rows, members, False)

    def pair(index, carry):
        sweep(out_ref, other_ref, keep_ref, square_ref, levels, rows, members, False)
        sweep(other_ref, out_ref, keep_ref, square_ref, levels, rows, members, False)
        return carry

    lax.fori_loop(0, SWEEPS // 2 - 1, pair, 0)
    for level in range(levels):
        for row in range(rows):
            out_ref[level, row] = out_ref[level, row] * inverse_ref[level, pl.ds(row, 1), :]


def finish_kernel(
    owner_ref,
    pert_ref,
    coeff_ref,
    interior_ref,
    strip_ref,
    from_left_ref,
    from_right_ref,
    out_ref,
    first_ref,
    second_ref,
    coeff_strip_ref,
    keep_ref,
    square_ref,
    local_ref,
    sum_ref,
):
    members, terms, levels, rows, lanes = pert_ref.shape
    slab_rows = out_ref.shape[2]
    folded_rows = rows // 2
    slots = min(4, folded_rows)
    packs = folded_rows // slots
    half = lanes // 2
    block = half // slots
    edge = SWEEPS
    for level in range(levels):
        for pack in range(packs):
            place = level * packs + pack
            left = from_left_ref[pl.ds(place * members, members), :]
            right = from_right_ref[pl.ds(place * members, members), :]
            coeff_place = levels * packs * members + place
            coeff_left = spread(from_left_ref[pl.ds(coeff_place, 1), :], 8)
            coeff_right = spread(from_right_ref[pl.ds(coeff_place, 1), :], 8)
            for slot in range(slots):
                row = pack * slots + slot
                first_ref[level, row] = joined_strip(
                    strip_ref[level, row], left, right, slot, block
                )
                own = own_strip(
                    spread(coeff_ref[level, pl.ds(row, 1), :], 8),
                    spread(coeff_ref[level, pl.ds(rows - 1 - row, 1), :], 8),
                )
                coeff_strip_ref[level, row] = joined_strip(own, coeff_left, coeff_right, slot, block)

    def coeff_at(level, row):
        return coeff_strip_ref[level, row]

    for level in range(levels):
        for row in range(folded_rows):
            here, around = neighbour_total(coeff_at, level, row, levels, folded_rows, True)
            keep_ref[level, pl.ds(row, 1), :] = (1.0 - here * around)[0:1]
            square_ref[level, pl.ds(row, 1), :] = (here * here)[0:1]
    all_sweeps(first_ref, second_ref, keep_ref, square_ref, levels, folded_rows, members, True)
    lane = lane_index((members, lanes))
    for level in range(levels):
        for row in range(folded_rows):
            coeff = coeff_strip_ref[level, row][0:1]
            final = first_ref[level, row] / jnp.where(coeff > 0.0, coeff, 1.0)
            for target, before, after in (
                (row, -edge, edge - half),
                (rows - 1 - row, -edge - half, edge),
            ):
                start = lane_roll(final, before)
                stop = lane_roll(final, after)
                inner = interior_ref[level, target]
                merged = jnp.where(
                    lane < edge, start, jnp.where(lane >= lanes - edge, stop, inner)
                )
                local_ref[pl.ds((level * rows + target) * members, members), :] = merged

    def add_level(level, carry):
        base = level * rows
        fields = [
            local_ref[pl.ds(base * members + member, rows, stride=members), :]
            for member in range(members)
        ]
        for term in range(terms):
            result = None
            for member in range(members):
                piece = pert_ref[member, term, level].astype(jnp.float32) * fields[member]
                result = piece if result is None else result + piece
            start = pl.multiple_of(term * levels * rows + base, rows)
            sum_ref[pl.ds(start, rows), :] = result
        return carry

    lax.fori_loop(0, levels, add_level, 0)
    for slab in range(rows // slab_rows):
        owner = owner_ref[slab]
        for term in range(terms):
            for inner in range(slab_rows):
                row = slab * slab_rows + inner
                out_ref[owner, term, inner] = sum_ref[
                    pl.ds(term * levels * rows + row, levels, stride=rows), :
                ]


def whole(memory_space=pltpu.VMEM):
    return pl.BlockSpec(memory_space=memory_space)


def body(perturbations, gradient_store, diffusivity, slab_owner):
    members, slots, variables, levels, rows, lanes = perturbations.shape
    terms = slots * variables
    n_member = lax.axis_size("member")
    n_tile = lax.axis_size("tile")
    slab_rows = gradient_store.shape[3]
    folded_rows = rows // 2
    packs = folded_rows // min(4, folded_rows)
    edge_rows = levels * packs * (members + 1)
    f32 = jnp.float32
    params = pltpu.CompilerParams(vmem_limit_bytes=VMEM_LIMIT)

    pert = perturbations.reshape(members, terms, levels, rows, lanes)
    slab = gradient_store.reshape(terms, levels, slab_rows, lanes).swapaxes(1, 2)
    gathered = lax.all_gather(slab, "member", axis=0, tiled=False)

    field, strip, to_right, to_left = pl.pallas_call(
        weigh_kernel,
        out_shape=(
            jax.ShapeDtypeStruct((levels * rows * members, lanes), f32),
            jax.ShapeDtypeStruct((levels, folded_rows, members, lanes), f32),
            jax.ShapeDtypeStruct((edge_rows, lanes), f32),
            jax.ShapeDtypeStruct((edge_rows, lanes), f32),
        ),
        in_specs=[whole(pltpu.SMEM), whole(), whole(), whole()],
        out_specs=(whole(),) * 4,
        scratch_shapes=[pltpu.VMEM((terms * levels * rows, lanes), f32)],
        compiler_params=params,
        name="weigh",
    )(slab_owner, gathered, pert, diffusivity)

    up = [(i, i + 1) for i in range(n_tile - 1)]
    down = [(i + 1, i) for i in range(n_tile - 1)]
    from_left = lax.ppermute(to_right, "tile", up)
    from_right = lax.ppermute(to_left, "tile", down)

    interior = pl.pallas_call(
        interior_kernel,
        out_shape=jax.ShapeDtypeStruct((levels, rows, members, lanes), f32),
        in_specs=[whole(), whole()],
        out_specs=whole(),
        scratch_shapes=[
            pltpu.VMEM((levels, rows, members, lanes), f32),
            pltpu.VMEM((levels, rows, lanes), f32),
            pltpu.VMEM((levels, rows, lanes), f32),
            pltpu.VMEM((levels, rows, lanes), f32),
        ],
        compiler_params=params,
        cost_estimate=pl.CostEstimate(
            flops=SWEEPS * 8 * levels * rows * members * lanes,
            bytes_accessed=8 * levels * rows * members * lanes,
            transcendentals=0,
        ),
        name="interior",
    )(field.reshape(levels, rows, members, lanes), diffusivity)

    sums = pl.pallas_call(
        finish_kernel,
        out_shape=jax.ShapeDtypeStruct((n_member, terms, slab_rows, levels, lanes), f32),
        in_specs=[whole(pltpu.SMEM)] + [whole()] * 6,
        out_specs=whole(),
        scratch_shapes=[
            pltpu.VMEM((levels, folded_rows, members, lanes), f32),
            pltpu.VMEM((levels, folded_rows, members, lanes), f32),
            pltpu.VMEM((levels, folded_rows, 8, lanes), f32),
            pltpu.VMEM((levels, folded_rows, lanes), f32),
            pltpu.VMEM((levels, folded_rows, lanes), f32),
            pltpu.VMEM((levels * rows * members, lanes), f32),
            pltpu.VMEM((terms * levels * rows, lanes), f32),
        ],
        compiler_params=params,
        name="finish",
    )(slab_owner, pert, diffusivity, interior, strip, from_left, from_right)

    received = lax.all_to_all(sums, "member", 0, 0, tiled=True)
    norm_factor = 1.0 / (members * n_member - 1)
    owned = jnp.sum(received, axis=0) * norm_factor
    return owned.swapaxes(1, 2).reshape(slots, variables, levels, slab_rows, lanes)


def solution(mesh):
    in_specs = (
        P("member", None, None, None, None, "tile"),
        P(None, None, None, "member", "tile"),
        P(None, None, "tile"),
        P(),
    )
    out_specs = P(None, None, None, "member", "tile")
    return jax.shard_map(body, mesh=mesh, in_specs=in_specs, out_specs=out_specs, check_vma=False)
```

```python
import functools

import jax
import jax.numpy as jnp
from jax import lax
from jax.experimental import pallas as pl
from jax.experimental.pallas import tpu as pltpu
from jax.sharding import PartitionSpec as P

SWEEPS = 10
GROUPS = 4
VMEM_LIMIT = 48 * 1024 * 1024


def lane_roll(value, shift):
    shift = shift % value.shape[-1]
    return value if shift == 0 else pltpu.roll(value, shift, 1)


def lane_index(shape):
    return lax.broadcasted_iota(jnp.int32, shape, 1)


def pick(values, which):
    result = values[0]
    for index in range(1, len(values)):
        result = jnp.where(which == index, values[index], result)
    return result


def spread(row, rows):
    return jnp.broadcast_to(row, (rows, row.shape[-1]))


def own_strip(near, far):
    lanes = near.shape[-1]
    part = lanes // GROUPS
    group = lane_index(near.shape) // part
    return pick(
        [
            lane_roll(near, SWEEPS),
            lane_roll(near, 2 * part - SWEEPS),
            lane_roll(far, 2 * part + SWEEPS),
            lane_roll(far, lanes - SWEEPS),
        ],
        group,
    )


def packed_edges(strips):
    lanes = strips[0].shape[-1]
    half = lanes // 2
    block = half // len(strips)
    slot = (lane_index(strips[0].shape) % half) // block
    to_right = pick([lane_roll(s, i * block) for i, s in enumerate(strips)], slot)
    to_left = pick([lane_roll(s, (i + 1) * block - half) for i, s in enumerate(strips)], slot)
    return to_right, to_left


def joined_strip(own, from_left, from_right, slot, block):
    lanes = own.shape[-1]
    half = lanes // 2
    place = lane_index(own.shape) % half
    left = lane_roll(from_left, -slot * block)
    right = lane_roll(from_right, half - (slot + 1) * block)
    return jnp.where(place < SWEEPS, left, jnp.where(place >= half - SWEEPS, right, own))


def total(terms):
    terms = list(terms)
    while len(terms) > 1:
        terms = [
            terms[i] + terms[i + 1] if i + 1 < len(terms) else terms[i]
            for i in range(0, len(terms), 2)
        ]
    return terms[0]


def neighbour_total(read, level, row, levels, rows, folded):
    here = read(level, row)
    terms = [lane_roll(here, 1), lane_roll(here, -1)]
    if row > 0:
        terms.append(read(level, row - 1))
    if row < rows - 1:
        terms.append(read(level, row + 1))
    elif folded:
        terms.append(lane_roll(here, here.shape[-1] // 2))
    if level > 0:
        terms.append(read(level - 1, row))
    if level < levels - 1:
        terms.append(read(level + 1, row))
    return here, total(terms)


def sweep(source, target, keep_ref, square_ref, levels, rows, members, folded):
    def read(level, row):
        return source[level, row]

    for level in range(levels):
        for row in range(rows):
            here, around = neighbour_total(read, level, row, levels, rows, folded)
            keep = keep_ref[level, pl.ds(row, 1), :]
            square = square_ref[level, pl.ds(row, 1), :]
            target[level, row] = keep * here + square * around


def all_sweeps(first, second, keep_ref, square_ref, levels, rows, members, folded):
    def pair(index, carry):
        sweep(first, second, keep_ref, square_ref, levels, rows, members, folded)
        sweep(second, first, keep_ref, square_ref, levels, rows, members, folded)
        return carry

    lax.fori_loop(0, SWEEPS // 2, pair, 0)


def weigh_kernel(
    owner_ref, gathered_ref, pert_ref, coeff_ref, field_ref, strip_ref, edge_ref, grad_ref
):
    tile = lax.axis_index("tile")
    right_ref = edge_ref.at[jnp.minimum(tile + 1, edge_ref.shape[0] - 1)]
    left_ref = edge_ref.at[jnp.maximum(tile - 1, 0)]
    members, terms, levels, rows, lanes = pert_ref.shape
    slab_rows = gathered_ref.shape[2]
    folded_rows = rows // 2
    slots = min(4, folded_rows)
    packs = folded_rows // slots
    for slab in range(rows // slab_rows):
        owner = owner_ref[slab]
        for term in range(terms):
            for inner in range(slab_rows):
                row = slab * slab_rows + inner
                grad_ref[pl.ds(term * levels * rows + row, levels, stride=rows), :] = gathered_ref[
                    owner, term, inner
                ]

    def weigh_level(level, carry):
        base = level * rows
        coeff = coeff_ref[level]
        for member in range(members):
            weighted = None
            for term in range(terms):
                start = pl.multiple_of(term * levels * rows + base, rows)
                piece = pert_ref[member, term, level].astype(jnp.float32) * grad_ref[
                    pl.ds(start, rows), :
                ]
                weighted = piece if weighted is None else weighted + piece
            field_ref[pl.ds(base * members + member, rows, stride=members), :] = coeff * weighted
        return carry

    lax.fori_loop(0, levels, weigh_level, 0)

    def field_at(level, row):
        return field_ref[pl.ds((level * rows + row) * members, members), :]

    for level in range(levels):
        for pack in range(packs):
            strips, coeffs = [], []
            for slot in range(slots):
                row = pack * slots + slot
                strip = own_strip(field_at(level, row), field_at(level, rows - 1 - row))
                strip_ref[level, row] = strip
                strips.append(strip)
                coeffs.append(
                    own_strip(
                        spread(coeff_ref[level, pl.ds(row, 1), :], 8),
                        spread(coeff_ref[level, pl.ds(rows - 1 - row, 1), :], 8),
                    )
                )
            place = level * packs + pack
            for ref, packed, coeff_packed in zip(
                (right_ref, left_ref), packed_edges(strips), packed_edges(coeffs)
            ):
                ref[pl.ds(place * members, members), :] = packed
                ref[pl.ds(levels * packs * members + place, 1), :] = coeff_packed[0:1]


def interior_kernel(field_ref, coeff_ref, out_ref, other_ref, keep_ref, square_ref, inverse_ref):
    levels, rows, members, lanes = field_ref.shape
    row_index = lax.broadcasted_iota(jnp.int32, (rows, lanes), 0)
    for level in range(levels):
        here = coeff_ref[level]
        terms = [
            lane_roll(here, 1),
            lane_roll(here, -1),
            jnp.where(row_index > 0, pltpu.roll(here, 1, 0), 0.0),
            jnp.where(row_index < rows - 1, pltpu.roll(here, rows - 1, 0), 0.0),
        ]
        if level > 0:
            terms.append(coeff_ref[level - 1])
        if level < levels - 1:
            terms.append(coeff_ref[level + 1])
        keep_ref[level] = 1.0 - here * total(terms)
        square_ref[level] = here * here
        inverse_ref[level] = 1.0 / here
    sweep(field_ref, other_ref, keep_ref, square_ref, levels, rows, members, False)
    sweep(other_ref, out_ref, keep_ref, square_ref, levels, rows, members, False)

    def pair(index, carry):
        sweep(out_ref, other_ref, keep_ref, square_ref, levels, rows, members, False)
        sweep(other_ref, out_ref, keep_ref, square_ref, levels, rows, members, False)
        return carry

    lax.fori_loop(0, SWEEPS // 2 - 1, pair, 0)
    for level in range(levels):
        for row in range(rows):
            out_ref[level, row] = out_ref[level, row] * inverse_ref[level, pl.ds(row, 1), :]


def finish_kernel(
    owner_ref,
    pert_ref,
    coeff_ref,
    interior_ref,
    strip_ref,
    edge_ref,
    out_ref,
    first_ref,
    second_ref,
    coeff_strip_ref,
    keep_ref,
    square_ref,
    local_ref,
    sum_ref,
):
    members, terms, levels, rows, lanes = pert_ref.shape
    slab_rows = out_ref.shape[2]
    folded_rows = rows // 2
    slots = min(4, folded_rows)
    packs = folded_rows // slots
    half = lanes // 2
    block = half // slots
    edge = SWEEPS
    tile = lax.axis_index("tile")
    n_tile = edge_ref.shape[0]
    from_left_ref = edge_ref.at[jnp.maximum(tile - 1, 0)]
    from_right_ref = edge_ref.at[jnp.minimum(tile + 1, n_tile - 1)]

    def inside(condition, value):
        return jnp.where(jnp.broadcast_to(condition, value.shape), value, 0.0)

    for level in range(levels):
        for pack in range(packs):
            place = level * packs + pack
            left = inside(tile > 0, from_left_ref[pl.ds(place * members, members), :])
            right = inside(tile < n_tile - 1, from_right_ref[pl.ds(place * members, members), :])
            coeff_place = levels * packs * members + place
            coeff_left = inside(tile > 0, spread(from_left_ref[pl.ds(coeff_place, 1), :], 8))
            coeff_right = inside(
                tile < n_tile - 1, spread(from_right_ref[pl.ds(coeff_place, 1), :], 8)
            )
            for slot in range(slots):
                row = pack * slots + slot
                first_ref[level, row] = joined_strip(
                    strip_ref[level, row], left, right, slot, block
                )
                own = own_strip(
                    spread(coeff_ref[level, pl.ds(row, 1), :], 8),
                    spread(coeff_ref[level, pl.ds(rows - 1 - row, 1), :], 8),
                )
                coeff_strip_ref[level, row] = joined_strip(own, coeff_left, coeff_right, slot, block)

    def coeff_at(level, row):
        return coeff_strip_ref[level, row]

    for level in range(levels):
        for row in range(folded_rows):
            here, around = neighbour_total(coeff_at, level, row, levels, folded_rows, True)
            keep_ref[level, pl.ds(row, 1), :] = (1.0 - here * around)[0:1]
            square_ref[level, pl.ds(row, 1), :] = (here * here)[0:1]
    all_sweeps(first_ref, second_ref, keep_ref, square_ref, levels, folded_rows, members, True)
    lane = lane_index((members, lanes))
    for level in range(levels):
        for row in range(folded_rows):
            coeff = coeff_strip_ref[level, row][0:1]
            final = first_ref[level, row] / jnp.where(coeff > 0.0, coeff, 1.0)
            for target, before, after in (
                (row, -edge, edge - half),
                (rows - 1 - row, -edge - half, edge),
            ):
                start = lane_roll(final, before)
                stop = lane_roll(final, after)
                inner = interior_ref[level, target]
                merged = jnp.where(
                    lane < edge, start, jnp.where(lane >= lanes - edge, stop, inner)
                )
                local_ref[pl.ds((level * rows + target) * members, members), :] = merged

    def add_level(level, carry):
        base = level * rows
        fields = [
            local_ref[pl.ds(base * members + member, rows, stride=members), :]
            for member in range(members)
        ]
        for term in range(terms):
            result = None
            for member in range(members):
                piece = pert_ref[member, term, level].astype(jnp.float32) * fields[member]
                result = piece if result is None else result + piece
            start = pl.multiple_of(term * levels * rows + base, rows)
            sum_ref[pl.ds(start, rows), :] = result
        return carry

    lax.fori_loop(0, levels, add_level, 0)
    for slab in range(rows // slab_rows):
        owner = owner_ref[slab]
        for term in range(terms):
            for inner in range(slab_rows):
                row = slab * slab_rows + inner
                out_ref[owner, term, inner] = sum_ref[
                    pl.ds(term * levels * rows + row, levels, stride=rows), :
                ]


def whole(memory_space=pltpu.VMEM):
    return pl.BlockSpec(memory_space=memory_space)


def body(perturbations, gradient_store, diffusivity, slab_owner):
    members, slots, variables, levels, rows, lanes = perturbations.shape
    terms = slots * variables
    n_member = lax.axis_size("member")
    n_tile = lax.axis_size("tile")
    slab_rows = gradient_store.shape[3]
    folded_rows = rows // 2
    packs = folded_rows // min(4, folded_rows)
    edge_rows = levels * packs * (members + 1)
    f32 = jnp.float32
    params = pltpu.CompilerParams(vmem_limit_bytes=VMEM_LIMIT)

    pert = perturbations.reshape(members, terms, levels, rows, lanes)
    slab = gradient_store.reshape(terms, levels, slab_rows, lanes).swapaxes(1, 2)
    gathered = lax.all_gather(slab, "member", axis=0, tiled=False)

    field, strip, edges = pl.pallas_call(
        weigh_kernel,
        out_shape=(
            jax.ShapeDtypeStruct((levels * rows * members, lanes), f32),
            jax.ShapeDtypeStruct((levels, folded_rows, members, lanes), f32),
            jax.ShapeDtypeStruct((n_tile, edge_rows, lanes), f32),
        ),
        in_specs=[whole(pltpu.SMEM), whole(), whole(), whole()],
        out_specs=(whole(),) * 3,
        scratch_shapes=[pltpu.VMEM((terms * levels * rows, lanes), f32)],
        compiler_params=params,
        name="weigh",
    )(slab_owner, gathered, pert, diffusivity)

    edges = lax.all_to_all(edges, "tile", 0, 0, tiled=True)

    interior = pl.pallas_call(
        interior_kernel,
        out_shape=jax.ShapeDtypeStruct((levels, rows, members, lanes), f32),
        in_specs=[whole(), whole()],
        out_specs=whole(),
        scratch_shapes=[
            pltpu.VMEM((levels, rows, members, lanes), f32),
            pltpu.VMEM((levels, rows, lanes), f32),
            pltpu.VMEM((levels, rows, lanes), f32),
            pltpu.VMEM((levels, rows, lanes), f32),
        ],
        compiler_params=params,
        cost_estimate=pl.CostEstimate(
            flops=SWEEPS * 8 * levels * rows * members * lanes,
            bytes_accessed=8 * levels * rows * members * lanes,
            transcendentals=0,
        ),
        name="interior",
    )(field.reshape(levels, rows, members, lanes), diffusivity)

    sums = pl.pallas_call(
        finish_kernel,
        out_shape=jax.ShapeDtypeStruct((n_member, terms, slab_rows, levels, lanes), f32),
        in_specs=[whole(pltpu.SMEM)] + [whole()] * 5,
        out_specs=whole(),
        scratch_shapes=[
            pltpu.VMEM((levels, folded_rows, members, lanes), f32),
            pltpu.VMEM((levels, folded_rows, members, lanes), f32),
            pltpu.VMEM((levels, folded_rows, 8, lanes), f32),
            pltpu.VMEM((levels, folded_rows, lanes), f32),
            pltpu.VMEM((levels, folded_rows, lanes), f32),
            pltpu.VMEM((levels * rows * members, lanes), f32),
            pltpu.VMEM((terms * levels * rows, lanes), f32),
        ],
        compiler_params=params,
        name="finish",
    )(slab_owner, pert, diffusivity, interior, strip, edges)

    norm_factor = 1.0 / (members * n_member - 1)
    owned = lax.psum_scatter(sums, "member", scatter_dimension=0, tiled=False) * norm_factor
    return owned.swapaxes(1, 2).reshape(slots, variables, levels, slab_rows, lanes)


def solution(mesh):
    in_specs = (
        P("member", None, None, None, None, "tile"),
        P(None, None, None, "member", "tile"),
        P(None, None, "tile"),
        P(),
    )
    out_specs = P(None, None, None, "member", "tile")
    return jax.shard_map(body, mesh=mesh, in_specs=in_specs, out_specs=out_specs, check_vma=False)
```

```python
import math

import jax
import jax.numpy as jnp
from jax import lax
from jax.experimental import pallas as pl
from jax.experimental.pallas import tpu as pltpu
from jax.sharding import PartitionSpec as P

SWEEPS = 10
SLOTS = 4
VMEM_LIMIT = 48 * 1024 * 1024


def lane_roll(value, shift):
    shift = shift % value.shape[-1]
    return value if shift == 0 else pltpu.roll(value, shift, 1)


def lane_index(shape):
    return lax.broadcasted_iota(jnp.int32, shape, 1)


def pick(values, which):
    result = values[0]
    for index in range(1, len(values)):
        result = jnp.where(which == index, values[index], result)
    return result


def spread(row, rows=8):
    return jnp.broadcast_to(row, (rows, row.shape[-1]))


def pack_sizes(rows):
    folded_rows = rows // 2
    slots = min(SLOTS, folded_rows)
    return folded_rows, slots, folded_rows // slots


def own_strip(near, far):
    lanes = near.shape[-1]
    half, part = lanes // 2, lanes // 4
    lane = lane_index(near.shape)
    far = lane_roll(far, half)
    start = half - SWEEPS
    first = jnp.where((lane >= start) & (lane < start + part), far, near)
    start = half + SWEEPS - part
    second = jnp.where((lane >= start) & (lane < start + part), far, near)
    return jnp.where(
        lane % half < part,
        lane_roll(first, SWEEPS),
        lane_roll(second, half - SWEEPS),
    )


def strip_ends(strip):
    lanes = strip.shape[-1]
    half, part = lanes // 2, lanes // 4
    lane = lane_index(strip.shape)
    ends = jnp.where(
        lane % half < part, lane_roll(strip, -SWEEPS), lane_roll(strip, half + SWEEPS)
    )
    return ends, lane_roll(ends, half)


def packed_edges(strips):
    lanes = strips[0].shape[-1]
    half = lanes // 2
    block = half // len(strips)
    slot = (lane_index(strips[0].shape) % half) // block
    to_right = pick([lane_roll(s, i * block) for i, s in enumerate(strips)], slot)
    to_left = pick([lane_roll(s, (i + 1) * block - half) for i, s in enumerate(strips)], slot)
    return to_right, to_left


def joined_strip(own, from_left, from_right, slot, block):
    lanes = own.shape[-1]
    half = lanes // 2
    place = lane_index(own.shape) % half
    left = lane_roll(from_left, -slot * block)
    right = lane_roll(from_right, half - (slot + 1) * block)
    return jnp.where(place < SWEEPS, left, jnp.where(place >= half - SWEEPS, right, own))


def total(terms):
    terms = list(terms)
    while len(terms) > 1:
        terms = [
            terms[i] + terms[i + 1] if i + 1 < len(terms) else terms[i]
            for i in range(0, len(terms), 2)
        ]
    return terms[0]


def around(planes, level, row, folded):
    levels, rows = len(planes), len(planes[level])
    here = planes[level][row]
    terms = [lane_roll(here, 1), lane_roll(here, -1)]
    if row > 0:
        terms.append(planes[level][row - 1])
    if row < rows - 1:
        terms.append(planes[level][row + 1])
    elif folded:
        terms.append(lane_roll(here, here.shape[-1] // 2))
    if level > 0:
        terms.append(planes[level - 1][row])
    if level < levels - 1:
        terms.append(planes[level + 1][row])
    return total(terms)


def sweep(source, target, keep_ref, square_ref, folded):
    levels, rows = source.shape[0], source.shape[1]
    planes = [[source[level, row] for row in range(rows)] for level in range(levels)]
    for level in range(levels):
        for row in range(rows):
            keep = keep_ref[level, pl.ds(row, 1), :]
            square = square_ref[level, pl.ds(row, 1), :]
            target[level, row] = keep * planes[level][row] + square * around(
                planes, level, row, folded
            )


def coefficient_kernel(coeff_ref, strip_ref, right_ref, left_ref):
    levels, rows, lanes = coeff_ref.shape
    folded_rows, slots, packs = pack_sizes(rows)
    for level in range(levels):
        for pack in range(packs):
            strips = []
            for slot in range(slots):
                row = pack * slots + slot
                strip = own_strip(
                    spread(coeff_ref[level, pl.ds(row, 1), :]),
                    spread(coeff_ref[level, pl.ds(rows - 1 - row, 1), :]),
                )
                strip_ref[level, pl.ds(row, 1), :] = strip[0:1]
                strips.append(strip)
            for ref, packed in zip((right_ref, left_ref), packed_edges(strips)):
                ref[pl.ds(level * packs + pack, 1), :] = packed[0:1]


def weigh_kernel(
    owner_ref, gathered_ref, pert_ref, coeff_ref, field_ref, strip_ref, right_ref, left_ref, grad_ref
):
    members, terms, levels, rows, lanes = pert_ref.shape
    slab_rows = gathered_ref.shape[2]
    folded_rows, slots, packs = pack_sizes(rows)
    for slab in range(rows // slab_rows):
        owner = owner_ref[slab]
        for term in range(terms):
            for inner in range(slab_rows):
                row = slab * slab_rows + inner
                grad_ref[pl.ds(term * levels * rows + row, levels, stride=rows), :] = gathered_ref[
                    owner, term, inner
                ]

    def weigh_level(level, carry):
        base = level * rows
        coeff = coeff_ref[level]
        gradients = [
            coeff * grad_ref[pl.ds(pl.multiple_of(term * levels * rows + base, rows), rows), :]
            for term in range(terms)
        ]
        for member in range(members):
            weighted = total(
                pert_ref[member, term, level].astype(jnp.float32) * gradients[term]
                for term in range(terms)
            )
            field_ref[pl.ds(base * members + member, rows, stride=members), :] = weighted
        return carry

    lax.fori_loop(0, levels, weigh_level, 0)

    def field_at(level, row):
        return field_ref[pl.ds((level * rows + row) * members, members), :]

    for level in range(levels):
        for pack in range(packs):
            strips = []
            for slot in range(slots):
                row = pack * slots + slot
                strip = own_strip(field_at(level, row), field_at(level, rows - 1 - row))
                strip_ref[level, row] = strip
                strips.append(strip)
            place = level * packs + pack
            for ref, packed in zip((right_ref, left_ref), packed_edges(strips)):
                ref[pl.ds(place * members, members), :] = packed


def interior_kernel(
    field_ref,
    coeff_ref,
    coeff_strip_ref,
    left_coeff_ref,
    right_coeff_ref,
    out_ref,
    strip_keep_ref,
    strip_square_ref,
    strip_inverse_ref,
    other_ref,
    keep_ref,
    square_ref,
    inverse_ref,
):
    levels, rows, members, lanes = field_ref.shape
    folded_rows, slots, packs = pack_sizes(rows)
    block = lanes // 2 // slots
    row_index = lax.broadcasted_iota(jnp.int32, (rows, lanes), 0)
    for level in range(levels):
        here = coeff_ref[level]
        terms = [
            lane_roll(here, 1),
            lane_roll(here, -1),
            jnp.where(row_index > 0, pltpu.roll(here, 1, 0), 0.0),
            jnp.where(row_index < rows - 1, pltpu.roll(here, rows - 1, 0), 0.0),
        ]
        if level > 0:
            terms.append(coeff_ref[level - 1])
        if level < levels - 1:
            terms.append(coeff_ref[level + 1])
        keep_ref[level] = 1.0 - here * total(terms)
        square_ref[level] = here * here
        inverse_ref[level] = 1.0 / here
    sweep(field_ref, other_ref, keep_ref, square_ref, False)
    sweep(other_ref, out_ref, keep_ref, square_ref, False)

    def pair(index, carry):
        sweep(out_ref, other_ref, keep_ref, square_ref, False)
        sweep(other_ref, out_ref, keep_ref, square_ref, False)
        return carry

    lax.fori_loop(0, SWEEPS // 2 - 1, pair, 0)
    for level in range(levels):
        for row in range(rows):
            out_ref[level, row] = out_ref[level, row] * inverse_ref[level, pl.ds(row, 1), :]

    planes = []
    for level in range(levels):
        plane = []
        for pack in range(packs):
            place = pl.ds(level * packs + pack, 1)
            for slot in range(slots):
                row = pack * slots + slot
                plane.append(
                    joined_strip(
                        spread(coeff_strip_ref[level, pl.ds(row, 1), :]),
                        spread(left_coeff_ref[place, :]),
                        spread(right_coeff_ref[place, :]),
                        slot,
                        block,
                    )
                )
        planes.append(plane)
    for level in range(levels):
        for row in range(folded_rows):
            here = planes[level][row]
            keep = 1.0 - here * around(planes, level, row, True)
            inverse = 1.0 / jnp.where(here > 0.0, here, 1.0)
            strip_keep_ref[level, pl.ds(row, 1), :] = keep[0:1]
            strip_square_ref[level, pl.ds(row, 1), :] = (here * here)[0:1]
            strip_inverse_ref[level, pl.ds(row, 1), :] = inverse[0:1]


def finish_kernel(
    owner_ref,
    pert_ref,
    interior_ref,
    strip_ref,
    keep_ref,
    square_ref,
    inverse_ref,
    from_left_ref,
    from_right_ref,
    out_ref,
    first_ref,
    second_ref,
    local_ref,
    sum_ref,
):
    members, terms, levels, rows, lanes = pert_ref.shape
    slab_rows = out_ref.shape[2]
    folded_rows, slots, packs = pack_sizes(rows)
    block = lanes // 2 // slots
    for level in range(levels):
        for pack in range(packs):
            place = level * packs + pack
            left = from_left_ref[pl.ds(place * members, members), :]
            right = from_right_ref[pl.ds(place * members, members), :]
            for slot in range(slots):
                row = pack * slots + slot
                first_ref[level, row] = joined_strip(
                    strip_ref[level, row], left, right, slot, block
                )

    def pair(index, carry):
        sweep(first_ref, second_ref, keep_ref, square_ref, True)
        sweep(second_ref, first_ref, keep_ref, square_ref, True)
        return carry

    lax.fori_loop(0, SWEEPS // 2, pair, 0)
    lane = lane_index((members, lanes))
    for level in range(levels):
        for row in range(folded_rows):
            ends = strip_ends(first_ref[level, row] * inverse_ref[level, pl.ds(row, 1), :])
            for target, end in zip((row, rows - 1 - row), ends):
                local_ref[pl.ds((level * rows + target) * members, members), :] = jnp.where(
                    (lane < SWEEPS) | (lane >= lanes - SWEEPS), end, interior_ref[level, target]
                )

    def add_level(level, carry):
        base = level * rows
        fields = [
            local_ref[pl.ds(base * members + member, rows, stride=members), :]
            for member in range(members)
        ]
        for term in range(terms):
            start = pl.multiple_of(term * levels * rows + base, rows)
            sum_ref[pl.ds(start, rows), :] = total(
                pert_ref[member, term, level].astype(jnp.float32) * fields[member]
                for member in range(members)
            )
        return carry

    lax.fori_loop(0, levels, add_level, 0)
    for slab in range(rows // slab_rows):
        owner = owner_ref[slab]
        for term in range(terms):
            for inner in range(slab_rows):
                row = slab * slab_rows + inner
                out_ref[owner, term, inner] = sum_ref[
                    pl.ds(term * levels * rows + row, levels, stride=rows), :
                ]


def whole(memory_space=pltpu.VMEM):
    return pl.BlockSpec(memory_space=memory_space)


def local_call(kernel, name, outs, scratch, operands, work, scalars=0):
    f32 = jnp.float32
    moved = sum(x.size * x.dtype.itemsize for x in operands)
    moved += sum(4 * math.prod(shape) for shape in outs)
    single = len(outs) == 1
    shapes = tuple(jax.ShapeDtypeStruct(shape, f32) for shape in outs)
    specs = tuple(whole() for _ in outs)
    return pl.pallas_call(
        kernel,
        out_shape=shapes[0] if single else shapes,
        in_specs=[whole(pltpu.SMEM)] * scalars + [whole()] * (len(operands) - scalars),
        out_specs=specs[0] if single else specs,
        scratch_shapes=[pltpu.VMEM(shape, f32) for shape in scratch],
        compiler_params=pltpu.CompilerParams(vmem_limit_bytes=VMEM_LIMIT),
        cost_estimate=pl.CostEstimate(flops=work, bytes_accessed=moved, transcendentals=0),
        name=name,
    )(*operands)


def body(perturbations, gradient_store, diffusivity, slab_owner):
    members, slots, variables, levels, rows, lanes = perturbations.shape
    terms = slots * variables
    n_member = lax.axis_size("member")
    n_tile = lax.axis_size("tile")
    slab_rows = gradient_store.shape[3]
    folded_rows, _, packs = pack_sizes(rows)
    cells = levels * rows * lanes
    up = [(i, i + 1) for i in range(n_tile - 1)]
    down = [(i + 1, i) for i in range(n_tile - 1)]

    pert = perturbations.reshape(members, terms, levels, rows, lanes)
    slab = gradient_store.reshape(terms, levels, slab_rows, lanes).swapaxes(1, 2)
    copies = jnp.broadcast_to(slab[None], (n_member,) + slab.shape)
    gathered = lax.all_to_all(copies, "member", 0, 0, tiled=True)

    strip_shape = (levels, folded_rows, lanes)
    coeff_strip, coeff_right, coeff_left = local_call(
        coefficient_kernel,
        "coefficient_strips",
        [strip_shape, (levels * packs, lanes), (levels * packs, lanes)],
        [],
        (diffusivity,),
        8 * cells,
    )
    left_coeff = lax.ppermute(coeff_right, "tile", up)
    right_coeff = lax.ppermute(coeff_left, "tile", down)

    wide_strip = (levels, folded_rows, members, lanes)
    edge_shape = (levels * packs * members, lanes)
    field, strip, to_right, to_left = local_call(
        weigh_kernel,
        "weigh",
        [(levels * rows * members, lanes), wide_strip, edge_shape, edge_shape],
        [(terms * levels * rows, lanes)],
        (slab_owner, gathered, pert, diffusivity),
        2 * terms * members * cells,
        scalars=1,
    )
    from_left = lax.ppermute(to_right, "tile", up)
    from_right = lax.ppermute(to_left, "tile", down)

    wide_field = (levels, rows, members, lanes)
    field_coeff = (levels, rows, lanes)
    interior, keep, square, inverse = local_call(
        interior_kernel,
        "interior",
        [wide_field, strip_shape, strip_shape, strip_shape],
        [wide_field, field_coeff, field_coeff, field_coeff],
        (field.reshape(wide_field), diffusivity, coeff_strip, left_coeff, right_coeff),
        8 * SWEEPS * members * cells,
    )
    sums = local_call(
        finish_kernel,
        "finish",
        [(n_member, terms, slab_rows, levels, lanes)],
        [wide_strip, wide_strip, (levels * rows * members, lanes), (terms * levels * rows, lanes)],
        (slab_owner, pert, interior, strip, keep, square, inverse, from_left, from_right),
        2 * terms * members * cells,
        scalars=1,
    )
    received = lax.all_to_all(sums, "member", 0, 0, tiled=True)
    norm_factor = 1.0 / (members * n_member - 1)
    owned = jnp.sum(received, axis=0) * norm_factor
    return owned.swapaxes(1, 2).reshape(slots, variables, levels, slab_rows, lanes)


def solution(mesh):
    in_specs = (
        P("member", None, None, None, None, "tile"),
        P(None, None, None, "member", "tile"),
        P(None, None, "tile"),
        P(),
    )
    out_specs = P(None, None, None, "member", "tile")
    return jax.shard_map(body, mesh=mesh, in_specs=in_specs, out_specs=out_specs, check_vma=False)
```

```python
import math

import jax
import jax.numpy as jnp
from jax import lax
from jax.experimental import pallas as pl
from jax.experimental.pallas import tpu as pltpu
from jax.sharding import PartitionSpec as P

SWEEPS = 10
SLOTS = 4
CHUNKS = 4
VMEM_LIMIT = 16 * 1024 * 1024


def lane_roll(value, shift):
    shift = shift % value.shape[-1]
    return value if shift == 0 else pltpu.roll(value, shift, 1)


def lane_index(shape):
    return lax.broadcasted_iota(jnp.int32, shape, 1)


def pick(values, which):
    result = values[0]
    for index in range(1, len(values)):
        result = jnp.where(which == index, values[index], result)
    return result


def spread(row, rows=8):
    return jnp.broadcast_to(row, (rows, row.shape[-1]))


def pack_sizes(rows):
    folded_rows = rows // 2
    slots = min(SLOTS, folded_rows)
    return folded_rows, slots, folded_rows // slots


def own_strip(near, far):
    lanes = near.shape[-1]
    half, part = lanes // 2, lanes // 4
    lane = lane_index(near.shape)
    far = lane_roll(far, half)
    start = half - SWEEPS
    first = jnp.where((lane >= start) & (lane < start + part), far, near)
    start = half + SWEEPS - part
    second = jnp.where((lane >= start) & (lane < start + part), far, near)
    return jnp.where(
        lane % half < part,
        lane_roll(first, SWEEPS),
        lane_roll(second, half - SWEEPS),
    )


def strip_ends(strip):
    lanes = strip.shape[-1]
    half, part = lanes // 2, lanes // 4
    lane = lane_index(strip.shape)
    ends = jnp.where(
        lane % half < part, lane_roll(strip, -SWEEPS), lane_roll(strip, half + SWEEPS)
    )
    return ends, lane_roll(ends, half)


def packed_edges(strips):
    lanes = strips[0].shape[-1]
    half = lanes // 2
    block = half // len(strips)
    slot = (lane_index(strips[0].shape) % half) // block
    to_right = pick([lane_roll(s, i * block) for i, s in enumerate(strips)], slot)
    to_left = pick([lane_roll(s, (i + 1) * block - half) for i, s in enumerate(strips)], slot)
    return to_right, to_left


def joined_strip(own, from_left, from_right, slot, block):
    lanes = own.shape[-1]
    half = lanes // 2
    place = lane_index(own.shape) % half
    left = lane_roll(from_left, -slot * block)
    right = lane_roll(from_right, half - (slot + 1) * block)
    return jnp.where(place < SWEEPS, left, jnp.where(place >= half - SWEEPS, right, own))


def total(terms):
    terms = list(terms)
    while len(terms) > 1:
        terms = [
            terms[i] + terms[i + 1] if i + 1 < len(terms) else terms[i]
            for i in range(0, len(terms), 2)
        ]
    return terms[0]


def around(planes, level, row, folded):
    levels, rows = len(planes), len(planes[level])
    here = planes[level][row]
    terms = [lane_roll(here, 1), lane_roll(here, -1)]
    if row > 0:
        terms.append(planes[level][row - 1])
    if row < rows - 1:
        terms.append(planes[level][row + 1])
    elif folded:
        terms.append(lane_roll(here, here.shape[-1] // 2))
    if level > 0:
        terms.append(planes[level - 1][row])
    if level < levels - 1:
        terms.append(planes[level + 1][row])
    return total(terms)


def sweep(source, target, keep_ref, square_ref, folded):
    levels, rows = source.shape[0], source.shape[1]
    planes = [[source[level, row] for row in range(rows)] for level in range(levels)]
    for level in range(levels):
        for row in range(rows):
            keep = keep_ref[level, pl.ds(row, 1), :]
            square = square_ref[level, pl.ds(row, 1), :]
            target[level, row] = keep * planes[level][row] + square * around(
                planes, level, row, folded
            )


def own_coefficient_strip(coeff_ref, level, row):
    rows = coeff_ref.shape[1]
    return own_strip(
        spread(coeff_ref[level, pl.ds(row, 1), :]),
        spread(coeff_ref[level, pl.ds(rows - 1 - row, 1), :]),
    )


def weigh_kernel(
    gathered_ref,
    owner_hbm,
    pert_hbm,
    coeff_hbm,
    field_ref,
    strip_ref,
    right_ref,
    left_ref,
    pert_ref,
    owner_ref,
    coeff_ref,
    grad_ref,
    owner_sem,
    coeff_sem,
    pert_sems,
):
    members, terms, levels, rows, lanes = pert_ref.shape
    slab_rows = gathered_ref.shape[2]
    folded_rows, slots, packs = pack_sizes(rows)
    chunks = pert_sems.shape[0]
    chunk = members // chunks
    coeff_copy = pltpu.make_async_copy(coeff_hbm, coeff_ref, coeff_sem)
    owner_copy = pltpu.make_async_copy(owner_hbm, owner_ref, owner_sem)
    coeff_copy.start()
    owner_copy.start()
    pert_copies = []
    for index in range(chunks):
        part = pl.ds(index * chunk, chunk)
        copy = pltpu.make_async_copy(pert_hbm.at[part], pert_ref.at[part], pert_sems.at[index])
        copy.start()
        pert_copies.append(copy)

    coeff_copy.wait()
    for level in range(levels):
        for pack in range(packs):
            strips = [
                own_coefficient_strip(coeff_ref, level, pack * slots + slot)
                for slot in range(slots)
            ]
            place = levels * packs * members + level * packs + pack
            for ref, packed in zip((right_ref, left_ref), packed_edges(strips)):
                ref[pl.ds(place, 1), :] = packed[0:1]

    owner_copy.wait()
    for slab in range(rows // slab_rows):
        owner = owner_ref[slab]
        for inner in range(slab_rows):
            row = slab * slab_rows + inner
            coeff = jnp.concatenate(
                [coeff_ref[level, pl.ds(row, 1), :] for level in range(levels)], axis=0
            )
            for term in range(terms):
                grad_ref[pl.ds(term * levels * rows + row, levels, stride=rows), :] = (
                    coeff * gathered_ref[owner, term, inner]
                )

    for index in range(chunks):
        pert_copies[index].wait()

        def weigh_level(level, carry):
            base = level * rows
            gradients = [
                grad_ref[pl.ds(pl.multiple_of(term * levels * rows + base, rows), rows), :]
                for term in range(terms)
            ]
            for member in range(index * chunk, (index + 1) * chunk):
                field_ref[pl.ds(base * members + member, rows, stride=members), :] = total(
                    pert_ref[member, term, level].astype(jnp.float32) * gradients[term]
                    for term in range(terms)
                )
            return carry

        lax.fori_loop(0, levels, weigh_level, 0)

    def field_at(level, row):
        return field_ref[pl.ds((level * rows + row) * members, members), :]

    for level in range(levels):
        for pack in range(packs):
            strips = []
            for slot in range(slots):
                row = pack * slots + slot
                strip = own_strip(field_at(level, row), field_at(level, rows - 1 - row))
                strip_ref[level, row] = strip
                strips.append(strip)
            place = level * packs + pack
            for ref, packed in zip((right_ref, left_ref), packed_edges(strips)):
                ref[pl.ds(place * members, members), :] = packed


def interior_kernel(
    field_ref,
    coeff_ref,
    out_ref,
    coeff_strip_ref,
    other_ref,
    keep_ref,
    square_ref,
    inverse_ref,
):
    levels, rows, members, lanes = field_ref.shape
    folded_rows = rows // 2
    row_index = lax.broadcasted_iota(jnp.int32, (rows, lanes), 0)
    for level in range(levels):
        here = coeff_ref[level]
        terms = [
            lane_roll(here, 1),
            lane_roll(here, -1),
            jnp.where(row_index > 0, pltpu.roll(here, 1, 0), 0.0),
            jnp.where(row_index < rows - 1, pltpu.roll(here, rows - 1, 0), 0.0),
        ]
        if level > 0:
            terms.append(coeff_ref[level - 1])
        if level < levels - 1:
            terms.append(coeff_ref[level + 1])
        keep_ref[level] = 1.0 - here * total(terms)
        square_ref[level] = here * here
        inverse_ref[level] = 1.0 / here
    sweep(field_ref, other_ref, keep_ref, square_ref, False)
    sweep(other_ref, out_ref, keep_ref, square_ref, False)

    def pair(index, carry):
        sweep(out_ref, other_ref, keep_ref, square_ref, False)
        sweep(other_ref, out_ref, keep_ref, square_ref, False)
        return carry

    lax.fori_loop(0, SWEEPS // 2 - 1, pair, 0)
    for level in range(levels):
        for row in range(rows):
            out_ref[level, row] = out_ref[level, row] * inverse_ref[level, pl.ds(row, 1), :]

    for level in range(levels):
        for row in range(folded_rows):
            coeff_strip_ref[level, pl.ds(row, 1), :] = own_coefficient_strip(
                coeff_ref, level, row
            )[0:1]


def finish_kernel(
    owner_ref,
    pert_ref,
    interior_ref,
    strip_ref,
    coeff_strip_ref,
    from_left_ref,
    from_right_ref,
    out_ref,
    first_ref,
    second_ref,
    keep_ref,
    square_ref,
    inverse_ref,
    local_ref,
    sum_ref,
):
    members, terms, levels, rows, lanes = pert_ref.shape
    slab_rows = out_ref.shape[2]
    folded_rows, slots, packs = pack_sizes(rows)
    block = lanes // 2 // slots
    for level in range(levels):
        for pack in range(packs):
            place = level * packs + pack
            left = from_left_ref[pl.ds(place * members, members), :]
            right = from_right_ref[pl.ds(place * members, members), :]
            for slot in range(slots):
                row = pack * slots + slot
                first_ref[level, row] = joined_strip(
                    strip_ref[level, row], left, right, slot, block
                )

    planes = []
    for level in range(levels):
        plane = []
        for pack in range(packs):
            place = pl.ds(levels * packs * members + level * packs + pack, 1)
            for slot in range(slots):
                row = pack * slots + slot
                plane.append(
                    joined_strip(
                        spread(coeff_strip_ref[level, pl.ds(row, 1), :]),
                        spread(from_left_ref[place, :]),
                        spread(from_right_ref[place, :]),
                        slot,
                        block,
                    )
                )
        planes.append(plane)
    for level in range(levels):
        for row in range(folded_rows):
            here = planes[level][row]
            keep = 1.0 - here * around(planes, level, row, True)
            inverse = 1.0 / jnp.where(here > 0.0, here, 1.0)
            keep_ref[level, pl.ds(row, 1), :] = keep[0:1]
            square_ref[level, pl.ds(row, 1), :] = (here * here)[0:1]
            inverse_ref[level, pl.ds(row, 1), :] = inverse[0:1]

    def pair(index, carry):
        sweep(first_ref, second_ref, keep_ref, square_ref, True)
        sweep(second_ref, first_ref, keep_ref, square_ref, True)
        return carry

    lax.fori_loop(0, SWEEPS // 2, pair, 0)
    lane = lane_index((members, lanes))
    for level in range(levels):
        for row in range(folded_rows):
            ends = strip_ends(first_ref[level, row] * inverse_ref[level, pl.ds(row, 1), :])
            for target, end in zip((row, rows - 1 - row), ends):
                local_ref[pl.ds((level * rows + target) * members, members), :] = jnp.where(
                    (lane < SWEEPS) | (lane >= lanes - SWEEPS), end, interior_ref[level, target]
                )

    def add_level(level, carry):
        base = level * rows
        fields = [
            local_ref[pl.ds(base * members + member, rows, stride=members), :]
            for member in range(members)
        ]
        for term in range(terms):
            start = pl.multiple_of(term * levels * rows + base, rows)
            sum_ref[pl.ds(start, rows), :] = total(
                pert_ref[member, term, level].astype(jnp.float32) * fields[member]
                for member in range(members)
            )
        return carry

    lax.fori_loop(0, levels, add_level, 0)
    for slab in range(rows // slab_rows):
        owner = owner_ref[slab]
        for term in range(terms):
            for inner in range(slab_rows):
                row = slab * slab_rows + inner
                out_ref[owner, term, inner] = sum_ref[
                    pl.ds(term * levels * rows + row, levels, stride=rows), :
                ]


def whole(memory_space=pltpu.VMEM):
    return pl.BlockSpec(memory_space=memory_space)


def local_call(kernel, name, outs, scratch, operands, places, work):
    def shape_of(out):
        return out if isinstance(out, jax.ShapeDtypeStruct) else jax.ShapeDtypeStruct(out, jnp.float32)

    shapes = tuple(shape_of(out) for out in outs)
    specs = tuple(whole() for _ in outs)
    moved = sum(math.prod(x.shape) * x.dtype.itemsize for x in tuple(operands) + shapes)
    single = len(outs) == 1
    return pl.pallas_call(
        kernel,
        out_shape=shapes[0] if single else shapes,
        in_specs=[whole(place) for place in places],
        out_specs=specs[0] if single else specs,
        scratch_shapes=[
            pltpu.VMEM(item, jnp.float32) if isinstance(item, tuple) else item for item in scratch
        ],
        compiler_params=pltpu.CompilerParams(vmem_limit_bytes=VMEM_LIMIT),
        cost_estimate=pl.CostEstimate(flops=work, bytes_accessed=moved, transcendentals=0),
        name=name,
    )(*operands)


def body(perturbations, gradient_store, diffusivity, slab_owner):
    members, slots, variables, levels, rows, lanes = perturbations.shape
    terms = slots * variables
    n_member = lax.axis_size("member")
    n_tile = lax.axis_size("tile")
    slab_rows = gradient_store.shape[3]
    folded_rows, _, packs = pack_sizes(rows)
    cells = levels * rows * lanes
    wide_strip = (levels, folded_rows, members, lanes)
    strip_shape = (levels, folded_rows, lanes)
    wide_field = (levels, rows, members, lanes)
    flat_field = (levels * rows * members, lanes)
    field_coeff = (levels, rows, lanes)
    edge_shape = (levels * packs * (members + 1), lanes)
    grad_shape = (terms * levels * rows, lanes)
    hbm, vmem, smem = pl.ANY, pltpu.VMEM, pltpu.SMEM

    pert = perturbations.reshape(members, terms, levels, rows, lanes)
    slab = gradient_store.reshape(terms, levels, slab_rows, lanes).swapaxes(1, 2)
    gathered = lax.all_gather(slab, "member", axis=0, tiled=False)

    field, strip, to_right, to_left, pert_here = local_call(
        weigh_kernel,
        "weigh",
        [
            flat_field,
            wide_strip,
            edge_shape,
            edge_shape,
            jax.ShapeDtypeStruct(pert.shape, pert.dtype),
        ],
        [
            pltpu.SMEM(slab_owner.shape, slab_owner.dtype),
            field_coeff,
            grad_shape,
            pltpu.SemaphoreType.DMA,
            pltpu.SemaphoreType.DMA,
            pltpu.SemaphoreType.DMA((math.gcd(members, CHUNKS),)),
        ],
        (gathered, slab_owner, pert, diffusivity),
        (vmem, hbm, hbm, hbm),
        2 * terms * members * cells,
    )
    up = [(i, i + 1) for i in range(n_tile - 1)]
    down = [(i + 1, i) for i in range(n_tile - 1)]
    from_left = lax.ppermute(to_right, "tile", up)
    from_right = lax.ppermute(to_left, "tile", down)

    interior, coeff_strip = local_call(
        interior_kernel,
        "interior",
        [wide_field, strip_shape],
        [wide_field, field_coeff, field_coeff, field_coeff],
        (field.reshape(wide_field), diffusivity),
        (vmem, vmem),
        8 * SWEEPS * members * cells,
    )
    sums = local_call(
        finish_kernel,
        "finish",
        [(n_member, terms, slab_rows, levels, lanes)],
        [wide_strip, wide_strip, strip_shape, strip_shape, strip_shape, flat_field, grad_shape],
        (slab_owner, pert_here, interior, strip, coeff_strip, from_left, from_right),
        (smem,) + (vmem,) * 6,
        2 * terms * members * cells,
    )
    received = lax.all_to_all(sums, "member", 0, 0, tiled=True)
    norm_factor = 1.0 / (members * n_member - 1)
    owned = jnp.sum(received, axis=0) * norm_factor
    return owned.swapaxes(1, 2).reshape(slots, variables, levels, slab_rows, lanes)


def solution(mesh):
    in_specs = (
        P("member", None, None, None, None, "tile"),
        P(None, None, None, "member", "tile"),
        P(None, None, "tile"),
        P(),
    )
    out_specs = P(None, None, None, "member", "tile")
    return jax.shard_map(body, mesh=mesh, in_specs=in_specs, out_specs=out_specs, check_vma=False)
```

```python
import math

import jax
import jax.numpy as jnp
from jax import lax
from jax.experimental import pallas as pl
from jax.experimental.pallas import tpu as pltpu
from jax.sharding import PartitionSpec as P

SWEEPS = 10
SLOTS = 4
CHUNKS = 4
VMEM_LIMIT = 16 * 1024 * 1024


def lane_roll(value, shift):
    shift = shift % value.shape[-1]
    return value if shift == 0 else pltpu.roll(value, shift, 1)


def lane_index(shape):
    return lax.broadcasted_iota(jnp.int32, shape, 1)


def pick(values, which):
    result = values[0]
    for index in range(1, len(values)):
        result = jnp.where(which == index, values[index], result)
    return result


def spread(row, rows=8):
    return jnp.broadcast_to(row, (rows, row.shape[-1]))


def pack_sizes(rows):
    folded_rows = rows // 2
    slots = min(SLOTS, folded_rows)
    return folded_rows, slots, folded_rows // slots


def own_strip(near, far):
    lanes = near.shape[-1]
    half, part = lanes // 2, lanes // 4
    lane = lane_index(near.shape)
    far = lane_roll(far, half)
    start = half - SWEEPS
    first = jnp.where((lane >= start) & (lane < start + part), far, near)
    start = half + SWEEPS - part
    second = jnp.where((lane >= start) & (lane < start + part), far, near)
    return jnp.where(
        lane % half < part,
        lane_roll(first, SWEEPS),
        lane_roll(second, half - SWEEPS),
    )


def strip_ends(strip):
    lanes = strip.shape[-1]
    half, part = lanes // 2, lanes // 4
    lane = lane_index(strip.shape)
    ends = jnp.where(
        lane % half < part, lane_roll(strip, -SWEEPS), lane_roll(strip, half + SWEEPS)
    )
    return ends, lane_roll(ends, half)


def packed_edges(strips):
    lanes = strips[0].shape[-1]
    half = lanes // 2
    block = half // len(strips)
    slot = (lane_index(strips[0].shape) % half) // block
    to_right = pick([lane_roll(s, i * block) for i, s in enumerate(strips)], slot)
    to_left = pick([lane_roll(s, (i + 1) * block - half) for i, s in enumerate(strips)], slot)
    return to_right, to_left


def joined_strip(own, from_left, from_right, slot, block):
    lanes = own.shape[-1]
    half = lanes // 2
    place = lane_index(own.shape) % half
    left = lane_roll(from_left, -slot * block)
    right = lane_roll(from_right, half - (slot + 1) * block)
    return jnp.where(place < SWEEPS, left, jnp.where(place >= half - SWEEPS, right, own))


def total(terms):
    terms = list(terms)
    while len(terms) > 1:
        terms = [
            terms[i] + terms[i + 1] if i + 1 < len(terms) else terms[i]
            for i in range(0, len(terms), 2)
        ]
    return terms[0]


def around(planes, level, row, folded):
    levels, rows = len(planes), len(planes[level])
    here = planes[level][row]
    terms = [lane_roll(here, 1), lane_roll(here, -1)]
    if row > 0:
        terms.append(planes[level][row - 1])
    if row < rows - 1:
        terms.append(planes[level][row + 1])
    elif folded:
        terms.append(lane_roll(here, here.shape[-1] // 2))
    if level > 0:
        terms.append(planes[level - 1][row])
    if level < levels - 1:
        terms.append(planes[level + 1][row])
    return total(terms)


def sweep(source, target, keep_ref, square_ref, folded):
    levels, rows = source.shape[0], source.shape[1]
    planes = [[source[level, row] for row in range(rows)] for level in range(levels)]
    for level in range(levels):
        for row in range(rows):
            keep = keep_ref[level, pl.ds(row, 1), :]
            square = square_ref[level, pl.ds(row, 1), :]
            target[level, row] = keep * planes[level][row] + square * around(
                planes, level, row, folded
            )


def own_coefficient_strip(coeff_ref, level, row):
    rows = coeff_ref.shape[1]
    return own_strip(
        spread(coeff_ref[level, pl.ds(row, 1), :]),
        spread(coeff_ref[level, pl.ds(rows - 1 - row, 1), :]),
    )


def weigh_kernel(
    gathered_ref,
    owner_hbm,
    pert_hbm,
    coeff_hbm,
    field_ref,
    strip_ref,
    right_ref,
    left_ref,
    pert_ref,
    owner_ref,
    coeff_ref,
    grad_ref,
    owner_sem,
    coeff_sem,
    pert_sems,
):
    members, terms, levels, rows, lanes = pert_ref.shape
    slab_rows = gathered_ref.shape[2]
    folded_rows, slots, packs = pack_sizes(rows)
    chunks = pert_sems.shape[0]
    chunk = members // chunks
    coeff_copy = pltpu.make_async_copy(coeff_hbm, coeff_ref, coeff_sem)
    owner_copy = pltpu.make_async_copy(owner_hbm, owner_ref, owner_sem)
    coeff_copy.start()
    owner_copy.start()
    pert_copies = []
    for index in range(chunks):
        part = pl.ds(index * chunk, chunk)
        copy = pltpu.make_async_copy(pert_hbm.at[part], pert_ref.at[part], pert_sems.at[index])
        copy.start()
        pert_copies.append(copy)

    coeff_copy.wait()
    for level in range(levels):
        for pack in range(packs):
            strips = [
                own_coefficient_strip(coeff_ref, level, pack * slots + slot)
                for slot in range(slots)
            ]
            place = levels * packs * members + level * packs + pack
            for ref, packed in zip((right_ref, left_ref), packed_edges(strips)):
                ref[pl.ds(place, 1), :] = packed[0:1]

    owner_copy.wait()
    for slab in range(rows // slab_rows):
        owner = owner_ref[slab]
        for inner in range(slab_rows):
            row = slab * slab_rows + inner
            coeff = jnp.concatenate(
                [coeff_ref[level, pl.ds(row, 1), :] for level in range(levels)], axis=0
            )
            for term in range(terms):
                grad_ref[pl.ds(term * levels * rows + row, levels, stride=rows), :] = (
                    coeff * gathered_ref[owner, term, inner]
                )

    for index in range(chunks):
        pert_copies[index].wait()

        def weigh_level(level, carry):
            base = level * rows
            gradients = [
                grad_ref[pl.ds(pl.multiple_of(term * levels * rows + base, rows), rows), :]
                for term in range(terms)
            ]
            for member in range(index * chunk, (index + 1) * chunk):
                field_ref[pl.ds(base * members + member, rows, stride=members), :] = total(
                    pert_ref[member, term, level].astype(jnp.float32) * gradients[term]
                    for term in range(terms)
                )
            return carry

        lax.fori_loop(0, levels, weigh_level, 0)

    def field_at(level, row):
        return field_ref[pl.ds((level * rows + row) * members, members), :]

    for level in range(levels):
        for pack in range(packs):
            strips = []
            for slot in range(slots):
                row = pack * slots + slot
                strip = own_strip(field_at(level, row), field_at(level, rows - 1 - row))
                strip_ref[level, row] = strip
                strips.append(strip)
            place = level * packs + pack
            for ref, packed in zip((right_ref, left_ref), packed_edges(strips)):
                ref[pl.ds(place * members, members), :] = packed


def interior_kernel(
    field_ref,
    coeff_ref,
    out_ref,
    coeff_strip_ref,
    other_ref,
    keep_ref,
    square_ref,
    inverse_ref,
):
    levels, rows, members, lanes = field_ref.shape
    folded_rows = rows // 2
    row_index = lax.broadcasted_iota(jnp.int32, (rows, lanes), 0)
    for level in range(levels):
        here = coeff_ref[level]
        terms = [
            lane_roll(here, 1),
            lane_roll(here, -1),
            jnp.where(row_index > 0, pltpu.roll(here, 1, 0), 0.0),
            jnp.where(row_index < rows - 1, pltpu.roll(here, rows - 1, 0), 0.0),
        ]
        if level > 0:
            terms.append(coeff_ref[level - 1])
        if level < levels - 1:
            terms.append(coeff_ref[level + 1])
        keep_ref[level] = 1.0 - here * total(terms)
        square_ref[level] = here * here
        inverse_ref[level] = 1.0 / here
    sweep(field_ref, other_ref, keep_ref, square_ref, False)
    sweep(other_ref, out_ref, keep_ref, square_ref, False)

    def pair(index, carry):
        sweep(out_ref, other_ref, keep_ref, square_ref, False)
        sweep(other_ref, out_ref, keep_ref, square_ref, False)
        return carry

    lax.fori_loop(0, SWEEPS // 2 - 1, pair, 0)
    for level in range(levels):
        for row in range(rows):
            out_ref[level, row] = out_ref[level, row] * inverse_ref[level, pl.ds(row, 1), :]

    for level in range(levels):
        for row in range(folded_rows):
            coeff_strip_ref[level, pl.ds(row, 1), :] = own_coefficient_strip(
                coeff_ref, level, row
            )[0:1]


def finish_kernel(
    owner_ref,
    pert_ref,
    interior_ref,
    strip_ref,
    coeff_strip_ref,
    from_left_ref,
    from_right_ref,
    out_ref,
    first_ref,
    second_ref,
    keep_ref,
    square_ref,
    inverse_ref,
    local_ref,
    sum_ref,
):
    members, terms, levels, rows, lanes = pert_ref.shape
    slab_rows = out_ref.shape[2]
    folded_rows, slots, packs = pack_sizes(rows)
    block = lanes // 2 // slots
    for level in range(levels):
        for pack in range(packs):
            place = level * packs + pack
            left = from_left_ref[pl.ds(place * members, members), :]
            right = from_right_ref[pl.ds(place * members, members), :]
            for slot in range(slots):
                row = pack * slots + slot
                first_ref[level, row] = joined_strip(
                    strip_ref[level, row], left, right, slot, block
                )

    planes = []
    for level in range(levels):
        plane = []
        for pack in range(packs):
            place = pl.ds(levels * packs * members + level * packs + pack, 1)
            for slot in range(slots):
                row = pack * slots + slot
                plane.append(
                    joined_strip(
                        spread(coeff_strip_ref[level, pl.ds(row, 1), :]),
                        spread(from_left_ref[place, :]),
                        spread(from_right_ref[place, :]),
                        slot,
                        block,
                    )
                )
        planes.append(plane)
    for level in range(levels):
        for row in range(folded_rows):
            here = planes[level][row]
            keep = 1.0 - here * around(planes, level, row, True)
            inverse = 1.0 / jnp.where(here > 0.0, here, 1.0)
            keep_ref[level, pl.ds(row, 1), :] = keep[0:1]
            square_ref[level, pl.ds(row, 1), :] = (here * here)[0:1]
            inverse_ref[level, pl.ds(row, 1), :] = inverse[0:1]

    def pair(index, carry):
        sweep(first_ref, second_ref, keep_ref, square_ref, True)
        sweep(second_ref, first_ref, keep_ref, square_ref, True)
        return carry

    lax.fori_loop(0, SWEEPS // 2, pair, 0)
    lane = lane_index((members, lanes))
    for level in range(levels):
        for row in range(folded_rows):
            ends = strip_ends(first_ref[level, row] * inverse_ref[level, pl.ds(row, 1), :])
            for target, end in zip((row, rows - 1 - row), ends):
                local_ref[pl.ds((level * rows + target) * members, members), :] = jnp.where(
                    (lane < SWEEPS) | (lane >= lanes - SWEEPS), end, interior_ref[level, target]
                )

    def add_level(level, carry):
        base = level * rows
        fields = [
            local_ref[pl.ds(base * members + member, rows, stride=members), :]
            for member in range(members)
        ]
        for term in range(terms):
            start = pl.multiple_of(term * levels * rows + base, rows)
            sum_ref[pl.ds(start, rows), :] = total(
                pert_ref[member, term, level].astype(jnp.float32) * fields[member]
                for member in range(members)
            )
        return carry

    lax.fori_loop(0, levels, add_level, 0)
    for slab in range(rows // slab_rows):
        owner = owner_ref[slab]
        for term in range(terms):
            for inner in range(slab_rows):
                row = slab * slab_rows + inner
                out_ref[owner, term, inner] = sum_ref[
                    pl.ds(term * levels * rows + row, levels, stride=rows), :
                ]


def whole(memory_space=pltpu.VMEM):
    return pl.BlockSpec(memory_space=memory_space)


def local_call(kernel, name, outs, scratch, operands, places, work):
    def shape_of(out):
        return out if isinstance(out, jax.ShapeDtypeStruct) else jax.ShapeDtypeStruct(out, jnp.float32)

    shapes = tuple(shape_of(out) for out in outs)
    specs = tuple(whole() for _ in outs)
    moved = sum(math.prod(x.shape) * x.dtype.itemsize for x in tuple(operands) + shapes)
    single = len(outs) == 1
    return pl.pallas_call(
        kernel,
        out_shape=shapes[0] if single else shapes,
        in_specs=[whole(place) for place in places],
        out_specs=specs[0] if single else specs,
        scratch_shapes=[
            pltpu.VMEM(item, jnp.float32) if isinstance(item, tuple) else item for item in scratch
        ],
        compiler_params=pltpu.CompilerParams(vmem_limit_bytes=VMEM_LIMIT),
        cost_estimate=pl.CostEstimate(flops=work, bytes_accessed=moved, transcendentals=0),
        name=name,
    )(*operands)


def body(perturbations, gradient_store, diffusivity, slab_owner):
    members, slots, variables, levels, rows, lanes = perturbations.shape
    terms = slots * variables
    n_member = lax.axis_size("member")
    n_tile = lax.axis_size("tile")
    slab_rows = gradient_store.shape[3]
    folded_rows, _, packs = pack_sizes(rows)
    cells = levels * rows * lanes
    wide_strip = (levels, folded_rows, members, lanes)
    strip_shape = (levels, folded_rows, lanes)
    wide_field = (levels, rows, members, lanes)
    flat_field = (levels * rows * members, lanes)
    field_coeff = (levels, rows, lanes)
    edge_shape = (levels * packs * (members + 1), lanes)
    grad_shape = (terms * levels * rows, lanes)
    hbm, vmem, smem = pltpu.HBM, pltpu.VMEM, pltpu.SMEM

    pert = perturbations.reshape(members, terms, levels, rows, lanes)
    slab = gradient_store.reshape(terms, levels, slab_rows, lanes).swapaxes(1, 2)
    gathered = lax.all_gather(slab, "member", axis=0, tiled=False)

    field, strip, to_right, to_left, pert_here = local_call(
        weigh_kernel,
        "weigh",
        [
            flat_field,
            wide_strip,
            edge_shape,
            edge_shape,
            jax.ShapeDtypeStruct(pert.shape, pert.dtype),
        ],
        [
            pltpu.SMEM(slab_owner.shape, slab_owner.dtype),
            field_coeff,
            grad_shape,
            pltpu.SemaphoreType.DMA,
            pltpu.SemaphoreType.DMA,
            pltpu.SemaphoreType.DMA((math.gcd(members, CHUNKS),)),
        ],
        (gathered,) + tuple(
            pltpu.with_memory_space_constraint(x, hbm) for x in (slab_owner, pert, diffusivity)
        ),
        (vmem, hbm, hbm, hbm),
        2 * terms * members * cells,
    )
    up = [(i, i + 1) for i in range(n_tile - 1)]
    down = [(i + 1, i) for i in range(n_tile - 1)]
    from_left = lax.ppermute(to_right, "tile", up)
    from_right = lax.ppermute(to_left, "tile", down)

    interior, coeff_strip = local_call(
        interior_kernel,
        "interior",
        [wide_field, strip_shape],
        [wide_field, field_coeff, field_coeff, field_coeff],
        (field.reshape(wide_field), diffusivity),
        (vmem, vmem),
        8 * SWEEPS * members * cells,
    )
    sums = local_call(
        finish_kernel,
        "finish",
        [(n_member, terms, slab_rows, levels, lanes)],
        [wide_strip, wide_strip, strip_shape, strip_shape, strip_shape, flat_field, grad_shape],
        (slab_owner, pert_here, interior, strip, coeff_strip, from_left, from_right),
        (smem,) + (vmem,) * 6,
        2 * terms * members * cells,
    )
    received = lax.all_to_all(sums, "member", 0, 0, tiled=True)
    norm_factor = 1.0 / (members * n_member - 1)
    owned = jnp.sum(received, axis=0) * norm_factor
    return owned.swapaxes(1, 2).reshape(slots, variables, levels, slab_rows, lanes)


def solution(mesh):
    in_specs = (
        P("member", None, None, None, None, "tile"),
        P(None, None, None, "member", "tile"),
        P(None, None, "tile"),
        P(),
    )
    out_specs = P(None, None, None, "member", "tile")
    return jax.shard_map(body, mesh=mesh, in_specs=in_specs, out_specs=out_specs, check_vma=False)
```

```python
import math

import jax
import jax.numpy as jnp
from jax import lax
from jax.experimental import pallas as pl
from jax.experimental.pallas import tpu as pltpu
from jax.sharding import PartitionSpec as P

SWEEPS = 10
SLOTS = 4
STAGE_WORK = 10**10
VMEM_LIMIT = 16 * 1024 * 1024


def lane_roll(value, shift):
    shift = shift % value.shape[-1]
    return value if shift == 0 else pltpu.roll(value, shift, 1)


def lane_index(shape):
    return lax.broadcasted_iota(jnp.int32, shape, 1)


def pick(values, which):
    result = values[0]
    for index in range(1, len(values)):
        result = jnp.where(which == index, values[index], result)
    return result


def spread(row, rows=8):
    return jnp.broadcast_to(row, (rows, row.shape[-1]))


def pack_sizes(rows):
    folded_rows = rows // 2
    slots = min(SLOTS, folded_rows)
    return folded_rows, slots, folded_rows // slots


def own_strip(near, far):
    lanes = near.shape[-1]
    half, part = lanes // 2, lanes // 4
    lane = lane_index(near.shape)
    far = lane_roll(far, half)
    start = half - SWEEPS
    first = jnp.where((lane >= start) & (lane < start + part), far, near)
    start = half + SWEEPS - part
    second = jnp.where((lane >= start) & (lane < start + part), far, near)
    return jnp.where(
        lane % half < part,
        lane_roll(first, SWEEPS),
        lane_roll(second, half - SWEEPS),
    )


def strip_ends(strip):
    lanes = strip.shape[-1]
    half, part = lanes // 2, lanes // 4
    lane = lane_index(strip.shape)
    ends = jnp.where(
        lane % half < part, lane_roll(strip, -SWEEPS), lane_roll(strip, half + SWEEPS)
    )
    return ends, lane_roll(ends, half)


def packed_edges(strips):
    lanes = strips[0].shape[-1]
    half = lanes // 2
    block = half // len(strips)
    slot = (lane_index(strips[0].shape) % half) // block
    to_right = pick([lane_roll(s, i * block) for i, s in enumerate(strips)], slot)
    to_left = pick([lane_roll(s, (i + 1) * block - half) for i, s in enumerate(strips)], slot)
    return to_right, to_left


def joined_strip(own, from_left, from_right, slot, block):
    lanes = own.shape[-1]
    half = lanes // 2
    place = lane_index(own.shape) % half
    left = lane_roll(from_left, -slot * block)
    right = lane_roll(from_right, half - (slot + 1) * block)
    return jnp.where(place < SWEEPS, left, jnp.where(place >= half - SWEEPS, right, own))


def total(terms):
    terms = list(terms)
    while len(terms) > 1:
        terms = [
            terms[i] + terms[i + 1] if i + 1 < len(terms) else terms[i]
            for i in range(0, len(terms), 2)
        ]
    return terms[0]


def around(planes, level, row, folded):
    levels, rows = len(planes), len(planes[level])
    here = planes[level][row]
    terms = [lane_roll(here, 1), lane_roll(here, -1)]
    if row > 0:
        terms.append(planes[level][row - 1])
    if row < rows - 1:
        terms.append(planes[level][row + 1])
    elif folded:
        terms.append(lane_roll(here, here.shape[-1] // 2))
    if level > 0:
        terms.append(planes[level - 1][row])
    if level < levels - 1:
        terms.append(planes[level + 1][row])
    return total(terms)


def sweep(source, target, keep_at, square_at, folded):
    levels, rows = source.shape[0], source.shape[1]
    planes = [[source[level, row] for row in range(rows)] for level in range(levels)]
    for level in range(levels):
        for row in range(rows):
            target[level, row] = keep_at(level, row) * planes[level][row] + square_at(
                level, row
            ) * around(planes, level, row, folded)


def level_rows(coeff_ref, row):
    levels = coeff_ref.shape[0]
    return jnp.concatenate([coeff_ref[level, pl.ds(row, 1), :] for level in range(levels)], axis=0)


def own_coefficient_strip(coeff_ref, row):
    rows = coeff_ref.shape[1]
    return own_strip(level_rows(coeff_ref, row), level_rows(coeff_ref, rows - 1 - row))


def stage_kernel(slab_hbm, slab_ref, sem):
    copy = pltpu.make_async_copy(slab_hbm, slab_ref, sem)
    copy.start()
    copy.wait()


def weigh_kernel(
    owner_ref, gathered_ref, pert_ref, coeff_ref, field_ref, strip_ref, right_ref, left_ref, grad_ref
):
    members, terms, levels, rows, lanes = pert_ref.shape
    slab_rows = gathered_ref.shape[2]
    folded_rows, slots, packs = pack_sizes(rows)
    for pack in range(packs):
        strips = [own_coefficient_strip(coeff_ref, pack * slots + slot) for slot in range(slots)]
        for ref, packed in zip((right_ref, left_ref), packed_edges(strips)):
            ref[pl.ds(levels * (packs * members + pack), levels), :] = packed

    for slab in range(rows // slab_rows):
        owner = owner_ref[slab]
        for inner in range(slab_rows):
            row = slab * slab_rows + inner
            coeff = level_rows(coeff_ref, row)
            for term in range(terms):
                grad_ref[pl.ds(term * levels * rows + row, levels, stride=rows), :] = (
                    coeff * gathered_ref[owner, term, inner]
                )

    def weigh_level(level, carry):
        base = level * rows
        gradients = [
            grad_ref[pl.ds(pl.multiple_of(term * levels * rows + base, rows), rows), :]
            for term in range(terms)
        ]
        for member in range(members):
            field_ref[pl.ds(base * members + member, rows, stride=members), :] = total(
                pert_ref[member, term, level].astype(jnp.float32) * gradients[term]
                for term in range(terms)
            )
        return carry

    lax.fori_loop(0, levels, weigh_level, 0)

    def field_at(level, row):
        return field_ref[pl.ds((level * rows + row) * members, members), :]

    for level in range(levels):
        for pack in range(packs):
            strips = []
            for slot in range(slots):
                row = pack * slots + slot
                strip = own_strip(field_at(level, row), field_at(level, rows - 1 - row))
                strip_ref[level, row] = strip
                strips.append(strip)
            place = level * packs + pack
            for ref, packed in zip((right_ref, left_ref), packed_edges(strips)):
                ref[pl.ds(place * members, members), :] = packed


def interior_kernel(
    field_ref,
    coeff_ref,
    out_ref,
    coeff_strip_ref,
    other_ref,
    keep_ref,
    square_ref,
    inverse_ref,
):
    levels, rows, members, lanes = field_ref.shape
    folded_rows = rows // 2
    row_index = lax.broadcasted_iota(jnp.int32, (rows, lanes), 0)
    for level in range(levels):
        here = coeff_ref[level]
        terms = [
            lane_roll(here, 1),
            lane_roll(here, -1),
            jnp.where(row_index > 0, pltpu.roll(here, 1, 0), 0.0),
            jnp.where(row_index < rows - 1, pltpu.roll(here, rows - 1, 0), 0.0),
        ]
        if level > 0:
            terms.append(coeff_ref[level - 1])
        if level < levels - 1:
            terms.append(coeff_ref[level + 1])
        keep_ref[level] = 1.0 - here * total(terms)
        square_ref[level] = here * here
        inverse_ref[level] = 1.0 / here
    def keep_at(level, row):
        return keep_ref[level, pl.ds(row, 1), :]

    def square_at(level, row):
        return square_ref[level, pl.ds(row, 1), :]

    sweep(field_ref, other_ref, keep_at, square_at, False)
    sweep(other_ref, out_ref, keep_at, square_at, False)

    def pair(index, carry):
        sweep(out_ref, other_ref, keep_at, square_at, False)
        sweep(other_ref, out_ref, keep_at, square_at, False)
        return carry

    lax.fori_loop(0, SWEEPS // 2 - 1, pair, 0)
    for level in range(levels):
        for row in range(rows):
            out_ref[level, row] = out_ref[level, row] * inverse_ref[level, pl.ds(row, 1), :]

    for row in range(folded_rows):
        coeff_strip_ref[row] = own_coefficient_strip(coeff_ref, row)


def finish_kernel(
    owner_ref,
    pert_ref,
    interior_ref,
    strip_ref,
    coeff_strip_ref,
    from_left_ref,
    from_right_ref,
    out_ref,
    first_ref,
    second_ref,
    keep_ref,
    square_ref,
    inverse_ref,
    local_ref,
    sum_ref,
):
    members, terms, levels, rows, lanes = pert_ref.shape
    slab_rows = out_ref.shape[2]
    folded_rows, slots, packs = pack_sizes(rows)
    block = lanes // 2 // slots
    for level in range(levels):
        for pack in range(packs):
            place = level * packs + pack
            left = from_left_ref[pl.ds(place * members, members), :]
            right = from_right_ref[pl.ds(place * members, members), :]
            for slot in range(slots):
                row = pack * slots + slot
                first_ref[level, row] = joined_strip(
                    strip_ref[level, row], left, right, slot, block
                )

    strips = []
    for pack in range(packs):
        place = pl.ds(levels * (packs * members + pack), levels)
        for slot in range(slots):
            own = coeff_strip_ref[pack * slots + slot]
            strips.append(
                joined_strip(own, from_left_ref[place, :], from_right_ref[place, :], slot, block)
            )
    level_index = lax.broadcasted_iota(jnp.int32, (levels, lanes), 0)
    for row, here in enumerate(strips):
        terms_here = [
            lane_roll(here, 1),
            lane_roll(here, -1),
            jnp.where(level_index > 0, pltpu.roll(here, 1, 0), 0.0),
            jnp.where(level_index < levels - 1, pltpu.roll(here, levels - 1, 0), 0.0),
            strips[row + 1] if row < folded_rows - 1 else lane_roll(here, lanes // 2),
        ]
        if row > 0:
            terms_here.append(strips[row - 1])
        keep_ref[row] = 1.0 - here * total(terms_here)
        square_ref[row] = here * here
        inverse_ref[row] = 1.0 / jnp.where(here > 0.0, here, 1.0)

    def keep_at(level, row):
        return keep_ref[row, pl.ds(level, 1), :]

    def square_at(level, row):
        return square_ref[row, pl.ds(level, 1), :]

    def pair(index, carry):
        sweep(first_ref, second_ref, keep_at, square_at, True)
        sweep(second_ref, first_ref, keep_at, square_at, True)
        return carry

    lax.fori_loop(0, SWEEPS // 2, pair, 0)
    lane = lane_index((members, lanes))
    for level in range(levels):
        for row in range(folded_rows):
            ends = strip_ends(first_ref[level, row] * inverse_ref[row, pl.ds(level, 1), :])
            for target, end in zip((row, rows - 1 - row), ends):
                local_ref[pl.ds((level * rows + target) * members, members), :] = jnp.where(
                    (lane < SWEEPS) | (lane >= lanes - SWEEPS), end, interior_ref[level, target]
                )

    def add_level(level, carry):
        base = level * rows
        fields = [
            local_ref[pl.ds(base * members + member, rows, stride=members), :]
            for member in range(members)
        ]
        for term in range(terms):
            start = pl.multiple_of(term * levels * rows + base, rows)
            sum_ref[pl.ds(start, rows), :] = total(
                pert_ref[member, term, level].astype(jnp.float32) * fields[member]
                for member in range(members)
            )
        return carry

    lax.fori_loop(0, levels, add_level, 0)
    for slab in range(rows // slab_rows):
        owner = owner_ref[slab]
        for term in range(terms):
            for inner in range(slab_rows):
                row = slab * slab_rows + inner
                out_ref[owner, term, inner] = sum_ref[
                    pl.ds(term * levels * rows + row, levels, stride=rows), :
                ]


def whole(memory_space=pltpu.VMEM):
    return pl.BlockSpec(memory_space=memory_space)


def local_call(kernel, name, outs, scratch, operands, places, work):
    def shape_of(out):
        return out if isinstance(out, jax.ShapeDtypeStruct) else jax.ShapeDtypeStruct(out, jnp.float32)

    shapes = tuple(shape_of(out) for out in outs)
    specs = tuple(whole() for _ in outs)
    moved = sum(math.prod(x.shape) * x.dtype.itemsize for x in tuple(operands) + shapes)
    single = len(outs) == 1
    return pl.pallas_call(
        kernel,
        out_shape=shapes[0] if single else shapes,
        in_specs=[whole(place) for place in places],
        out_specs=specs[0] if single else specs,
        scratch_shapes=[
            pltpu.VMEM(item, jnp.float32) if isinstance(item, tuple) else item for item in scratch
        ],
        compiler_params=pltpu.CompilerParams(vmem_limit_bytes=VMEM_LIMIT),
        cost_estimate=pl.CostEstimate(flops=work, bytes_accessed=moved, transcendentals=0),
        name=name,
    )(*operands)


def body(perturbations, gradient_store, diffusivity, slab_owner):
    members, slots, variables, levels, rows, lanes = perturbations.shape
    terms = slots * variables
    n_member = lax.axis_size("member")
    n_tile = lax.axis_size("tile")
    slab_rows = gradient_store.shape[3]
    folded_rows, _, packs = pack_sizes(rows)
    cells = levels * rows * lanes
    wide_strip = (levels, folded_rows, members, lanes)
    strip_shape = (folded_rows, levels, lanes)
    wide_field = (levels, rows, members, lanes)
    flat_field = (levels * rows * members, lanes)
    field_coeff = (levels, rows, lanes)
    edge_shape = (levels * packs * (members + 1), lanes)
    grad_shape = (terms * levels * rows, lanes)
    vmem, smem = pltpu.VMEM, pltpu.SMEM

    pert = perturbations.reshape(members, terms, levels, rows, lanes)
    slab = gradient_store.reshape(terms, levels, slab_rows, lanes).swapaxes(1, 2)
    staged = local_call(
        stage_kernel,
        "stage",
        [slab.shape],
        [pltpu.SemaphoreType.DMA],
        (pltpu.with_memory_space_constraint(slab, pltpu.HBM),),
        (pltpu.HBM,),
        STAGE_WORK,
    )
    gathered = lax.all_gather(staged, "member", axis=0, tiled=False)

    field, strip, to_right, to_left = local_call(
        weigh_kernel,
        "weigh",
        [flat_field, wide_strip, edge_shape, edge_shape],
        [grad_shape],
        (slab_owner, gathered, pert, diffusivity),
        (smem, vmem, vmem, vmem),
        2 * terms * members * cells,
    )
    up = [(i, i + 1) for i in range(n_tile - 1)]
    down = [(i + 1, i) for i in range(n_tile - 1)]
    from_left = lax.ppermute(to_right, "tile", up)
    from_right = lax.ppermute(to_left, "tile", down)

    interior, coeff_strip = local_call(
        interior_kernel,
        "interior",
        [wide_field, strip_shape],
        [wide_field, field_coeff, field_coeff, field_coeff],
        (field.reshape(wide_field), diffusivity),
        (vmem, vmem),
        8 * SWEEPS * members * cells,
    )
    sums = local_call(
        finish_kernel,
        "finish",
        [(n_member, terms, slab_rows, levels, lanes)],
        [wide_strip, wide_strip, strip_shape, strip_shape, strip_shape, flat_field, grad_shape],
        (slab_owner, pert, interior, strip, coeff_strip, from_left, from_right),
        (smem,) + (vmem,) * 6,
        2 * terms * members * cells,
    )
    received = lax.all_to_all(sums, "member", 0, 0, tiled=True)
    norm_factor = 1.0 / (members * n_member - 1)
    owned = jnp.sum(received, axis=0) * norm_factor
    return owned.swapaxes(1, 2).reshape(slots, variables, levels, slab_rows, lanes)


def solution(mesh):
    in_specs = (
        P("member", None, None, None, None, "tile"),
        P(None, None, None, "member", "tile"),
        P(None, None, "tile"),
        P(),
    )
    out_specs = P(None, None, None, "member", "tile")
    return jax.shard_map(body, mesh=mesh, in_specs=in_specs, out_specs=out_specs, check_vma=False)
```

```python
import math

import jax
import jax.numpy as jnp
from jax import lax
from jax.experimental import pallas as pl
from jax.experimental.pallas import tpu as pltpu
from jax.sharding import PartitionSpec as P

SWEEPS = 10
SLOTS = 4
ANCHOR_WORK = 10**10
VMEM_LIMIT = 16 * 1024 * 1024


def lane_roll(value, shift):
    shift = shift % value.shape[-1]
    return value if shift == 0 else pltpu.roll(value, shift, 1)


def lane_index(shape):
    return lax.broadcasted_iota(jnp.int32, shape, 1)


def pick(values, which):
    result = values[0]
    for index in range(1, len(values)):
        result = jnp.where(which == index, values[index], result)
    return result


def spread(row, rows=8):
    return jnp.broadcast_to(row, (rows, row.shape[-1]))


def pack_sizes(rows):
    folded_rows = rows // 2
    slots = min(SLOTS, folded_rows)
    return folded_rows, slots, folded_rows // slots


def own_strip(near, far):
    lanes = near.shape[-1]
    half, part = lanes // 2, lanes // 4
    lane = lane_index(near.shape)
    far = lane_roll(far, half)
    start = half - SWEEPS
    first = jnp.where((lane >= start) & (lane < start + part), far, near)
    start = half + SWEEPS - part
    second = jnp.where((lane >= start) & (lane < start + part), far, near)
    return jnp.where(
        lane % half < part,
        lane_roll(first, SWEEPS),
        lane_roll(second, half - SWEEPS),
    )


def strip_ends(strip):
    lanes = strip.shape[-1]
    half, part = lanes // 2, lanes // 4
    lane = lane_index(strip.shape)
    ends = jnp.where(
        lane % half < part, lane_roll(strip, -SWEEPS), lane_roll(strip, half + SWEEPS)
    )
    return ends, lane_roll(ends, half)


def packed_edges(strips):
    lanes = strips[0].shape[-1]
    half = lanes // 2
    block = half // len(strips)
    slot = (lane_index(strips[0].shape) % half) // block
    to_right = pick([lane_roll(s, i * block) for i, s in enumerate(strips)], slot)
    to_left = pick([lane_roll(s, (i + 1) * block - half) for i, s in enumerate(strips)], slot)
    return to_right, to_left


def joined_strip(own, from_left, from_right, slot, block):
    lanes = own.shape[-1]
    half = lanes // 2
    place = lane_index(own.shape) % half
    left = lane_roll(from_left, -slot * block)
    right = lane_roll(from_right, half - (slot + 1) * block)
    return jnp.where(place < SWEEPS, left, jnp.where(place >= half - SWEEPS, right, own))


def total(terms):
    terms = list(terms)
    while len(terms) > 1:
        terms = [
            terms[i] + terms[i + 1] if i + 1 < len(terms) else terms[i]
            for i in range(0, len(terms), 2)
        ]
    return terms[0]


def around(planes, level, row, folded):
    levels, rows = len(planes), len(planes[level])
    here = planes[level][row]
    terms = [lane_roll(here, 1), lane_roll(here, -1)]
    if row > 0:
        terms.append(planes[level][row - 1])
    if row < rows - 1:
        terms.append(planes[level][row + 1])
    elif folded:
        terms.append(lane_roll(here, here.shape[-1] // 2))
    if level > 0:
        terms.append(planes[level - 1][row])
    if level < levels - 1:
        terms.append(planes[level + 1][row])
    return total(terms)


def sweep(source, target, keep_at, square_at, folded):
    levels, rows = source.shape[0], source.shape[1]
    planes = [[source[level, row] for row in range(rows)] for level in range(levels)]
    for level in range(levels):
        for row in range(rows):
            target[level, row] = keep_at(level, row) * planes[level][row] + square_at(
                level, row
            ) * around(planes, level, row, folded)


def level_rows(coeff_ref, row):
    levels = coeff_ref.shape[0]
    return jnp.concatenate([coeff_ref[level, pl.ds(row, 1), :] for level in range(levels)], axis=0)


def own_coefficient_strip(coeff_ref, row):
    rows = coeff_ref.shape[1]
    return own_strip(level_rows(coeff_ref, row), level_rows(coeff_ref, rows - 1 - row))


def anchor_kernel(out_ref):
    out_ref[...] = jnp.zeros_like(out_ref)


def weigh_kernel(
    owner_ref,
    gathered_ref,
    pert_ref,
    coeff_ref,
    anchor_ref,
    field_ref,
    strip_ref,
    right_ref,
    left_ref,
    grad_ref,
):
    members, terms, levels, rows, lanes = pert_ref.shape
    slab_rows = gathered_ref.shape[2]
    folded_rows, slots, packs = pack_sizes(rows)
    for pack in range(packs):
        strips = [own_coefficient_strip(coeff_ref, pack * slots + slot) for slot in range(slots)]
        for ref, packed in zip((right_ref, left_ref), packed_edges(strips)):
            ref[pl.ds(levels * (packs * members + pack), levels), :] = packed

    for slab in range(rows // slab_rows):
        owner = owner_ref[slab]
        for inner in range(slab_rows):
            row = slab * slab_rows + inner
            coeff = level_rows(coeff_ref, row)
            for term in range(terms):
                grad_ref[pl.ds(term * levels * rows + row, levels, stride=rows), :] = (
                    coeff * gathered_ref[owner, term, inner]
                )

    def weigh_level(level, carry):
        base = level * rows
        gradients = [
            grad_ref[pl.ds(pl.multiple_of(term * levels * rows + base, rows), rows), :]
            for term in range(terms)
        ]
        for member in range(members):
            field_ref[pl.ds(base * members + member, rows, stride=members), :] = total(
                pert_ref[member, term, level].astype(jnp.float32) * gradients[term]
                for term in range(terms)
            )
        return carry

    lax.fori_loop(0, levels, weigh_level, 0)

    def field_at(level, row):
        return field_ref[pl.ds((level * rows + row) * members, members), :]

    for level in range(levels):
        for pack in range(packs):
            strips = []
            for slot in range(slots):
                row = pack * slots + slot
                strip = own_strip(field_at(level, row), field_at(level, rows - 1 - row))
                strip_ref[level, row] = strip
                strips.append(strip)
            place = level * packs + pack
            for ref, packed in zip((right_ref, left_ref), packed_edges(strips)):
                ref[pl.ds(place * members, members), :] = packed


def interior_kernel(
    field_ref,
    coeff_ref,
    out_ref,
    coeff_strip_ref,
    other_ref,
    keep_ref,
    square_ref,
    inverse_ref,
):
    levels, rows, members, lanes = field_ref.shape
    folded_rows = rows // 2
    row_index = lax.broadcasted_iota(jnp.int32, (rows, lanes), 0)
    for level in range(levels):
        here = coeff_ref[level]
        terms = [
            lane_roll(here, 1),
            lane_roll(here, -1),
            jnp.where(row_index > 0, pltpu.roll(here, 1, 0), 0.0),
            jnp.where(row_index < rows - 1, pltpu.roll(here, rows - 1, 0), 0.0),
        ]
        if level > 0:
            terms.append(coeff_ref[level - 1])
        if level < levels - 1:
            terms.append(coeff_ref[level + 1])
        keep_ref[level] = 1.0 - here * total(terms)
        square_ref[level] = here * here
        inverse_ref[level] = 1.0 / here
    def keep_at(level, row):
        return keep_ref[level, pl.ds(row, 1), :]

    def square_at(level, row):
        return square_ref[level, pl.ds(row, 1), :]

    sweep(field_ref, other_ref, keep_at, square_at, False)
    sweep(other_ref, out_ref, keep_at, square_at, False)

    def pair(index, carry):
        sweep(out_ref, other_ref, keep_at, square_at, False)
        sweep(other_ref, out_ref, keep_at, square_at, False)
        return carry

    lax.fori_loop(0, SWEEPS // 2 - 1, pair, 0)
    for level in range(levels):
        for row in range(rows):
            out_ref[level, row] = out_ref[level, row] * inverse_ref[level, pl.ds(row, 1), :]

    for row in range(folded_rows):
        coeff_strip_ref[row] = own_coefficient_strip(coeff_ref, row)


def finish_kernel(
    owner_ref,
    pert_ref,
    interior_ref,
    strip_ref,
    coeff_strip_ref,
    from_left_ref,
    from_right_ref,
    out_ref,
    first_ref,
    second_ref,
    keep_ref,
    square_ref,
    inverse_ref,
    local_ref,
    sum_ref,
):
    members, terms, levels, rows, lanes = pert_ref.shape
    slab_rows = out_ref.shape[2]
    folded_rows, slots, packs = pack_sizes(rows)
    block = lanes // 2 // slots
    for level in range(levels):
        for pack in range(packs):
            place = level * packs + pack
            left = from_left_ref[pl.ds(place * members, members), :]
            right = from_right_ref[pl.ds(place * members, members), :]
            for slot in range(slots):
                row = pack * slots + slot
                first_ref[level, row] = joined_strip(
                    strip_ref[level, row], left, right, slot, block
                )

    strips = []
    for pack in range(packs):
        place = pl.ds(levels * (packs * members + pack), levels)
        for slot in range(slots):
            own = coeff_strip_ref[pack * slots + slot]
            strips.append(
                joined_strip(own, from_left_ref[place, :], from_right_ref[place, :], slot, block)
            )
    level_index = lax.broadcasted_iota(jnp.int32, (levels, lanes), 0)
    for row, here in enumerate(strips):
        terms_here = [
            lane_roll(here, 1),
            lane_roll(here, -1),
            jnp.where(level_index > 0, pltpu.roll(here, 1, 0), 0.0),
            jnp.where(level_index < levels - 1, pltpu.roll(here, levels - 1, 0), 0.0),
            strips[row + 1] if row < folded_rows - 1 else lane_roll(here, lanes // 2),
        ]
        if row > 0:
            terms_here.append(strips[row - 1])
        keep_ref[row] = 1.0 - here * total(terms_here)
        square_ref[row] = here * here
        inverse_ref[row] = 1.0 / jnp.where(here > 0.0, here, 1.0)

    def keep_at(level, row):
        return keep_ref[row, pl.ds(level, 1), :]

    def square_at(level, row):
        return square_ref[row, pl.ds(level, 1), :]

    def pair(index, carry):
        sweep(first_ref, second_ref, keep_at, square_at, True)
        sweep(second_ref, first_ref, keep_at, square_at, True)
        return carry

    lax.fori_loop(0, SWEEPS // 2, pair, 0)
    lane = lane_index((members, lanes))
    for level in range(levels):
        for row in range(folded_rows):
            ends = strip_ends(first_ref[level, row] * inverse_ref[row, pl.ds(level, 1), :])
            for target, end in zip((row, rows - 1 - row), ends):
                local_ref[pl.ds((level * rows + target) * members, members), :] = jnp.where(
                    (lane < SWEEPS) | (lane >= lanes - SWEEPS), end, interior_ref[level, target]
                )

    def add_level(level, carry):
        base = level * rows
        fields = [
            local_ref[pl.ds(base * members + member, rows, stride=members), :]
            for member in range(members)
        ]
        for term in range(terms):
            start = pl.multiple_of(term * levels * rows + base, rows)
            sum_ref[pl.ds(start, rows), :] = total(
                pert_ref[member, term, level].astype(jnp.float32) * fields[member]
                for member in range(members)
            )
        return carry

    lax.fori_loop(0, levels, add_level, 0)
    for slab in range(rows // slab_rows):
        owner = owner_ref[slab]
        for term in range(terms):
            for inner in range(slab_rows):
                row = slab * slab_rows + inner
                out_ref[owner, term, inner] = sum_ref[
                    pl.ds(term * levels * rows + row, levels, stride=rows), :
                ]


def whole(memory_space=pltpu.VMEM):
    return pl.BlockSpec(memory_space=memory_space)


def local_call(kernel, name, outs, scratch, operands, places, work):
    def shape_of(out):
        return out if isinstance(out, jax.ShapeDtypeStruct) else jax.ShapeDtypeStruct(out, jnp.float32)

    shapes = tuple(shape_of(out) for out in outs)
    specs = tuple(whole() for _ in outs)
    moved = sum(math.prod(x.shape) * x.dtype.itemsize for x in tuple(operands) + shapes)
    single = len(outs) == 1
    return pl.pallas_call(
        kernel,
        out_shape=shapes[0] if single else shapes,
        in_specs=[whole(place) for place in places],
        out_specs=specs[0] if single else specs,
        scratch_shapes=[
            pltpu.VMEM(item, jnp.float32) if isinstance(item, tuple) else item for item in scratch
        ],
        compiler_params=pltpu.CompilerParams(vmem_limit_bytes=VMEM_LIMIT),
        cost_estimate=pl.CostEstimate(flops=work, bytes_accessed=moved, transcendentals=0),
        name=name,
    )(*operands)


def body(perturbations, gradient_store, diffusivity, slab_owner):
    members, slots, variables, levels, rows, lanes = perturbations.shape
    terms = slots * variables
    n_member = lax.axis_size("member")
    n_tile = lax.axis_size("tile")
    slab_rows = gradient_store.shape[3]
    folded_rows, _, packs = pack_sizes(rows)
    cells = levels * rows * lanes
    wide_strip = (levels, folded_rows, members, lanes)
    strip_shape = (folded_rows, levels, lanes)
    wide_field = (levels, rows, members, lanes)
    flat_field = (levels * rows * members, lanes)
    field_coeff = (levels, rows, lanes)
    edge_shape = (levels * packs * (members + 1), lanes)
    grad_shape = (terms * levels * rows, lanes)
    vmem, smem = pltpu.VMEM, pltpu.SMEM

    pert = perturbations.reshape(members, terms, levels, rows, lanes)
    slab = gradient_store.reshape(terms, levels, slab_rows, lanes).swapaxes(1, 2)
    anchor = local_call(anchor_kernel, "anchor", [(8, lanes)], [], (), (), ANCHOR_WORK)
    gathered = lax.all_gather(slab, "member", axis=0, tiled=False)

    field, strip, to_right, to_left = local_call(
        weigh_kernel,
        "weigh",
        [flat_field, wide_strip, edge_shape, edge_shape],
        [grad_shape],
        (slab_owner, gathered, pert, diffusivity, anchor),
        (smem, vmem, vmem, vmem, vmem),
        2 * terms * members * cells,
    )
    up = [(i, i + 1) for i in range(n_tile - 1)]
    down = [(i + 1, i) for i in range(n_tile - 1)]
    from_left = lax.ppermute(to_right, "tile", up)
    from_right = lax.ppermute(to_left, "tile", down)

    interior, coeff_strip = local_call(
        interior_kernel,
        "interior",
        [wide_field, strip_shape],
        [wide_field, field_coeff, field_coeff, field_coeff],
        (field.reshape(wide_field), diffusivity),
        (vmem, vmem),
        8 * SWEEPS * members * cells,
    )
    sums = local_call(
        finish_kernel,
        "finish",
        [(n_member, terms, slab_rows, levels, lanes)],
        [wide_strip, wide_strip, strip_shape, strip_shape, strip_shape, flat_field, grad_shape],
        (slab_owner, pert, interior, strip, coeff_strip, from_left, from_right),
        (smem,) + (vmem,) * 6,
        2 * terms * members * cells,
    )
    received = lax.all_to_all(sums, "member", 0, 0, tiled=True)
    norm_factor = 1.0 / (members * n_member - 1)
    owned = jnp.sum(received, axis=0) * norm_factor
    return owned.swapaxes(1, 2).reshape(slots, variables, levels, slab_rows, lanes)


def solution(mesh):
    in_specs = (
        P("member", None, None, None, None, "tile"),
        P(None, None, None, "member", "tile"),
        P(None, None, "tile"),
        P(),
    )
    out_specs = P(None, None, None, "member", "tile")
    return jax.shard_map(body, mesh=mesh, in_specs=in_specs, out_specs=out_specs, check_vma=False)
```

```python
import math

import jax
import jax.numpy as jnp
from jax import lax
from jax.experimental import pallas as pl
from jax.experimental.pallas import tpu as pltpu
from jax.sharding import PartitionSpec as P

SWEEPS = 10
SLOTS = 4
ANCHOR_WORK = 10**10
VMEM_LIMIT = 16 * 1024 * 1024


def lane_roll(value, shift):
    shift = shift % value.shape[-1]
    return value if shift == 0 else pltpu.roll(value, shift, 1)


def lane_index(shape):
    return lax.broadcasted_iota(jnp.int32, shape, 1)


def pick(values, which):
    result = values[0]
    for index in range(1, len(values)):
        result = jnp.where(which == index, values[index], result)
    return result


def spread(row, rows=8):
    return jnp.broadcast_to(row, (rows, row.shape[-1]))


def pack_sizes(rows):
    folded_rows = rows // 2
    slots = min(SLOTS, folded_rows)
    return folded_rows, slots, folded_rows // slots


def own_strip(near, far):
    lanes = near.shape[-1]
    half, part = lanes // 2, lanes // 4
    lane = lane_index(near.shape)
    far = lane_roll(far, half)
    start = half - SWEEPS
    first = jnp.where((lane >= start) & (lane < start + part), far, near)
    start = half + SWEEPS - part
    second = jnp.where((lane >= start) & (lane < start + part), far, near)
    return jnp.where(
        lane % half < part,
        lane_roll(first, SWEEPS),
        lane_roll(second, half - SWEEPS),
    )


def strip_ends(strip):
    lanes = strip.shape[-1]
    half, part = lanes // 2, lanes // 4
    lane = lane_index(strip.shape)
    ends = jnp.where(
        lane % half < part, lane_roll(strip, -SWEEPS), lane_roll(strip, half + SWEEPS)
    )
    return ends, lane_roll(ends, half)


def packed_edges(strips):
    lanes = strips[0].shape[-1]
    half = lanes // 2
    block = half // len(strips)
    slot = (lane_index(strips[0].shape) % half) // block
    to_right = pick([lane_roll(s, i * block) for i, s in enumerate(strips)], slot)
    to_left = pick([lane_roll(s, (i + 1) * block - half) for i, s in enumerate(strips)], slot)
    return to_right, to_left


def joined_strip(own, from_left, from_right, slot, block):
    lanes = own.shape[-1]
    half = lanes // 2
    place = lane_index(own.shape) % half
    left = lane_roll(from_left, -slot * block)
    right = lane_roll(from_right, half - (slot + 1) * block)
    return jnp.where(place < SWEEPS, left, jnp.where(place >= half - SWEEPS, right, own))


def total(terms):
    terms = list(terms)
    while len(terms) > 1:
        terms = [
            terms[i] + terms[i + 1] if i + 1 < len(terms) else terms[i]
            for i in range(0, len(terms), 2)
        ]
    return terms[0]


def around(planes, level, row, folded):
    levels, rows = len(planes), len(planes[level])
    here = planes[level][row]
    terms = [lane_roll(here, 1), lane_roll(here, -1)]
    if row > 0:
        terms.append(planes[level][row - 1])
    if row < rows - 1:
        terms.append(planes[level][row + 1])
    elif folded:
        terms.append(lane_roll(here, here.shape[-1] // 2))
    if level > 0:
        terms.append(planes[level - 1][row])
    if level < levels - 1:
        terms.append(planes[level + 1][row])
    return total(terms)


def sweep(source, target, keep_at, square_at, folded):
    levels, rows = source.shape[0], source.shape[1]
    planes = [[source[level, row] for row in range(rows)] for level in range(levels)]
    for level in range(levels):
        for row in range(rows):
            target[level, row] = keep_at(level, row) * planes[level][row] + square_at(
                level, row
            ) * around(planes, level, row, folded)


def level_rows(coeff_ref, row):
    levels = coeff_ref.shape[0]
    return jnp.concatenate([coeff_ref[level, pl.ds(row, 1), :] for level in range(levels)], axis=0)


def own_coefficient_strip(coeff_ref, row):
    rows = coeff_ref.shape[1]
    return own_strip(level_rows(coeff_ref, row), level_rows(coeff_ref, rows - 1 - row))


def anchor_kernel(gathered_ref, out_ref):
    out_ref[...] = jnp.zeros_like(out_ref)


def weigh_kernel(
    owner_ref,
    gathered_ref,
    pert_ref,
    coeff_ref,
    anchor_ref,
    field_ref,
    strip_ref,
    right_ref,
    left_ref,
    grad_ref,
):
    members, terms, levels, rows, lanes = pert_ref.shape
    slab_rows = gathered_ref.shape[2]
    folded_rows, slots, packs = pack_sizes(rows)
    for pack in range(packs):
        strips = [own_coefficient_strip(coeff_ref, pack * slots + slot) for slot in range(slots)]
        for ref, packed in zip((right_ref, left_ref), packed_edges(strips)):
            ref[pl.ds(levels * (packs * members + pack), levels), :] = packed

    for slab in range(rows // slab_rows):
        owner = owner_ref[slab]
        for inner in range(slab_rows):
            row = slab * slab_rows + inner
            coeff = level_rows(coeff_ref, row)
            for term in range(terms):
                grad_ref[pl.ds(term * levels * rows + row, levels, stride=rows), :] = (
                    coeff * gathered_ref[owner, term, inner]
                )

    def weigh_level(level, carry):
        base = level * rows
        gradients = [
            grad_ref[pl.ds(pl.multiple_of(term * levels * rows + base, rows), rows), :]
            for term in range(terms)
        ]
        for member in range(members):
            field_ref[pl.ds(base * members + member, rows, stride=members), :] = total(
                pert_ref[member, term, level].astype(jnp.float32) * gradients[term]
                for term in range(terms)
            )
        return carry

    lax.fori_loop(0, levels, weigh_level, 0)

    def field_at(level, row):
        return field_ref[pl.ds((level * rows + row) * members, members), :]

    for level in range(levels):
        for pack in range(packs):
            strips = []
            for slot in range(slots):
                row = pack * slots + slot
                strip = own_strip(field_at(level, row), field_at(level, rows - 1 - row))
                strip_ref[level, row] = strip
                strips.append(strip)
            place = level * packs + pack
            for ref, packed in zip((right_ref, left_ref), packed_edges(strips)):
                ref[pl.ds(place * members, members), :] = packed


def interior_kernel(
    field_ref,
    coeff_ref,
    out_ref,
    coeff_strip_ref,
    other_ref,
    keep_ref,
    square_ref,
    inverse_ref,
):
    levels, rows, members, lanes = field_ref.shape
    folded_rows = rows // 2
    row_index = lax.broadcasted_iota(jnp.int32, (rows, lanes), 0)
    for level in range(levels):
        here = coeff_ref[level]
        terms = [
            lane_roll(here, 1),
            lane_roll(here, -1),
            jnp.where(row_index > 0, pltpu.roll(here, 1, 0), 0.0),
            jnp.where(row_index < rows - 1, pltpu.roll(here, rows - 1, 0), 0.0),
        ]
        if level > 0:
            terms.append(coeff_ref[level - 1])
        if level < levels - 1:
            terms.append(coeff_ref[level + 1])
        keep_ref[level] = 1.0 - here * total(terms)
        square_ref[level] = here * here
        inverse_ref[level] = 1.0 / here
    def keep_at(level, row):
        return keep_ref[level, pl.ds(row, 1), :]

    def square_at(level, row):
        return square_ref[level, pl.ds(row, 1), :]

    sweep(field_ref, other_ref, keep_at, square_at, False)
    sweep(other_ref, out_ref, keep_at, square_at, False)

    def pair(index, carry):
        sweep(out_ref, other_ref, keep_at, square_at, False)
        sweep(other_ref, out_ref, keep_at, square_at, False)
        return carry

    lax.fori_loop(0, SWEEPS // 2 - 1, pair, 0)
    for level in range(levels):
        for row in range(rows):
            out_ref[level, row] = out_ref[level, row] * inverse_ref[level, pl.ds(row, 1), :]

    for row in range(folded_rows):
        coeff_strip_ref[row] = own_coefficient_strip(coeff_ref, row)


def finish_kernel(
    owner_ref,
    pert_ref,
    interior_ref,
    strip_ref,
    coeff_strip_ref,
    from_left_ref,
    from_right_ref,
    out_ref,
    first_ref,
    second_ref,
    keep_ref,
    square_ref,
    inverse_ref,
    local_ref,
    sum_ref,
):
    members, terms, levels, rows, lanes = pert_ref.shape
    slab_rows = out_ref.shape[2]
    folded_rows, slots, packs = pack_sizes(rows)
    block = lanes // 2 // slots
    for level in range(levels):
        for pack in range(packs):
            place = level * packs + pack
            left = from_left_ref[pl.ds(place * members, members), :]
            right = from_right_ref[pl.ds(place * members, members), :]
            for slot in range(slots):
                row = pack * slots + slot
                first_ref[level, row] = joined_strip(
                    strip_ref[level, row], left, right, slot, block
                )

    strips = []
    for pack in range(packs):
        place = pl.ds(levels * (packs * members + pack), levels)
        for slot in range(slots):
            own = coeff_strip_ref[pack * slots + slot]
            strips.append(
                joined_strip(own, from_left_ref[place, :], from_right_ref[place, :], slot, block)
            )
    level_index = lax.broadcasted_iota(jnp.int32, (levels, lanes), 0)
    for row, here in enumerate(strips):
        terms_here = [
            lane_roll(here, 1),
            lane_roll(here, -1),
            jnp.where(level_index > 0, pltpu.roll(here, 1, 0), 0.0),
            jnp.where(level_index < levels - 1, pltpu.roll(here, levels - 1, 0), 0.0),
            strips[row + 1] if row < folded_rows - 1 else lane_roll(here, lanes // 2),
        ]
        if row > 0:
            terms_here.append(strips[row - 1])
        keep_ref[row] = 1.0 - here * total(terms_here)
        square_ref[row] = here * here
        inverse_ref[row] = 1.0 / jnp.where(here > 0.0, here, 1.0)

    def keep_at(level, row):
        return keep_ref[row, pl.ds(level, 1), :]

    def square_at(level, row):
        return square_ref[row, pl.ds(level, 1), :]

    def pair(index, carry):
        sweep(first_ref, second_ref, keep_at, square_at, True)
        sweep(second_ref, first_ref, keep_at, square_at, True)
        return carry

    lax.fori_loop(0, SWEEPS // 2, pair, 0)
    lane = lane_index((members, lanes))
    for level in range(levels):
        for row in range(folded_rows):
            ends = strip_ends(first_ref[level, row] * inverse_ref[row, pl.ds(level, 1), :])
            for target, end in zip((row, rows - 1 - row), ends):
                local_ref[pl.ds((level * rows + target) * members, members), :] = jnp.where(
                    (lane < SWEEPS) | (lane >= lanes - SWEEPS), end, interior_ref[level, target]
                )

    def add_level(level, carry):
        base = level * rows
        fields = [
            local_ref[pl.ds(base * members + member, rows, stride=members), :]
            for member in range(members)
        ]
        for term in range(terms):
            start = pl.multiple_of(term * levels * rows + base, rows)
            sum_ref[pl.ds(start, rows), :] = total(
                pert_ref[member, term, level].astype(jnp.float32) * fields[member]
                for member in range(members)
            )
        return carry

    lax.fori_loop(0, levels, add_level, 0)
    for slab in range(rows // slab_rows):
        owner = owner_ref[slab]
        for term in range(terms):
            for inner in range(slab_rows):
                row = slab * slab_rows + inner
                out_ref[owner, term, inner] = sum_ref[
                    pl.ds(term * levels * rows + row, levels, stride=rows), :
                ]


def whole(memory_space=pltpu.VMEM):
    return pl.BlockSpec(memory_space=memory_space)


def local_call(kernel, name, outs, scratch, operands, places, work):
    def shape_of(out):
        return out if isinstance(out, jax.ShapeDtypeStruct) else jax.ShapeDtypeStruct(out, jnp.float32)

    shapes = tuple(shape_of(out) for out in outs)
    specs = tuple(whole() for _ in outs)
    moved = sum(math.prod(x.shape) * x.dtype.itemsize for x in tuple(operands) + shapes)
    single = len(outs) == 1
    return pl.pallas_call(
        kernel,
        out_shape=shapes[0] if single else shapes,
        in_specs=[whole(place) for place in places],
        out_specs=specs[0] if single else specs,
        scratch_shapes=[
            pltpu.VMEM(item, jnp.float32) if isinstance(item, tuple) else item for item in scratch
        ],
        compiler_params=pltpu.CompilerParams(vmem_limit_bytes=VMEM_LIMIT),
        cost_estimate=pl.CostEstimate(flops=work, bytes_accessed=moved, transcendentals=0),
        name=name,
    )(*operands)


def body(perturbations, gradient_store, diffusivity, slab_owner):
    members, slots, variables, levels, rows, lanes = perturbations.shape
    terms = slots * variables
    n_member = lax.axis_size("member")
    n_tile = lax.axis_size("tile")
    slab_rows = gradient_store.shape[3]
    folded_rows, _, packs = pack_sizes(rows)
    cells = levels * rows * lanes
    wide_strip = (levels, folded_rows, members, lanes)
    strip_shape = (folded_rows, levels, lanes)
    wide_field = (levels, rows, members, lanes)
    flat_field = (levels * rows * members, lanes)
    field_coeff = (levels, rows, lanes)
    edge_shape = (levels * packs * (members + 1), lanes)
    grad_shape = (terms * levels * rows, lanes)
    vmem, smem = pltpu.VMEM, pltpu.SMEM

    pert = perturbations.reshape(members, terms, levels, rows, lanes)
    slab = gradient_store.reshape(terms, levels, slab_rows, lanes).swapaxes(1, 2)
    gathered = lax.all_gather(slab, "member", axis=0, tiled=False)
    anchor = local_call(
        anchor_kernel, "anchor", [(8, lanes)], [], (gathered,), (pl.ANY,), ANCHOR_WORK
    )

    field, strip, to_right, to_left = local_call(
        weigh_kernel,
        "weigh",
        [flat_field, wide_strip, edge_shape, edge_shape],
        [grad_shape],
        (slab_owner, gathered, pert, diffusivity, anchor),
        (smem, vmem, vmem, vmem, vmem),
        2 * terms * members * cells,
    )
    up = [(i, i + 1) for i in range(n_tile - 1)]
    down = [(i + 1, i) for i in range(n_tile - 1)]
    from_left = lax.ppermute(to_right, "tile", up)
    from_right = lax.ppermute(to_left, "tile", down)

    interior, coeff_strip = local_call(
        interior_kernel,
        "interior",
        [wide_field, strip_shape],
        [wide_field, field_coeff, field_coeff, field_coeff],
        (field.reshape(wide_field), diffusivity),
        (vmem, vmem),
        8 * SWEEPS * members * cells,
    )
    sums = local_call(
        finish_kernel,
        "finish",
        [(n_member, terms, slab_rows, levels, lanes)],
        [wide_strip, wide_strip, strip_shape, strip_shape, strip_shape, flat_field, grad_shape],
        (slab_owner, pert, interior, strip, coeff_strip, from_left, from_right),
        (smem,) + (vmem,) * 6,
        2 * terms * members * cells,
    )
    received = lax.all_to_all(sums, "member", 0, 0, tiled=True)
    norm_factor = 1.0 / (members * n_member - 1)
    owned = jnp.sum(received, axis=0) * norm_factor
    return owned.swapaxes(1, 2).reshape(slots, variables, levels, slab_rows, lanes)


def solution(mesh):
    in_specs = (
        P("member", None, None, None, None, "tile"),
        P(None, None, None, "member", "tile"),
        P(None, None, "tile"),
        P(),
    )
    out_specs = P(None, None, None, "member", "tile")
    return jax.shard_map(body, mesh=mesh, in_specs=in_specs, out_specs=out_specs, check_vma=False)
```

```python
import math

import jax
import jax.numpy as jnp
from jax import lax
from jax.experimental import pallas as pl
from jax.experimental.pallas import tpu as pltpu
from jax.sharding import PartitionSpec as P

SWEEPS = 10
GROUPS = 4
ANCHOR_WORK = 10**10
VMEM_LIMIT = 16 * 1024 * 1024


def lane_roll(value, shift):
    shift = shift % value.shape[-1]
    return value if shift == 0 else pltpu.roll(value, shift, 1)


def lane_index(shape):
    return lax.broadcasted_iota(jnp.int32, shape, 1)


def spread(row, rows=8):
    return jnp.broadcast_to(row, (rows, row.shape[-1]))


def whole(memory_space=pltpu.VMEM):
    return pl.BlockSpec(memory_space=memory_space)


def mirrors(level, row, levels, rows):
    return [
        (far_level, far_row)
        for far_level in (level, levels - 1 - level)
        for far_row in (row, rows - 1 - row)
    ]


def group_index(shape, start):
    part = shape[-1] // GROUPS
    return (lane_index(shape) + start) % shape[-1] // part


def own_strips(values):
    part = values[0].shape[-1] // GROUPS
    rolled = [lane_roll(value, part * g) for g, value in enumerate(values)]
    both = []
    for start in (SWEEPS, part - SWEEPS):
        group = group_index(values[0].shape, start)
        strip = rolled[0]
        for g in range(1, GROUPS):
            strip = jnp.where(group == g, rolled[g], strip)
        both.append(strip)
    return both


def packed_edges(first, second):
    part = first.shape[-1] // GROUPS
    place = lane_index(first.shape) % part
    moved = lane_roll(second, part // 2)
    to_right = jnp.where(place >= part // 2, first, moved)
    to_left = jnp.where(place < part // 2, first, moved)
    return to_right, to_left


def joined_strip(own, edge, index, is_left):
    part = own.shape[-1] // GROUPS
    place = lane_index(own.shape) % part
    edge = lane_roll(edge, -(index % 2) * (part // 2))
    return jnp.where(place >= part - SWEEPS if is_left else place < SWEEPS, edge, own)


def row_mirrored(value, start):
    part = value.shape[-1] // GROUPS
    group = group_index(value.shape, start)
    return jnp.where(group % 2 == 0, lane_roll(value, -part), lane_roll(value, part))


def total(terms):
    terms = list(terms)
    while len(terms) > 1:
        terms = [
            terms[i] + terms[i + 1] if i + 1 < len(terms) else terms[i]
            for i in range(0, len(terms), 2)
        ]
    return terms[0]


def around(planes, level, row, start=None):
    levels, rows = len(planes), len(planes[level])
    here = planes[level][row]
    terms = [lane_roll(here, 1), lane_roll(here, -1)]
    if row > 0:
        terms.append(planes[level][row - 1])
    if row < rows - 1:
        terms.append(planes[level][row + 1])
    elif start is not None:
        terms.append(row_mirrored(here, start))
    if level > 0:
        terms.append(planes[level - 1][row])
    if level < levels - 1:
        terms.append(planes[level + 1][row])
    elif start is not None:
        terms.append(lane_roll(here, here.shape[-1] // 2))
    return total(terms)


def sweep(source, target, keep_at, square_at, start=None):
    levels, rows = source.shape[0], source.shape[1]
    planes = [[source[level, row] for row in range(rows)] for level in range(levels)]
    for level in range(levels):
        for row in range(rows):
            target[level, row] = keep_at(level, row) * planes[level][row] + square_at(
                level, row
            ) * around(planes, level, row, start)


def anchor_kernel(out_ref):
    out_ref[...] = jnp.zeros_like(out_ref)


def weigh_kernel(
    owner_ref,
    gathered_ref,
    pert_ref,
    coeff_ref,
    anchor_ref,
    field_ref,
    left_ref,
    right_ref,
    coeff_left_ref,
    coeff_right_ref,
    to_right_ref,
    to_left_ref,
    grad_ref,
):
    members, terms, levels, rows, lanes = pert_ref.shape
    slab_rows = gathered_ref.shape[2]
    strip_levels, strip_rows = left_ref.shape[:2]
    for slab in range(rows // slab_rows):
        owner = owner_ref[slab]
        for term in range(terms):
            for inner in range(slab_rows):
                row = slab * slab_rows + inner
                grad_ref[pl.ds(term * levels * rows + row, levels, stride=rows), :] = gathered_ref[
                    owner, term, inner
                ]

    def weigh_level(level, carry):
        base = level * rows
        coeff = coeff_ref[level]
        gradients = [
            coeff * grad_ref[pl.ds(pl.multiple_of(term * levels * rows + base, rows), rows), :]
            for term in range(terms)
        ]
        for member in range(members):
            field_ref[pl.ds(base * members + member, rows, stride=members), :] = total(
                pert_ref[member, term, level].astype(jnp.float32) * gradients[term]
                for term in range(terms)
            )
        return carry

    lax.fori_loop(0, levels, weigh_level, 0)

    pairs = strip_levels * strip_rows // 2
    fields, coeffs = [], []
    for level in range(strip_levels):
        for row in range(strip_rows):
            index = level * strip_rows + row
            cells = mirrors(level, row, levels, rows)
            field = own_strips(
                [field_ref[pl.ds((l * rows + r) * members, members), :] for l, r in cells]
            )
            coeff = own_strips([spread(coeff_ref[l, pl.ds(r, 1), :]) for l, r in cells])
            left_ref[level, row], right_ref[level, row] = field
            coeff_left_ref[pl.ds(index, 1), :] = coeff[0][0:1]
            coeff_right_ref[pl.ds(index, 1), :] = coeff[1][0:1]
            fields.append(field[0])
            coeffs.append(coeff[0])
    for pair in range(pairs):
        edges = packed_edges(fields[2 * pair], fields[2 * pair + 1])
        coeff_edges = packed_edges(coeffs[2 * pair], coeffs[2 * pair + 1])
        for ref, edge, coeff_edge in zip((to_right_ref, to_left_ref), edges, coeff_edges):
            ref[pl.ds(pair * members, members), :] = edge
            ref[pl.ds(pairs * members + pair, 1), :] = coeff_edge[0:1]


def interior_kernel(field_ref, coeff_ref, out_ref, other_ref, keep_ref, square_ref, inverse_ref):
    levels, rows, members, lanes = field_ref.shape
    row_index = lax.broadcasted_iota(jnp.int32, (rows, lanes), 0)
    for level in range(levels):
        here = coeff_ref[level]
        terms = [
            lane_roll(here, 1),
            lane_roll(here, -1),
            jnp.where(row_index > 0, pltpu.roll(here, 1, 0), 0.0),
            jnp.where(row_index < rows - 1, pltpu.roll(here, rows - 1, 0), 0.0),
        ]
        if level > 0:
            terms.append(coeff_ref[level - 1])
        if level < levels - 1:
            terms.append(coeff_ref[level + 1])
        keep_ref[level] = 1.0 - here * total(terms)
        square_ref[level] = here * here
        inverse_ref[level] = 1.0 / here

    def keep_at(level, row):
        return keep_ref[level, pl.ds(row, 1), :]

    def square_at(level, row):
        return square_ref[level, pl.ds(row, 1), :]

    sweep(field_ref, other_ref, keep_at, square_at)
    sweep(other_ref, out_ref, keep_at, square_at)

    def pair(index, carry):
        sweep(out_ref, other_ref, keep_at, square_at)
        sweep(other_ref, out_ref, keep_at, square_at)
        return carry

    lax.fori_loop(0, SWEEPS // 2 - 1, pair, 0)
    for level in range(levels):
        for row in range(rows):
            out_ref[level, row] = out_ref[level, row] * inverse_ref[level, pl.ds(row, 1), :]


def swept_ends(
    strip_ref, coeff_ref, edge_ref, levels, rows, is_left, put, first_ref, second_ref, keep_ref, square_ref
):
    strip_levels, strip_rows, members, lanes = strip_ref.shape
    part = lanes // GROUPS
    start = SWEEPS if is_left else part - SWEEPS
    pairs = strip_levels * strip_rows // 2
    coeffs = []
    for level in range(strip_levels):
        plane = []
        for row in range(strip_rows):
            index = level * strip_rows + row
            edge = edge_ref[pl.ds(index // 2 * members, members), :]
            coeff_edge = spread(edge_ref[pl.ds(pairs * members + index // 2, 1), :])
            first_ref[level, row] = joined_strip(strip_ref[level, row], edge, index, is_left)
            plane.append(
                joined_strip(spread(coeff_ref[pl.ds(index, 1), :]), coeff_edge, index, is_left)
            )
        coeffs.append(plane)
    for level in range(strip_levels):
        for row in range(strip_rows):
            here = coeffs[level][row]
            keep_ref[level, row] = 1.0 - here * around(coeffs, level, row, start)
            square_ref[level, row] = here * here

    def keep_at(level, row):
        return keep_ref[level, row]

    def square_at(level, row):
        return square_ref[level, row]

    def pair(index, carry):
        sweep(first_ref, second_ref, keep_at, square_at, start)
        sweep(second_ref, first_ref, keep_at, square_at, start)
        return carry

    lax.fori_loop(0, SWEEPS // 2, pair, 0)
    for level in range(strip_levels):
        for row in range(strip_rows):
            coeff = spread(coeff_ref[pl.ds(level * strip_rows + row, 1), :])
            final = first_ref[level, row] / jnp.where(coeff > 0.0, coeff, 1.0)
            for g, (l, r) in enumerate(mirrors(level, row, levels, rows)):
                put(l, r, lane_roll(final, -part * g))


def left_kernel(interior_ref, strip_ref, coeff_ref, edge_ref, out_ref, *scratch):
    levels, rows, members, lanes = interior_ref.shape
    lane = lane_index((members, lanes))

    def put(level, row, end):
        out_ref[level, row] = jnp.where(lane < SWEEPS, end, interior_ref[level, row])

    swept_ends(strip_ref, coeff_ref, edge_ref, levels, rows, True, put, *scratch)


def finish_kernel(
    owner_ref,
    pert_ref,
    partial_ref,
    strip_ref,
    coeff_ref,
    edge_ref,
    out_ref,
    local_ref,
    sum_ref,
    *scratch,
):
    members, terms, levels, rows, lanes = pert_ref.shape
    slab_rows = out_ref.shape[2]
    lane = lane_index((members, lanes))

    def put(level, row, end):
        local_ref[pl.ds((level * rows + row) * members, members), :] = jnp.where(
            lane >= lanes - SWEEPS, end, partial_ref[level, row]
        )

    swept_ends(strip_ref, coeff_ref, edge_ref, levels, rows, False, put, *scratch)

    def add_level(level, carry):
        base = level * rows
        fields = [
            local_ref[pl.ds(base * members + member, rows, stride=members), :]
            for member in range(members)
        ]
        for term in range(terms):
            start = pl.multiple_of(term * levels * rows + base, rows)
            sum_ref[pl.ds(start, rows), :] = total(
                pert_ref[member, term, level].astype(jnp.float32) * fields[member]
                for member in range(members)
            )
        return carry

    lax.fori_loop(0, levels, add_level, 0)
    for slab in range(rows // slab_rows):
        owner = owner_ref[slab]
        for term in range(terms):
            for inner in range(slab_rows):
                row = slab * slab_rows + inner
                out_ref[owner, term, inner] = sum_ref[
                    pl.ds(term * levels * rows + row, levels, stride=rows), :
                ]


def local_call(kernel, name, outs, scratch, operands, places, work):
    def shape_of(out):
        return out if isinstance(out, jax.ShapeDtypeStruct) else jax.ShapeDtypeStruct(out, jnp.float32)

    shapes = tuple(shape_of(out) for out in outs)
    specs = tuple(whole() for _ in outs)
    moved = sum(math.prod(x.shape) * x.dtype.itemsize for x in tuple(operands) + shapes)
    single = len(outs) == 1
    return pl.pallas_call(
        kernel,
        out_shape=shapes[0] if single else shapes,
        in_specs=[whole(place) for place in places],
        out_specs=specs[0] if single else specs,
        scratch_shapes=[
            pltpu.VMEM(item, jnp.float32) if isinstance(item, tuple) else item for item in scratch
        ],
        compiler_params=pltpu.CompilerParams(vmem_limit_bytes=VMEM_LIMIT),
        cost_estimate=pl.CostEstimate(flops=work, bytes_accessed=moved, transcendentals=0),
        name=name,
    )(*operands)


def body(perturbations, gradient_store, diffusivity, slab_owner):
    members, slots, variables, levels, rows, lanes = perturbations.shape
    terms = slots * variables
    n_member = lax.axis_size("member")
    n_tile = lax.axis_size("tile")
    slab_rows = gradient_store.shape[3]
    cells = levels * rows * lanes
    strip_levels, strip_rows = levels // 2, rows // 2
    strips = strip_levels * strip_rows
    wide_strip = (strip_levels, strip_rows, members, lanes)
    coeff_wide_strip = (strip_levels, strip_rows, 8, lanes)
    strip_scratch = [wide_strip, wide_strip, coeff_wide_strip, coeff_wide_strip]
    coeff_strip = (strips, lanes)
    wide_field = (levels, rows, members, lanes)
    flat_field = (levels * rows * members, lanes)
    field_coeff = (levels, rows, lanes)
    edge_shape = (strips // 2 * (members + 1), lanes)
    grad_shape = (terms * levels * rows, lanes)
    vmem, smem = pltpu.VMEM, pltpu.SMEM

    pert = perturbations.reshape(members, terms, levels, rows, lanes)
    slab = gradient_store.reshape(terms, levels, slab_rows, lanes).swapaxes(1, 2)
    anchor = local_call(anchor_kernel, "anchor", [(8, lanes)], [], (), (), ANCHOR_WORK)
    gathered = lax.all_gather(slab, "member", axis=0, tiled=False)

    field, left, right, coeff_left, coeff_right, to_right, to_left = local_call(
        weigh_kernel,
        "weigh",
        [flat_field, wide_strip, wide_strip, coeff_strip, coeff_strip, edge_shape, edge_shape],
        [grad_shape],
        (slab_owner, gathered, pert, diffusivity, anchor),
        (smem, vmem, vmem, vmem, vmem),
        2 * terms * members * cells,
    )
    up = [(i, i + 1) for i in range(n_tile - 1)]
    down = [(i + 1, i) for i in range(n_tile - 1)]
    from_left = lax.ppermute(to_right, "tile", up)
    from_right = lax.ppermute(to_left, "tile", down)

    interior = local_call(
        interior_kernel,
        "interior",
        [wide_field],
        [wide_field, field_coeff, field_coeff, field_coeff],
        (field.reshape(wide_field), diffusivity),
        (vmem, vmem),
        8 * SWEEPS * members * cells,
    )
    partial = local_call(
        left_kernel,
        "left_strips",
        [wide_field],
        strip_scratch,
        (interior, left, coeff_left, from_left),
        (vmem,) * 4,
        2 * SWEEPS * members * cells,
    )
    sums = local_call(
        finish_kernel,
        "finish",
        [(n_member, terms, slab_rows, levels, lanes)],
        [flat_field, grad_shape] + strip_scratch,
        (slab_owner, pert, partial, right, coeff_right, from_right),
        (smem,) + (vmem,) * 5,
        2 * terms * members * cells,
    )
    received = lax.all_to_all(sums, "member", 0, 0, tiled=True)
    norm_factor = 1.0 / (members * n_member - 1)
    owned = jnp.sum(received, axis=0) * norm_factor
    return owned.swapaxes(1, 2).reshape(slots, variables, levels, slab_rows, lanes)


def solution(mesh):
    in_specs = (
        P("member", None, None, None, None, "tile"),
        P(None, None, None, "member", "tile"),
        P(None, None, "tile"),
        P(),
    )
    out_specs = P(None, None, None, "member", "tile")
    return jax.shard_map(body, mesh=mesh, in_specs=in_specs, out_specs=out_specs, check_vma=False)
```

```python
import math

import jax
import jax.numpy as jnp
from jax import lax
from jax.experimental import pallas as pl
from jax.experimental.pallas import tpu as pltpu
from jax.sharding import PartitionSpec as P

SWEEPS = 10
GROUPS = 4
ANCHOR_WORK = 10**10
VMEM_LIMIT = 16 * 1024 * 1024


def lane_roll(value, shift):
    shift = shift % value.shape[-1]
    return value if shift == 0 else pltpu.roll(value, shift, 1)


def lane_index(shape):
    return lax.broadcasted_iota(jnp.int32, shape, 1)


def spread(row, rows=8):
    return jnp.broadcast_to(row, (rows, row.shape[-1]))


def whole(memory_space=pltpu.VMEM):
    return pl.BlockSpec(memory_space=memory_space)


def mirrors(level, row, levels, rows):
    return [
        (far_level, far_row)
        for far_level in (level, levels - 1 - level)
        for far_row in (row, rows - 1 - row)
    ]


def group_index(shape, start):
    part = shape[-1] // GROUPS
    return (lane_index(shape) + start) % shape[-1] // part


def own_strips(values):
    part = values[0].shape[-1] // GROUPS
    rolled = [lane_roll(value, part * g) for g, value in enumerate(values)]
    both = []
    for start in (SWEEPS, part - SWEEPS):
        group = group_index(values[0].shape, start)
        strip = rolled[0]
        for g in range(1, GROUPS):
            strip = jnp.where(group == g, rolled[g], strip)
        both.append(strip)
    return both


def packed_edges(first, second):
    part = first.shape[-1] // GROUPS
    place = lane_index(first.shape) % part
    moved = lane_roll(second, part // 2)
    to_right = jnp.where(place >= part // 2, first, moved)
    to_left = jnp.where(place < part // 2, first, moved)
    return to_right, to_left


def joined_strip(own, edge, index, is_left):
    part = own.shape[-1] // GROUPS
    place = lane_index(own.shape) % part
    edge = lane_roll(edge, -(index % 2) * (part // 2))
    return jnp.where(place >= part - SWEEPS if is_left else place < SWEEPS, edge, own)


def row_mirrored(value, start):
    part = value.shape[-1] // GROUPS
    group = group_index(value.shape, start)
    return jnp.where(group % 2 == 0, lane_roll(value, -part), lane_roll(value, part))


def total(terms):
    terms = list(terms)
    while len(terms) > 1:
        terms = [
            terms[i] + terms[i + 1] if i + 1 < len(terms) else terms[i]
            for i in range(0, len(terms), 2)
        ]
    return terms[0]


def around(planes, level, row, start=None):
    levels, rows = len(planes), len(planes[level])
    here = planes[level][row]
    terms = [lane_roll(here, 1), lane_roll(here, -1)]
    if row > 0:
        terms.append(planes[level][row - 1])
    if row < rows - 1:
        terms.append(planes[level][row + 1])
    elif start is not None:
        terms.append(row_mirrored(here, start))
    if level > 0:
        terms.append(planes[level - 1][row])
    if level < levels - 1:
        terms.append(planes[level + 1][row])
    elif start is not None:
        terms.append(lane_roll(here, here.shape[-1] // 2))
    return total(terms)


def sweep(source, target, keep_at, square_at, start=None):
    levels, rows = source.shape[0], source.shape[1]
    planes = [[source[level, row] for row in range(rows)] for level in range(levels)]
    for level in range(levels):
        for row in range(rows):
            target[level, row] = keep_at(level, row) * planes[level][row] + square_at(
                level, row
            ) * around(planes, level, row, start)


def anchor_kernel(out_ref):
    out_ref[...] = jnp.zeros_like(out_ref)


def weigh_kernel(
    owner_ref,
    gathered_ref,
    pert_ref,
    coeff_ref,
    anchor_ref,
    field_ref,
    left_ref,
    right_ref,
    coeff_left_ref,
    coeff_right_ref,
    to_right_ref,
    to_left_ref,
    grad_ref,
):
    members, terms, levels, rows, lanes = pert_ref.shape
    slab_rows = gathered_ref.shape[2]
    strip_levels, strip_rows = left_ref.shape[:2]
    for slab in range(rows // slab_rows):
        owner = owner_ref[slab]
        for term in range(terms):
            for inner in range(slab_rows):
                row = slab * slab_rows + inner
                grad_ref[pl.ds(term * levels * rows + row, levels, stride=rows), :] = gathered_ref[
                    owner, term, inner
                ]

    def weigh_level(level, carry):
        base = level * rows
        coeff = coeff_ref[level]
        gradients = [
            coeff * grad_ref[pl.ds(pl.multiple_of(term * levels * rows + base, rows), rows), :]
            for term in range(terms)
        ]
        for member in range(members):
            field_ref[pl.ds(base * members + member, rows, stride=members), :] = total(
                pert_ref[member, term, level].astype(jnp.float32) * gradients[term]
                for term in range(terms)
            )
        return carry

    lax.fori_loop(0, levels, weigh_level, 0)

    pairs = strip_levels * strip_rows // 2
    fields, coeffs = [], []
    for level in range(strip_levels):
        for row in range(strip_rows):
            index = level * strip_rows + row
            cells = mirrors(level, row, levels, rows)
            field = own_strips(
                [field_ref[pl.ds((l * rows + r) * members, members), :] for l, r in cells]
            )
            coeff = own_strips([spread(coeff_ref[l, pl.ds(r, 1), :]) for l, r in cells])
            left_ref[level, row], right_ref[level, row] = field
            coeff_left_ref[pl.ds(index, 1), :] = coeff[0][0:1]
            coeff_right_ref[pl.ds(index, 1), :] = coeff[1][0:1]
            fields.append(field[0])
            coeffs.append(coeff[0])
    for pair in range(pairs):
        edges = packed_edges(fields[2 * pair], fields[2 * pair + 1])
        coeff_edges = packed_edges(coeffs[2 * pair], coeffs[2 * pair + 1])
        for ref, edge, coeff_edge in zip((to_right_ref, to_left_ref), edges, coeff_edges):
            ref[pl.ds(pair * members, members), :] = edge
            ref[pl.ds(pairs * members + pair, 1), :] = coeff_edge[0:1]


def interior_kernel(
    field_ref, coeff_ref, pert_ref, out_ref, ends_ref, other_ref, keep_ref, square_ref, inverse_ref
):
    levels, rows, members, lanes = field_ref.shape
    terms = pert_ref.shape[1]
    width = lanes // levels
    slot = lane_index((rows, lanes)) // width

    def pack_ends(member):
        for term in range(terms):
            ends = None
            for index, level in enumerate(level_slots(levels)):
                value = pert_ref[member, term, level].astype(jnp.float32)
                moved = lane_roll(value, width * (index + 1))
                ends = moved if ends is None else jnp.where(slot == index, moved, ends)
            ends_ref[member, term] = ends

    row_index = lax.broadcasted_iota(jnp.int32, (rows, lanes), 0)
    for level in range(levels):
        here = coeff_ref[level]
        beside = [
            lane_roll(here, 1),
            lane_roll(here, -1),
            jnp.where(row_index > 0, pltpu.roll(here, 1, 0), 0.0),
            jnp.where(row_index < rows - 1, pltpu.roll(here, rows - 1, 0), 0.0),
        ]
        if level > 0:
            beside.append(coeff_ref[level - 1])
        if level < levels - 1:
            beside.append(coeff_ref[level + 1])
        keep_ref[level] = 1.0 - here * total(beside)
        square_ref[level] = here * here
        inverse_ref[level] = 1.0 / here

    def keep_at(level, row):
        return keep_ref[level, pl.ds(row, 1), :]

    def square_at(level, row):
        return square_ref[level, pl.ds(row, 1), :]

    sweep(field_ref, other_ref, keep_at, square_at)
    sweep(other_ref, out_ref, keep_at, square_at)

    pairs = SWEEPS // 2 - 1
    share = members // pairs

    def pair(index, carry):
        sweep(out_ref, other_ref, keep_at, square_at)
        sweep(other_ref, out_ref, keep_at, square_at)
        for extra in range(share):
            pack_ends(index * share + extra)
        return carry

    lax.fori_loop(0, pairs, pair, 0)
    for member in range(pairs * share, members):
        pack_ends(member)
    for level in range(levels):
        for row in range(rows):
            out_ref[level, row] = out_ref[level, row] * inverse_ref[level, pl.ds(row, 1), :]


def swept_strips(strip_ref, coeff_ref, edge_ref, is_left, keep_ref, square_ref):
    strip_levels, strip_rows, members, lanes = strip_ref.shape
    part = lanes // GROUPS
    start = SWEEPS if is_left else part - SWEEPS
    pairs = strip_levels * strip_rows // 2
    planes, coeffs = [], []
    for level in range(strip_levels):
        plane, coeff_plane = [], []
        for row in range(strip_rows):
            index = level * strip_rows + row
            edge = edge_ref[pl.ds(index // 2 * members, members), :]
            coeff_edge = spread(edge_ref[pl.ds(pairs * members + index // 2, 1), :])
            plane.append(joined_strip(strip_ref[level, row], edge, index, is_left))
            coeff_plane.append(
                joined_strip(spread(coeff_ref[pl.ds(index, 1), :]), coeff_edge, index, is_left)
            )
        planes.append(plane)
        coeffs.append(coeff_plane)
    for level in range(strip_levels):
        for row in range(strip_rows):
            here = coeffs[level][row]
            keep_ref[level, row] = 1.0 - here * around(coeffs, level, row, start)
            square_ref[level, row] = here * here
    for _ in range(SWEEPS):
        planes = [
            [
                keep_ref[level, row] * planes[level][row]
                + square_ref[level, row] * around(planes, level, row, start)
                for row in range(strip_rows)
            ]
            for level in range(strip_levels)
        ]
    for level in range(strip_levels):
        for row in range(strip_rows):
            coeff = spread(coeff_ref[pl.ds(level * strip_rows + row, 1), :])
            planes[level][row] = planes[level][row] / jnp.where(coeff > 0.0, coeff, 1.0)
    return planes


def level_slots(levels):
    near = list(range(levels // 2))
    return near + [levels - 1 - level for level in near]


def partial_kernel(
    pert_ref, interior_ref, strip_ref, coeff_ref, edge_ref, out_ref, local_ref, keep_ref, square_ref
):
    members, terms, levels, rows, lanes = pert_ref.shape
    part = lanes // GROUPS
    planes = swept_strips(strip_ref, coeff_ref, edge_ref, True, keep_ref, square_ref)
    lane = lane_index((members, lanes))
    for level, plane in enumerate(planes):
        for row, final in enumerate(plane):
            for g, (l, r) in enumerate(mirrors(level, row, levels, rows)):
                local_ref[pl.ds((l * rows + r) * members, members), :] = jnp.where(
                    lane < SWEEPS, lane_roll(final, -part * g), interior_ref[l, r]
                )

    def add_level(level, carry):
        base = level * rows
        fields = [
            local_ref[pl.ds(base * members + member, rows, stride=members), :]
            for member in range(members)
        ]
        for term in range(terms):
            start = pl.multiple_of(term * levels * rows + base, rows)
            out_ref[pl.ds(start, rows), :] = total(
                pert_ref[member, term, level].astype(jnp.float32) * fields[member]
                for member in range(members)
            )
        return carry

    lax.fori_loop(0, levels, add_level, 0)


def finish_kernel(
    owner_ref,
    ends_ref,
    partial_ref,
    strip_ref,
    coeff_ref,
    edge_ref,
    out_ref,
    local_ref,
    sum_ref,
    keep_ref,
    square_ref,
):
    members, terms, rows, lanes = ends_ref.shape
    slab_rows, levels = out_ref.shape[2], out_ref.shape[3]
    part, half, width = lanes // GROUPS, lanes // 2, lanes // levels
    planes = swept_strips(strip_ref, coeff_ref, edge_ref, False, keep_ref, square_ref)
    strip_levels, strip_rows = len(planes), len(planes[0])
    slot = lane_index((members, lanes)) % half // width
    for row in range(strip_rows):
        for mirror in range(2):
            ends = None
            for level in range(strip_levels):
                moved = lane_roll(planes[level][row], width * (level + 1) - part * mirror)
                ends = moved if ends is None else jnp.where(slot == level, moved, ends)
            target = rows - 1 - row if mirror else row
            local_ref[pl.ds(target, members, stride=rows), :] = ends
    fields = [local_ref[pl.ds(member * rows, rows), :] for member in range(members)]
    lane = lane_index((rows, lanes))
    for term in range(terms):
        added = total(ends_ref[member, term] * fields[member] for member in range(members))
        for index, level in enumerate(level_slots(levels)):
            place = pl.ds((term * levels + level) * rows, rows)
            sum_ref[place, :] = jnp.where(
                lane >= lanes - SWEEPS, lane_roll(added, -width * (index + 1)), partial_ref[place, :]
            )
    for slab in range(rows // slab_rows):
        owner = owner_ref[slab]
        for term in range(terms):
            for inner in range(slab_rows):
                row = slab * slab_rows + inner
                out_ref[owner, term, inner] = sum_ref[
                    pl.ds(term * levels * rows + row, levels, stride=rows), :
                ]


def local_call(kernel, name, outs, scratch, operands, places, work):
    def shape_of(out):
        return out if isinstance(out, jax.ShapeDtypeStruct) else jax.ShapeDtypeStruct(out, jnp.float32)

    shapes = tuple(shape_of(out) for out in outs)
    specs = tuple(whole() for _ in outs)
    moved = sum(math.prod(x.shape) * x.dtype.itemsize for x in tuple(operands) + shapes)
    single = len(outs) == 1
    return pl.pallas_call(
        kernel,
        out_shape=shapes[0] if single else shapes,
        in_specs=[whole(place) for place in places],
        out_specs=specs[0] if single else specs,
        scratch_shapes=[
            pltpu.VMEM(item, jnp.float32) if isinstance(item, tuple) else item for item in scratch
        ],
        compiler_params=pltpu.CompilerParams(vmem_limit_bytes=VMEM_LIMIT),
        cost_estimate=pl.CostEstimate(flops=work, bytes_accessed=moved, transcendentals=0),
        name=name,
    )(*operands)


def body(perturbations, gradient_store, diffusivity, slab_owner):
    members, slots, variables, levels, rows, lanes = perturbations.shape
    terms = slots * variables
    n_member = lax.axis_size("member")
    n_tile = lax.axis_size("tile")
    slab_rows = gradient_store.shape[3]
    cells = levels * rows * lanes
    strip_levels, strip_rows = levels // 2, rows // 2
    strips = strip_levels * strip_rows
    wide_strip = (strip_levels, strip_rows, members, lanes)
    coeff_wide_strip = (strip_levels, strip_rows, 8, lanes)
    strip_scratch = [coeff_wide_strip, coeff_wide_strip]
    coeff_strip = (strips, lanes)
    wide_field = (levels, rows, members, lanes)
    flat_field = (levels * rows * members, lanes)
    field_coeff = (levels, rows, lanes)
    edge_shape = (strips // 2 * (members + 1), lanes)
    grad_shape = (terms * levels * rows, lanes)
    vmem, smem = pltpu.VMEM, pltpu.SMEM

    pert = perturbations.reshape(members, terms, levels, rows, lanes)
    slab = gradient_store.reshape(terms, levels, slab_rows, lanes).swapaxes(1, 2)
    anchor = local_call(anchor_kernel, "anchor", [(8, lanes)], [], (), (), ANCHOR_WORK)
    gathered = lax.all_gather(slab, "member", axis=0, tiled=False)

    field, left, right, coeff_left, coeff_right, to_right, to_left = local_call(
        weigh_kernel,
        "weigh",
        [flat_field, wide_strip, wide_strip, coeff_strip, coeff_strip, edge_shape, edge_shape],
        [grad_shape],
        (slab_owner, gathered, pert, diffusivity, anchor),
        (smem, vmem, vmem, vmem, vmem),
        2 * terms * members * cells,
    )
    up = [(i, i + 1) for i in range(n_tile - 1)]
    down = [(i + 1, i) for i in range(n_tile - 1)]
    from_left = lax.ppermute(to_right, "tile", up)
    from_right = lax.ppermute(to_left, "tile", down)

    interior, ends = local_call(
        interior_kernel,
        "interior",
        [wide_field, (members, terms, rows, lanes)],
        [wide_field, field_coeff, field_coeff, field_coeff],
        (field.reshape(wide_field), diffusivity, pert),
        (vmem,) * 3,
        8 * SWEEPS * members * cells,
    )
    partial = local_call(
        partial_kernel,
        "partial",
        [grad_shape],
        [flat_field] + strip_scratch,
        (pert, interior, left, coeff_left, from_left),
        (vmem,) * 5,
        2 * SWEEPS * members * cells,
    )
    sums = local_call(
        finish_kernel,
        "finish",
        [(n_member, terms, slab_rows, levels, lanes)],
        [(members * rows, lanes), grad_shape] + strip_scratch,
        (slab_owner, ends, partial, right, coeff_right, from_right),
        (smem,) + (vmem,) * 5,
        2 * terms * members * cells,
    )
    received = lax.all_to_all(sums, "member", 0, 0, tiled=True)
    norm_factor = 1.0 / (members * n_member - 1)
    owned = jnp.sum(received, axis=0) * norm_factor
    return owned.swapaxes(1, 2).reshape(slots, variables, levels, slab_rows, lanes)


def solution(mesh):
    in_specs = (
        P("member", None, None, None, None, "tile"),
        P(None, None, None, "member", "tile"),
        P(None, None, "tile"),
        P(),
    )
    out_specs = P(None, None, None, "member", "tile")
    return jax.shard_map(body, mesh=mesh, in_specs=in_specs, out_specs=out_specs, check_vma=False)
```

```python
import math

import jax
import jax.numpy as jnp
from jax import lax
from jax.experimental import pallas as pl
from jax.experimental.pallas import tpu as pltpu
from jax.sharding import PartitionSpec as P

SWEEPS = 10
GROUPS = 4
ANCHOR_WORK = 10**10
VMEM_LIMIT = 16 * 1024 * 1024


def lane_roll(value, shift):
    shift = shift % value.shape[-1]
    return value if shift == 0 else pltpu.roll(value, shift, 1)


def lane_index(shape):
    return lax.broadcasted_iota(jnp.int32, shape, 1)


def spread(row, rows=8):
    return jnp.broadcast_to(row, (rows, row.shape[-1]))


def whole(memory_space=pltpu.VMEM):
    return pl.BlockSpec(memory_space=memory_space)


def mirrors(level, row, levels, rows):
    return [
        (far_level, far_row)
        for far_level in (level, levels - 1 - level)
        for far_row in (row, rows - 1 - row)
    ]


def group_index(shape, start):
    part = shape[-1] // GROUPS
    return (lane_index(shape) + start) % shape[-1] // part


def own_strips(values):
    part = values[0].shape[-1] // GROUPS
    rolled = [lane_roll(value, part * g) for g, value in enumerate(values)]
    both = []
    for start in (SWEEPS, part - SWEEPS):
        group = group_index(values[0].shape, start)
        strip = rolled[0]
        for g in range(1, GROUPS):
            strip = jnp.where(group == g, rolled[g], strip)
        both.append(strip)
    return both


def packed_edges(first, second):
    part = first.shape[-1] // GROUPS
    place = lane_index(first.shape) % part
    moved = lane_roll(second, part // 2)
    to_right = jnp.where(place >= part // 2, first, moved)
    to_left = jnp.where(place < part // 2, first, moved)
    return to_right, to_left


def joined_strip(own, edge, index, is_left):
    part = own.shape[-1] // GROUPS
    place = lane_index(own.shape) % part
    edge = lane_roll(edge, -(index % 2) * (part // 2))
    return jnp.where(place >= part - SWEEPS if is_left else place < SWEEPS, edge, own)


def row_mirrored(value, start):
    part = value.shape[-1] // GROUPS
    group = group_index(value.shape, start)
    return jnp.where(group % 2 == 0, lane_roll(value, -part), lane_roll(value, part))


def total(terms):
    terms = list(terms)
    while len(terms) > 1:
        terms = [
            terms[i] + terms[i + 1] if i + 1 < len(terms) else terms[i]
            for i in range(0, len(terms), 2)
        ]
    return terms[0]


def around(planes, level, row, start=None):
    levels, rows = len(planes), len(planes[level])
    here = planes[level][row]
    terms = [lane_roll(here, 1), lane_roll(here, -1)]
    if row > 0:
        terms.append(planes[level][row - 1])
    if row < rows - 1:
        terms.append(planes[level][row + 1])
    elif start is not None:
        terms.append(row_mirrored(here, start))
    if level > 0:
        terms.append(planes[level - 1][row])
    if level < levels - 1:
        terms.append(planes[level + 1][row])
    elif start is not None:
        terms.append(lane_roll(here, here.shape[-1] // 2))
    return total(terms)


def sweep(source, target, keep_at, square_at, start=None):
    levels, rows = source.shape[0], source.shape[1]
    planes = [[source[level, row] for row in range(rows)] for level in range(levels)]
    for level in range(levels):
        for row in range(rows):
            target[level, row] = keep_at(level, row) * planes[level][row] + square_at(
                level, row
            ) * around(planes, level, row, start)


def anchor_kernel(out_ref):
    out_ref[...] = jnp.zeros_like(out_ref)


def weigh_kernel(
    owner_ref,
    gathered_ref,
    pert_ref,
    coeff_ref,
    anchor_ref,
    field_ref,
    left_ref,
    right_ref,
    coeff_left_ref,
    coeff_right_ref,
    to_right_ref,
    to_left_ref,
    grad_ref,
):
    members, terms, levels, rows, lanes = pert_ref.shape
    slab_rows = gathered_ref.shape[2]
    strip_levels, strip_rows = left_ref.shape[:2]
    for slab in range(rows // slab_rows):
        owner = owner_ref[slab]
        for term in range(terms):
            for inner in range(slab_rows):
                row = slab * slab_rows + inner
                grad_ref[pl.ds(term * levels * rows + row, levels, stride=rows), :] = gathered_ref[
                    owner, term, inner
                ]

    for level in range(levels):
        base = level * rows
        coeff = coeff_ref[level]
        gradients = [
            coeff * grad_ref[pl.ds(term * levels * rows + base, rows), :] for term in range(terms)
        ]
        for member in range(members):
            field_ref[pl.ds(base * members + member, rows, stride=members), :] = total(
                pert_ref[member, term, level].astype(jnp.float32) * gradients[term]
                for term in range(terms)
            )

    pairs = strip_levels * strip_rows // 2
    fields, coeffs = [], []
    for level in range(strip_levels):
        for row in range(strip_rows):
            index = level * strip_rows + row
            cells = mirrors(level, row, levels, rows)
            field = own_strips(
                [field_ref[pl.ds((l * rows + r) * members, members), :] for l, r in cells]
            )
            coeff = own_strips([spread(coeff_ref[l, pl.ds(r, 1), :]) for l, r in cells])
            left_ref[level, row], right_ref[level, row] = field
            coeff_left_ref[pl.ds(index, 1), :] = coeff[0][0:1]
            coeff_right_ref[pl.ds(index, 1), :] = coeff[1][0:1]
            fields.append(field[0])
            coeffs.append(coeff[0])
    for pair in range(pairs):
        edges = packed_edges(fields[2 * pair], fields[2 * pair + 1])
        coeff_edges = packed_edges(coeffs[2 * pair], coeffs[2 * pair + 1])
        for ref, edge, coeff_edge in zip((to_right_ref, to_left_ref), edges, coeff_edges):
            ref[pl.ds(pair * members, members), :] = edge
            ref[pl.ds(pairs * members + pair, 1), :] = coeff_edge[0:1]


def interior_kernel(
    field_ref, coeff_ref, pert_ref, out_ref, ends_ref, other_ref, keep_ref, square_ref, inverse_ref
):
    levels, rows, members, lanes = field_ref.shape
    terms = pert_ref.shape[1]
    width = lanes // levels
    slot = lane_index((rows, lanes)) // width

    def pack_ends(member):
        for term in range(terms):
            ends = None
            for index, level in enumerate(level_slots(levels)):
                value = pert_ref[member, term, level].astype(jnp.float32)
                moved = lane_roll(value, width * (index + 1))
                ends = moved if ends is None else jnp.where(slot == index, moved, ends)
            ends_ref[member, term] = ends

    row_index = lax.broadcasted_iota(jnp.int32, (rows, lanes), 0)
    for level in range(levels):
        here = coeff_ref[level]
        beside = [
            lane_roll(here, 1),
            lane_roll(here, -1),
            jnp.where(row_index > 0, pltpu.roll(here, 1, 0), 0.0),
            jnp.where(row_index < rows - 1, pltpu.roll(here, rows - 1, 0), 0.0),
        ]
        if level > 0:
            beside.append(coeff_ref[level - 1])
        if level < levels - 1:
            beside.append(coeff_ref[level + 1])
        keep_ref[level] = 1.0 - here * total(beside)
        square_ref[level] = here * here
        inverse_ref[level] = 1.0 / here

    def keep_at(level, row):
        return keep_ref[level, pl.ds(row, 1), :]

    def square_at(level, row):
        return square_ref[level, pl.ds(row, 1), :]

    sweep(field_ref, other_ref, keep_at, square_at)
    sweep(other_ref, out_ref, keep_at, square_at)

    pairs = SWEEPS // 2 - 1
    share = members // pairs

    def pair(index, carry):
        sweep(out_ref, other_ref, keep_at, square_at)
        sweep(other_ref, out_ref, keep_at, square_at)
        for extra in range(share):
            pack_ends(index * share + extra)
        return carry

    lax.fori_loop(0, pairs, pair, 0)
    for member in range(pairs * share, members):
        pack_ends(member)
    for level in range(levels):
        for row in range(rows):
            out_ref[level, row] = out_ref[level, row] * inverse_ref[level, pl.ds(row, 1), :]


def swept_strips(strip_ref, coeff_ref, edge_ref, is_left, keep_ref, square_ref):
    strip_levels, strip_rows, members, lanes = strip_ref.shape
    part = lanes // GROUPS
    start = SWEEPS if is_left else part - SWEEPS
    pairs = strip_levels * strip_rows // 2
    planes, coeffs = [], []
    for level in range(strip_levels):
        plane, coeff_plane = [], []
        for row in range(strip_rows):
            index = level * strip_rows + row
            edge = edge_ref[pl.ds(index // 2 * members, members), :]
            coeff_edge = spread(edge_ref[pl.ds(pairs * members + index // 2, 1), :])
            plane.append(joined_strip(strip_ref[level, row], edge, index, is_left))
            coeff_plane.append(
                joined_strip(spread(coeff_ref[pl.ds(index, 1), :]), coeff_edge, index, is_left)
            )
        planes.append(plane)
        coeffs.append(coeff_plane)
    for level in range(strip_levels):
        for row in range(strip_rows):
            here = coeffs[level][row]
            keep_ref[level, row] = 1.0 - here * around(coeffs, level, row, start)
            square_ref[level, row] = here * here
    for _ in range(SWEEPS):
        planes = [
            [
                keep_ref[level, row] * planes[level][row]
                + square_ref[level, row] * around(planes, level, row, start)
                for row in range(strip_rows)
            ]
            for level in range(strip_levels)
        ]
    for level in range(strip_levels):
        for row in range(strip_rows):
            coeff = spread(coeff_ref[pl.ds(level * strip_rows + row, 1), :])
            planes[level][row] = planes[level][row] / jnp.where(coeff > 0.0, coeff, 1.0)
    return planes


def level_slots(levels):
    near = list(range(levels // 2))
    return near + [levels - 1 - level for level in near]


def partial_kernel(
    pert_ref, interior_ref, strip_ref, coeff_ref, edge_ref, out_ref, local_ref, keep_ref, square_ref
):
    members, terms, levels, rows, lanes = pert_ref.shape
    part = lanes // GROUPS
    planes = swept_strips(strip_ref, coeff_ref, edge_ref, True, keep_ref, square_ref)
    lane = lane_index((members, lanes))
    for level, plane in enumerate(planes):
        for row, final in enumerate(plane):
            for g, (l, r) in enumerate(mirrors(level, row, levels, rows)):
                local_ref[pl.ds((l * rows + r) * members, members), :] = jnp.where(
                    lane < SWEEPS, lane_roll(final, -part * g), interior_ref[l, r]
                )

    for level in range(levels):
        base = level * rows
        fields = [
            local_ref[pl.ds(base * members + member, rows, stride=members), :]
            for member in range(members)
        ]
        for term in range(terms):
            out_ref[pl.ds(term * levels * rows + base, rows), :] = total(
                pert_ref[member, term, level].astype(jnp.float32) * fields[member]
                for member in range(members)
            )


def finish_kernel(
    owner_ref,
    ends_ref,
    partial_ref,
    strip_ref,
    coeff_ref,
    edge_ref,
    out_ref,
    local_ref,
    sum_ref,
    keep_ref,
    square_ref,
):
    members, terms, rows, lanes = ends_ref.shape
    slab_rows, levels = out_ref.shape[2], out_ref.shape[3]
    part, half, width = lanes // GROUPS, lanes // 2, lanes // levels
    planes = swept_strips(strip_ref, coeff_ref, edge_ref, False, keep_ref, square_ref)
    strip_levels, strip_rows = len(planes), len(planes[0])
    slot = lane_index((members, lanes)) % half // width
    for row in range(strip_rows):
        for mirror in range(2):
            ends = None
            for level in range(strip_levels):
                moved = lane_roll(planes[level][row], width * (level + 1) - part * mirror)
                ends = moved if ends is None else jnp.where(slot == level, moved, ends)
            target = rows - 1 - row if mirror else row
            local_ref[pl.ds(target, members, stride=rows), :] = ends
    fields = [local_ref[pl.ds(member * rows, rows), :] for member in range(members)]
    lane = lane_index((rows, lanes))
    for term in range(terms):
        added = total(ends_ref[member, term] * fields[member] for member in range(members))
        for index, level in enumerate(level_slots(levels)):
            place = pl.ds((term * levels + level) * rows, rows)
            sum_ref[place, :] = jnp.where(
                lane >= lanes - SWEEPS, lane_roll(added, -width * (index + 1)), partial_ref[place, :]
            )
    for slab in range(rows // slab_rows):
        owner = owner_ref[slab]
        for term in range(terms):
            for inner in range(slab_rows):
                row = slab * slab_rows + inner
                out_ref[owner, term, inner] = sum_ref[
                    pl.ds(term * levels * rows + row, levels, stride=rows), :
                ]


def local_call(kernel, name, outs, scratch, operands, places, work):
    def shape_of(out):
        return out if isinstance(out, jax.ShapeDtypeStruct) else jax.ShapeDtypeStruct(out, jnp.float32)

    shapes = tuple(shape_of(out) for out in outs)
    specs = tuple(whole() for _ in outs)
    moved = sum(math.prod(x.shape) * x.dtype.itemsize for x in tuple(operands) + shapes)
    single = len(outs) == 1
    return pl.pallas_call(
        kernel,
        out_shape=shapes[0] if single else shapes,
        in_specs=[whole(place) for place in places],
        out_specs=specs[0] if single else specs,
        scratch_shapes=[
            pltpu.VMEM(item, jnp.float32) if isinstance(item, tuple) else item for item in scratch
        ],
        compiler_params=pltpu.CompilerParams(vmem_limit_bytes=VMEM_LIMIT),
        cost_estimate=pl.CostEstimate(flops=work, bytes_accessed=moved, transcendentals=0),
        name=name,
    )(*operands)


def body(perturbations, gradient_store, diffusivity, slab_owner):
    members, slots, variables, levels, rows, lanes = perturbations.shape
    terms = slots * variables
    n_member = lax.axis_size("member")
    n_tile = lax.axis_size("tile")
    slab_rows = gradient_store.shape[3]
    cells = levels * rows * lanes
    strip_levels, strip_rows = levels // 2, rows // 2
    strips = strip_levels * strip_rows
    wide_strip = (strip_levels, strip_rows, members, lanes)
    coeff_wide_strip = (strip_levels, strip_rows, 8, lanes)
    strip_scratch = [coeff_wide_strip, coeff_wide_strip]
    coeff_strip = (strips, lanes)
    wide_field = (levels, rows, members, lanes)
    flat_field = (levels * rows * members, lanes)
    field_coeff = (levels, rows, lanes)
    edge_shape = (strips // 2 * (members + 1), lanes)
    grad_shape = (terms * levels * rows, lanes)
    vmem, smem = pltpu.VMEM, pltpu.SMEM

    pert = perturbations.reshape(members, terms, levels, rows, lanes)
    slab = gradient_store.reshape(terms, levels, slab_rows, lanes).swapaxes(1, 2)
    anchor = local_call(anchor_kernel, "anchor", [(8, lanes)], [], (), (), ANCHOR_WORK)
    gathered = lax.all_gather(slab, "member", axis=0, tiled=False)

    field, left, right, coeff_left, coeff_right, to_right, to_left = local_call(
        weigh_kernel,
        "weigh",
        [flat_field, wide_strip, wide_strip, coeff_strip, coeff_strip, edge_shape, edge_shape],
        [grad_shape],
        (slab_owner, gathered, pert, diffusivity, anchor),
        (smem, vmem, vmem, vmem, vmem),
        2 * terms * members * cells,
    )
    up = [(i, i + 1) for i in range(n_tile - 1)]
    down = [(i + 1, i) for i in range(n_tile - 1)]
    from_left = lax.ppermute(to_right, "tile", up)
    from_right = lax.ppermute(to_left, "tile", down)

    interior, ends = local_call(
        interior_kernel,
        "interior",
        [wide_field, (members, terms, rows, lanes)],
        [wide_field, field_coeff, field_coeff, field_coeff],
        (field.reshape(wide_field), diffusivity, pert),
        (vmem,) * 3,
        8 * SWEEPS * members * cells,
    )
    partial = local_call(
        partial_kernel,
        "partial",
        [grad_shape],
        [flat_field] + strip_scratch,
        (pert, interior, left, coeff_left, from_left),
        (vmem,) * 5,
        2 * SWEEPS * members * cells,
    )
    sums = local_call(
        finish_kernel,
        "finish",
        [(n_member, terms, slab_rows, levels, lanes)],
        [(members * rows, lanes), grad_shape] + strip_scratch,
        (slab_owner, ends, partial, right, coeff_right, from_right),
        (smem,) + (vmem,) * 5,
        2 * terms * members * cells,
    )
    received = lax.all_to_all(sums, "member", 0, 0, tiled=True)
    norm_factor = 1.0 / (members * n_member - 1)
    owned = jnp.sum(received, axis=0) * norm_factor
    return owned.swapaxes(1, 2).reshape(slots, variables, levels, slab_rows, lanes)


def solution(mesh):
    in_specs = (
        P("member", None, None, None, None, "tile"),
        P(None, None, None, "member", "tile"),
        P(None, None, "tile"),
        P(),
    )
    out_specs = P(None, None, None, "member", "tile")
    return jax.shard_map(body, mesh=mesh, in_specs=in_specs, out_specs=out_specs, check_vma=False)
```

```python
import math

import jax
import jax.numpy as jnp
from jax import lax
from jax.experimental import pallas as pl
from jax.experimental.pallas import tpu as pltpu
from jax.sharding import PartitionSpec as P

SWEEPS = 10
GROUPS = 4
ANCHOR_WORK = 10**10
VMEM_LIMIT = 16 * 1024 * 1024


def lane_roll(value, shift):
    shift = shift % value.shape[-1]
    return value if shift == 0 else pltpu.roll(value, shift, 1)


def lane_index(shape):
    return lax.broadcasted_iota(jnp.int32, shape, 1)


def spread(row, rows=8):
    return jnp.broadcast_to(row, (rows, row.shape[-1]))


def whole(memory_space=pltpu.VMEM):
    return pl.BlockSpec(memory_space=memory_space)


def mirrors(level, row, levels, rows):
    return [
        (far_level, far_row)
        for far_level in (level, levels - 1 - level)
        for far_row in (row, rows - 1 - row)
    ]


def group_index(shape, start):
    part = shape[-1] // GROUPS
    return (lane_index(shape) + start) % shape[-1] // part


def own_strips(values):
    part = values[0].shape[-1] // GROUPS
    rolled = [lane_roll(value, part * g) for g, value in enumerate(values)]
    both = []
    for start in (SWEEPS, part - SWEEPS):
        group = group_index(values[0].shape, start)
        strip = rolled[0]
        for g in range(1, GROUPS):
            strip = jnp.where(group == g, rolled[g], strip)
        both.append(strip)
    return both


def packed_edges(first, second):
    part = first.shape[-1] // GROUPS
    place = lane_index(first.shape) % part
    moved = lane_roll(second, part // 2)
    to_right = jnp.where(place >= part // 2, first, moved)
    to_left = jnp.where(place < part // 2, first, moved)
    return to_right, to_left


def joined_strip(own, edge, index, halo):
    part = own.shape[-1] // GROUPS
    return jnp.where(halo, lane_roll(edge, -(index % 2) * (part // 2)), own)


def swap_sides(values, swapped):
    first, second = values
    return jnp.where(swapped, second, first), jnp.where(swapped, first, second)


def first_is_left():
    return lax.axis_index("tile") % 2 == 1


def total(terms):
    terms = list(terms)
    while len(terms) > 1:
        terms = [
            terms[i] + terms[i + 1] if i + 1 < len(terms) else terms[i]
            for i in range(0, len(terms), 2)
        ]
    return terms[0]


def around(planes, level, row, even_group=None):
    levels, rows = len(planes), len(planes[level])
    here = planes[level][row]
    terms = [lane_roll(here, 1), lane_roll(here, -1)]
    if row > 0:
        terms.append(planes[level][row - 1])
    if row < rows - 1:
        terms.append(planes[level][row + 1])
    elif even_group is not None:
        part = here.shape[-1] // GROUPS
        terms.append(jnp.where(even_group, lane_roll(here, -part), lane_roll(here, part)))
    if level > 0:
        terms.append(planes[level - 1][row])
    if level < levels - 1:
        terms.append(planes[level + 1][row])
    elif even_group is not None:
        terms.append(lane_roll(here, here.shape[-1] // 2))
    return total(terms)


def sweep(source, target, keep_at, square_at):
    levels, rows = source.shape[0], source.shape[1]
    planes = [[source[level, row] for row in range(rows)] for level in range(levels)]
    for level in range(levels):
        for row in range(rows):
            target[level, row] = keep_at(level, row) * planes[level][row] + square_at(
                level, row
            ) * around(planes, level, row)


def anchor_kernel(out_ref):
    out_ref[...] = jnp.zeros_like(out_ref)


def weigh_kernel(
    owner_ref,
    gathered_ref,
    pert_ref,
    coeff_ref,
    anchor_ref,
    field_ref,
    first_ref,
    second_ref,
    coeff_first_ref,
    coeff_second_ref,
    to_first_ref,
    to_second_ref,
    grad_ref,
):
    members, terms, levels, rows, lanes = pert_ref.shape
    slab_rows = gathered_ref.shape[2]
    strip_levels, strip_rows = first_ref.shape[:2]
    left_first = jnp.broadcast_to(first_is_left(), (8, lanes))
    for slab in range(rows // slab_rows):
        owner = owner_ref[slab]
        for term in range(terms):
            for inner in range(slab_rows):
                row = slab * slab_rows + inner
                grad_ref[pl.ds(term * levels * rows + row, levels, stride=rows), :] = gathered_ref[
                    owner, term, inner
                ]

    for level in range(levels):
        base = level * rows
        coeff = coeff_ref[level]
        gradients = [
            coeff * grad_ref[pl.ds(term * levels * rows + base, rows), :] for term in range(terms)
        ]
        for member in range(members):
            field_ref[pl.ds(base * members + member, rows, stride=members), :] = total(
                pert_ref[member, term, level].astype(jnp.float32) * gradients[term]
                for term in range(terms)
            )

    pairs = strip_levels * strip_rows // 2
    fields, coeffs = [], []
    for level in range(strip_levels):
        for row in range(strip_rows):
            index = level * strip_rows + row
            cells = mirrors(level, row, levels, rows)
            field = own_strips(
                [field_ref[pl.ds((l * rows + r) * members, members), :] for l, r in cells]
            )
            coeff = own_strips([spread(coeff_ref[l, pl.ds(r, 1), :]) for l, r in cells])
            fields.append(field[0])
            coeffs.append(coeff[0])
            field = swap_sides(field[::-1], left_first)
            coeff = swap_sides(coeff[::-1], left_first)
            first_ref[level, row], second_ref[level, row] = field
            coeff_first_ref[pl.ds(index, 1), :] = coeff[0][0:1]
            coeff_second_ref[pl.ds(index, 1), :] = coeff[1][0:1]
    for pair in range(pairs):
        edges = packed_edges(fields[2 * pair], fields[2 * pair + 1])
        coeff_edges = packed_edges(coeffs[2 * pair], coeffs[2 * pair + 1])
        edges = swap_sides(edges, left_first)
        coeff_edges = swap_sides(coeff_edges, left_first)
        for ref, edge, coeff_edge in zip((to_first_ref, to_second_ref), edges, coeff_edges):
            ref[pl.ds(pair * members, members), :] = edge
            ref[pl.ds(pairs * members + pair, 1), :] = coeff_edge[0:1]


def interior_kernel(
    field_ref, coeff_ref, pert_ref, out_ref, ends_ref, other_ref, keep_ref, square_ref, inverse_ref
):
    levels, rows, members, lanes = field_ref.shape
    terms = pert_ref.shape[1]
    width = lanes // levels
    shift = jnp.where(first_is_left(), 0, lanes - width)
    slot = (lane_index((rows, lanes)) + shift) % lanes // width

    def pack_ends(member):
        for term in range(terms):
            ends = None
            for index, level in enumerate(level_slots(levels)):
                value = pert_ref[member, term, level].astype(jnp.float32)
                moved = lane_roll(value, width * (index + 1))
                ends = moved if ends is None else jnp.where(slot == index, moved, ends)
            ends_ref[member, term] = ends

    row_index = lax.broadcasted_iota(jnp.int32, (rows, lanes), 0)
    for level in range(levels):
        here = coeff_ref[level]
        beside = [
            lane_roll(here, 1),
            lane_roll(here, -1),
            jnp.where(row_index > 0, pltpu.roll(here, 1, 0), 0.0),
            jnp.where(row_index < rows - 1, pltpu.roll(here, rows - 1, 0), 0.0),
        ]
        if level > 0:
            beside.append(coeff_ref[level - 1])
        if level < levels - 1:
            beside.append(coeff_ref[level + 1])
        keep_ref[level] = 1.0 - here * total(beside)
        square_ref[level] = here * here
        inverse_ref[level] = 1.0 / here

    def keep_at(level, row):
        return keep_ref[level, pl.ds(row, 1), :]

    def square_at(level, row):
        return square_ref[level, pl.ds(row, 1), :]

    sweep(field_ref, other_ref, keep_at, square_at)
    sweep(other_ref, out_ref, keep_at, square_at)

    pairs = SWEEPS // 2 - 1
    share = members // pairs

    def pair(index, carry):
        sweep(out_ref, other_ref, keep_at, square_at)
        sweep(other_ref, out_ref, keep_at, square_at)
        for extra in range(share):
            pack_ends(index * share + extra)
        return carry

    lax.fori_loop(0, pairs, pair, 0)
    for member in range(pairs * share, members):
        pack_ends(member)
    for level in range(levels):
        for row in range(rows):
            out_ref[level, row] = out_ref[level, row] * inverse_ref[level, pl.ds(row, 1), :]


def swept_strips(strip_ref, coeff_ref, edge_ref, is_left, keep_ref, square_ref):
    strip_levels, strip_rows, members, lanes = strip_ref.shape
    part = lanes // GROUPS
    pairs = strip_levels * strip_rows // 2
    lane = lane_index((members, lanes))
    even_group = (lane + jnp.where(is_left, SWEEPS, part - SWEEPS)) // part % 2 == 0
    halo = (lane + jnp.where(is_left, SWEEPS, 0)) % part < SWEEPS
    planes, coeffs = [], []
    for level in range(strip_levels):
        plane, coeff_plane = [], []
        for row in range(strip_rows):
            index = level * strip_rows + row
            edge = edge_ref[pl.ds(index // 2 * members, members), :]
            coeff_edge = spread(edge_ref[pl.ds(pairs * members + index // 2, 1), :], members)
            plane.append(joined_strip(strip_ref[level, row], edge, index, halo))
            coeff_own = spread(coeff_ref[pl.ds(index, 1), :], members)
            coeff_plane.append(joined_strip(coeff_own, coeff_edge, index, halo))
        planes.append(plane)
        coeffs.append(coeff_plane)
    for level in range(strip_levels):
        for row in range(strip_rows):
            here = coeffs[level][row]
            keep_ref[level, row] = 1.0 - here * around(coeffs, level, row, even_group)
            square_ref[level, row] = here * here
    for _ in range(SWEEPS):
        planes = [
            [
                keep_ref[level, row] * planes[level][row]
                + square_ref[level, row] * around(planes, level, row, even_group)
                for row in range(strip_rows)
            ]
            for level in range(strip_levels)
        ]
    for level in range(strip_levels):
        for row in range(strip_rows):
            coeff = spread(coeff_ref[pl.ds(level * strip_rows + row, 1), :], members)
            planes[level][row] = planes[level][row] / jnp.where(coeff > 0.0, coeff, 1.0)
    return planes


def outer_lanes(shape, is_left):
    return (lane_index(shape) + jnp.where(is_left, 0, SWEEPS)) % shape[-1] < SWEEPS


def level_slots(levels):
    near = list(range(levels // 2))
    return near + [levels - 1 - level for level in near]


def partial_kernel(
    pert_ref, interior_ref, strip_ref, coeff_ref, edge_ref, out_ref, local_ref, keep_ref, square_ref
):
    members, terms, levels, rows, lanes = pert_ref.shape
    part = lanes // GROUPS
    is_left = first_is_left()
    planes = swept_strips(strip_ref, coeff_ref, edge_ref, is_left, keep_ref, square_ref)
    outer = outer_lanes((members, lanes), is_left)
    for level, plane in enumerate(planes):
        for row, final in enumerate(plane):
            for g, (l, r) in enumerate(mirrors(level, row, levels, rows)):
                local_ref[pl.ds((l * rows + r) * members, members), :] = jnp.where(
                    outer, lane_roll(final, -part * g), interior_ref[l, r]
                )

    for level in range(levels):
        base = level * rows
        fields = [
            local_ref[pl.ds(base * members + member, rows, stride=members), :]
            for member in range(members)
        ]
        for term in range(terms):
            out_ref[pl.ds(term * levels * rows + base, rows), :] = total(
                pert_ref[member, term, level].astype(jnp.float32) * fields[member]
                for member in range(members)
            )


def finish_kernel(
    owner_ref,
    ends_ref,
    partial_ref,
    strip_ref,
    coeff_ref,
    edge_ref,
    out_ref,
    local_ref,
    sum_ref,
    keep_ref,
    square_ref,
):
    members, terms, rows, lanes = ends_ref.shape
    slab_rows, levels = out_ref.shape[2], out_ref.shape[3]
    part, half, width = lanes // GROUPS, lanes // 2, lanes // levels
    is_left = jnp.logical_not(first_is_left())
    planes = swept_strips(strip_ref, coeff_ref, edge_ref, is_left, keep_ref, square_ref)
    strip_levels, strip_rows = len(planes), len(planes[0])
    shift = jnp.where(is_left, half - width, 0)
    slot = (lane_index((members, lanes)) + shift) % half // width
    for row in range(strip_rows):
        for mirror in range(2):
            ends = None
            for level in range(strip_levels):
                moved = lane_roll(planes[level][row], width * (level + 1) - part * mirror)
                ends = moved if ends is None else jnp.where(slot == level, moved, ends)
            target = rows - 1 - row if mirror else row
            local_ref[pl.ds(target, members, stride=rows), :] = ends
    fields = [local_ref[pl.ds(member * rows, rows), :] for member in range(members)]
    outer = outer_lanes((rows, lanes), is_left)
    for term in range(terms):
        added = total(ends_ref[member, term] * fields[member] for member in range(members))
        for index, level in enumerate(level_slots(levels)):
            place = pl.ds((term * levels + level) * rows, rows)
            sum_ref[place, :] = jnp.where(
                outer, lane_roll(added, -width * (index + 1)), partial_ref[place, :]
            )
    for slab in range(rows // slab_rows):
        owner = owner_ref[slab]
        for term in range(terms):
            for inner in range(slab_rows):
                row = slab * slab_rows + inner
                out_ref[owner, term, inner] = sum_ref[
                    pl.ds(term * levels * rows + row, levels, stride=rows), :
                ]


def local_call(kernel, name, outs, scratch, operands, places, work):
    def shape_of(out):
        return out if isinstance(out, jax.ShapeDtypeStruct) else jax.ShapeDtypeStruct(out, jnp.float32)

    shapes = tuple(shape_of(out) for out in outs)
    specs = tuple(whole() for _ in outs)
    moved = sum(math.prod(x.shape) * x.dtype.itemsize for x in tuple(operands) + shapes)
    single = len(outs) == 1
    return pl.pallas_call(
        kernel,
        out_shape=shapes[0] if single else shapes,
        in_specs=[whole(place) for place in places],
        out_specs=specs[0] if single else specs,
        scratch_shapes=[
            pltpu.VMEM(item, jnp.float32) if isinstance(item, tuple) else item for item in scratch
        ],
        compiler_params=pltpu.CompilerParams(vmem_limit_bytes=VMEM_LIMIT),
        cost_estimate=pl.CostEstimate(flops=work, bytes_accessed=moved, transcendentals=0),
        name=name,
    )(*operands)


def body(perturbations, gradient_store, diffusivity, slab_owner):
    members, slots, variables, levels, rows, lanes = perturbations.shape
    terms = slots * variables
    n_member = lax.axis_size("member")
    n_tile = lax.axis_size("tile")
    slab_rows = gradient_store.shape[3]
    cells = levels * rows * lanes
    strip_levels, strip_rows = levels // 2, rows // 2
    strips = strip_levels * strip_rows
    wide_strip = (strip_levels, strip_rows, members, lanes)
    strip_scratch = [wide_strip, wide_strip]
    coeff_strip = (strips, lanes)
    wide_field = (levels, rows, members, lanes)
    flat_field = (levels * rows * members, lanes)
    field_coeff = (levels, rows, lanes)
    edge_shape = (strips // 2 * (members + 1), lanes)
    grad_shape = (terms * levels * rows, lanes)
    vmem, smem = pltpu.VMEM, pltpu.SMEM

    pert = perturbations.reshape(members, terms, levels, rows, lanes)
    slab = gradient_store.reshape(terms, levels, slab_rows, lanes).swapaxes(1, 2)
    anchor = local_call(anchor_kernel, "anchor", [(8, lanes)], [], (), (), ANCHOR_WORK)
    gathered = lax.all_gather(slab, "member", axis=0, tiled=False)

    field, first, second, coeff_first, coeff_second, to_first, to_second = local_call(
        weigh_kernel,
        "weigh",
        [flat_field, wide_strip, wide_strip, coeff_strip, coeff_strip, edge_shape, edge_shape],
        [grad_shape],
        (slab_owner, gathered, pert, diffusivity, anchor),
        (smem, vmem, vmem, vmem, vmem),
        2 * terms * members * cells,
    )
    from_first, from_second = (
        lax.ppermute(
            edges,
            "tile",
            [pair for i in range(start, n_tile - 1, 2) for pair in ((i, i + 1), (i + 1, i))],
        )
        for start, edges in ((0, to_first), (1, to_second))
    )

    interior, ends = local_call(
        interior_kernel,
        "interior",
        [wide_field, (members, terms, rows, lanes)],
        [wide_field, field_coeff, field_coeff, field_coeff],
        (field.reshape(wide_field), diffusivity, pert),
        (vmem,) * 3,
        8 * SWEEPS * members * cells,
    )
    partial = local_call(
        partial_kernel,
        "partial",
        [grad_shape],
        [flat_field] + strip_scratch,
        (pert, interior, first, coeff_first, from_first),
        (vmem,) * 5,
        2 * SWEEPS * members * cells,
    )
    sums = local_call(
        finish_kernel,
        "finish",
        [(n_member, terms, slab_rows, levels, lanes)],
        [(members * rows, lanes), grad_shape] + strip_scratch,
        (slab_owner, ends, partial, second, coeff_second, from_second),
        (smem,) + (vmem,) * 5,
        2 * terms * members * cells,
    )
    received = lax.all_to_all(sums, "member", 0, 0, tiled=True)
    norm_factor = 1.0 / (members * n_member - 1)
    owned = jnp.sum(received, axis=0) * norm_factor
    return owned.swapaxes(1, 2).reshape(slots, variables, levels, slab_rows, lanes)


def solution(mesh):
    in_specs = (
        P("member", None, None, None, None, "tile"),
        P(None, None, None, "member", "tile"),
        P(None, None, "tile"),
        P(),
    )
    out_specs = P(None, None, None, "member", "tile")
    return jax.shard_map(body, mesh=mesh, in_specs=in_specs, out_specs=out_specs, check_vma=False)
```

```python
import math

import jax
import jax.numpy as jnp
from jax import lax
from jax.experimental import pallas as pl
from jax.experimental.pallas import tpu as pltpu
from jax.sharding import PartitionSpec as P

SWEEPS = 10
GROUPS = 4
CLASSES = 3
ANCHOR_WORK = 10**10
VMEM_LIMIT = 16 * 1024 * 1024


def lane_roll(value, shift):
    shift = shift % value.shape[-1]
    return value if shift == 0 else pltpu.roll(value, shift, 1)


def lane_index(shape):
    return lax.broadcasted_iota(jnp.int32, shape, 1)


def spread(row, rows=8):
    return jnp.broadcast_to(row, (rows, row.shape[-1]))


def whole(memory_space=pltpu.VMEM):
    return pl.BlockSpec(memory_space=memory_space)


def mirrors(level, row, levels, rows):
    return [
        (far_level, far_row)
        for far_level in (level, levels - 1 - level)
        for far_row in (row, rows - 1 - row)
    ]


def group_index(shape, start):
    part = shape[-1] // GROUPS
    return (lane_index(shape) + start) % shape[-1] // part


def own_strips(values):
    part = values[0].shape[-1] // GROUPS
    rolled = [lane_roll(value, part * g) for g, value in enumerate(values)]
    both = []
    for start in (SWEEPS, part - SWEEPS):
        group = group_index(values[0].shape, start)
        strip = rolled[0]
        for g in range(1, GROUPS):
            strip = jnp.where(group == g, rolled[g], strip)
        both.append(strip)
    return both


def packed_edges(first, second):
    part = first.shape[-1] // GROUPS
    place = lane_index(first.shape) % part
    moved = lane_roll(second, part // 2)
    to_right = jnp.where(place >= part // 2, first, moved)
    to_left = jnp.where(place < part // 2, first, moved)
    return to_right, to_left


def joined_strip(own, edge, index, halo):
    part = own.shape[-1] // GROUPS
    return jnp.where(halo, lane_roll(edge, -(index % 2) * (part // 2)), own)


def right_round():
    return lax.axis_index("tile") % CLASSES


def first_is_left():
    return (lax.axis_index("tile") == 0) | (right_round() != 0)


def total(terms):
    terms = list(terms)
    while len(terms) > 1:
        terms = [
            terms[i] + terms[i + 1] if i + 1 < len(terms) else terms[i]
            for i in range(0, len(terms), 2)
        ]
    return terms[0]


def around(planes, level, row, even_group=None):
    levels, rows = len(planes), len(planes[level])
    here = planes[level][row]
    terms = [lane_roll(here, 1), lane_roll(here, -1)]
    if row > 0:
        terms.append(planes[level][row - 1])
    if row < rows - 1:
        terms.append(planes[level][row + 1])
    elif even_group is not None:
        part = here.shape[-1] // GROUPS
        terms.append(jnp.where(even_group, lane_roll(here, -part), lane_roll(here, part)))
    if level > 0:
        terms.append(planes[level - 1][row])
    if level < levels - 1:
        terms.append(planes[level + 1][row])
    elif even_group is not None:
        terms.append(lane_roll(here, here.shape[-1] // 2))
    return total(terms)


def sweep(source, target, keep_at, square_at):
    levels, rows = source.shape[0], source.shape[1]
    planes = [[source[level, row] for row in range(rows)] for level in range(levels)]
    for level in range(levels):
        for row in range(rows):
            target[level, row] = keep_at(level, row) * planes[level][row] + square_at(
                level, row
            ) * around(planes, level, row)


def anchor_kernel(out_ref):
    out_ref[...] = jnp.zeros_like(out_ref)


def weigh_kernel(
    owner_ref,
    gathered_ref,
    pert_ref,
    coeff_ref,
    anchor_ref,
    field_ref,
    left_ref,
    right_ref,
    coeff_left_ref,
    coeff_right_ref,
    swept_ref,
    *rest,
):
    edge_refs, (grad_ref, keep_ref, square_ref) = rest[:CLASSES], rest[CLASSES:]
    members, terms, levels, rows, lanes = pert_ref.shape
    slab_rows = gathered_ref.shape[2]
    strip_levels, strip_rows = left_ref.shape[:2]
    for slab in range(rows // slab_rows):
        owner = owner_ref[slab]
        for term in range(terms):
            for inner in range(slab_rows):
                row = slab * slab_rows + inner
                grad_ref[pl.ds(term * levels * rows + row, levels, stride=rows), :] = gathered_ref[
                    owner, term, inner
                ]

    for level in range(levels):
        base = level * rows
        coeff = coeff_ref[level]
        gradients = [
            coeff * grad_ref[pl.ds(term * levels * rows + base, rows), :] for term in range(terms)
        ]
        for member in range(members):
            field_ref[pl.ds(base * members + member, rows, stride=members), :] = total(
                pert_ref[member, term, level].astype(jnp.float32) * gradients[term]
                for term in range(terms)
            )

    pairs = strip_levels * strip_rows // 2
    fields, coeffs = [], []
    for level in range(strip_levels):
        for row in range(strip_rows):
            index = level * strip_rows + row
            cells = mirrors(level, row, levels, rows)
            field = own_strips(
                [field_ref[pl.ds((l * rows + r) * members, members), :] for l, r in cells]
            )
            coeff = own_strips([spread(coeff_ref[l, pl.ds(r, 1), :]) for l, r in cells])
            fields.append(field[0])
            coeffs.append(coeff[0])
            left_ref[level, row], right_ref[level, row] = field
            coeff_left_ref[pl.ds(index, 1), :] = coeff[0][0:1]
            coeff_right_ref[pl.ds(index, 1), :] = coeff[1][0:1]
    for pair in range(pairs):
        edges = packed_edges(fields[2 * pair], fields[2 * pair + 1])
        coeff_edges = packed_edges(coeffs[2 * pair], coeffs[2 * pair + 1])
        for index, ref in enumerate(edge_refs):
            to_right = jnp.broadcast_to(right_round() == index, (members, lanes))
            ref[pl.ds(pair * members, members), :] = jnp.where(to_right, *edges)
            ref[pl.ds(pairs * members + pair, 1), :] = jnp.where(to_right, *coeff_edges)[0:1]

    @pl.when(lax.axis_index("tile") == 0)
    def _():
        sweep_strips(left_ref, coeff_left_ref, None, True, swept_ref, keep_ref, square_ref)


def interior_kernel(
    field_ref, coeff_ref, pert_ref, out_ref, ends_ref, other_ref, keep_ref, square_ref, inverse_ref
):
    levels, rows, members, lanes = field_ref.shape
    terms = pert_ref.shape[1]
    width = lanes // levels
    shift = jnp.where(first_is_left(), 0, lanes - width)
    slot = (lane_index((rows, lanes)) + shift) % lanes // width

    def pack_ends(member):
        for term in range(terms):
            ends = None
            for index, level in enumerate(level_slots(levels)):
                value = pert_ref[member, term, level].astype(jnp.float32)
                moved = lane_roll(value, width * (index + 1))
                ends = moved if ends is None else jnp.where(slot == index, moved, ends)
            ends_ref[member, term] = ends

    row_index = lax.broadcasted_iota(jnp.int32, (rows, lanes), 0)
    for level in range(levels):
        here = coeff_ref[level]
        beside = [
            lane_roll(here, 1),
            lane_roll(here, -1),
            jnp.where(row_index > 0, pltpu.roll(here, 1, 0), 0.0),
            jnp.where(row_index < rows - 1, pltpu.roll(here, rows - 1, 0), 0.0),
        ]
        if level > 0:
            beside.append(coeff_ref[level - 1])
        if level < levels - 1:
            beside.append(coeff_ref[level + 1])
        keep_ref[level] = 1.0 - here * total(beside)
        square_ref[level] = here * here
        inverse_ref[level] = 1.0 / here

    def keep_at(level, row):
        return keep_ref[level, pl.ds(row, 1), :]

    def square_at(level, row):
        return square_ref[level, pl.ds(row, 1), :]

    sweep(field_ref, other_ref, keep_at, square_at)
    sweep(other_ref, out_ref, keep_at, square_at)

    pairs = SWEEPS // 2 - 1
    share = members // pairs

    def pair(index, carry):
        sweep(out_ref, other_ref, keep_at, square_at)
        sweep(other_ref, out_ref, keep_at, square_at)
        for extra in range(share):
            pack_ends(index * share + extra)
        return carry

    lax.fori_loop(0, pairs, pair, 0)
    for member in range(pairs * share, members):
        pack_ends(member)
    for level in range(levels):
        for row in range(rows):
            out_ref[level, row] = out_ref[level, row] * inverse_ref[level, pl.ds(row, 1), :]


def swept_strips(strip_at, coeff_at, edge_at, shape, is_left, keep_ref, square_ref):
    strip_levels, strip_rows, members, lanes = shape
    part = lanes // GROUPS
    pairs = strip_levels * strip_rows // 2
    lane = lane_index((members, lanes))
    even_group = (lane + jnp.where(is_left, SWEEPS, part - SWEEPS)) // part % 2 == 0
    halo = (lane + jnp.where(is_left, SWEEPS, 0)) % part < SWEEPS
    planes, coeffs = [], []
    for level in range(strip_levels):
        plane, coeff_plane = [], []
        for row in range(strip_rows):
            index = level * strip_rows + row
            edge = edge_at(index // 2 * members, members)
            coeff_edge = spread(edge_at(pairs * members + index // 2, 1), members)
            plane.append(joined_strip(strip_at(level, row), edge, index, halo))
            coeff_own = spread(coeff_at(index), members)
            coeff_plane.append(joined_strip(coeff_own, coeff_edge, index, halo))
        planes.append(plane)
        coeffs.append(coeff_plane)
    for level in range(strip_levels):
        for row in range(strip_rows):
            here = coeffs[level][row]
            keep_ref[level, row] = 1.0 - here * around(coeffs, level, row, even_group)
            square_ref[level, row] = here * here
    for _ in range(SWEEPS):
        planes = [
            [
                keep_ref[level, row] * planes[level][row]
                + square_ref[level, row] * around(planes, level, row, even_group)
                for row in range(strip_rows)
            ]
            for level in range(strip_levels)
        ]
    for level in range(strip_levels):
        for row in range(strip_rows):
            coeff = spread(coeff_at(level * strip_rows + row), members)
            planes[level][row] = planes[level][row] / jnp.where(coeff > 0.0, coeff, 1.0)
    return planes


def edge_reader(edge_ref, lanes):
    if edge_ref is None:
        return lambda place, rows: jnp.zeros((rows, lanes), jnp.float32)
    return lambda place, rows: edge_ref[pl.ds(place, rows), :]


def sweep_strips(strip_ref, coeff_ref, edge_ref, is_left, out_ref, keep_ref, square_ref):
    planes = swept_strips(
        lambda level, row: strip_ref[level, row],
        lambda index: coeff_ref[pl.ds(index, 1), :],
        edge_reader(edge_ref, strip_ref.shape[-1]),
        strip_ref.shape,
        is_left,
        keep_ref,
        square_ref,
    )
    for level, plane in enumerate(planes):
        for row, value in enumerate(plane):
            out_ref[level, row] = value


def early_kernel(
    left_ref, right_ref, coeff_left_ref, coeff_right_ref, edge_ref, before_ref, out_ref, *scratch
):
    tile, turn = lax.axis_index("tile"), right_round()
    out_ref[...] = before_ref[...]

    @pl.when(turn == 1)
    def _():
        sweep_strips(left_ref, coeff_left_ref, edge_ref, True, out_ref, *scratch)

    @pl.when((turn == 0) & (tile > 0))
    def _():
        sweep_strips(right_ref, coeff_right_ref, edge_ref, False, out_ref, *scratch)


def later_kernel(left_ref, coeff_left_ref, edge_ref, before_ref, out_ref, *scratch):
    out_ref[...] = before_ref[...]

    @pl.when(right_round() == 2)
    def _():
        sweep_strips(left_ref, coeff_left_ref, edge_ref, True, out_ref, *scratch)


def outer_lanes(shape, is_left):
    return (lane_index(shape) + jnp.where(is_left, 0, SWEEPS)) % shape[-1] < SWEEPS


def level_slots(levels):
    near = list(range(levels // 2))
    return near + [levels - 1 - level for level in near]


def partial_kernel(pert_ref, interior_ref, swept_ref, out_ref, local_ref):
    members, terms, levels, rows, lanes = pert_ref.shape
    part = lanes // GROUPS
    outer = outer_lanes((members, lanes), first_is_left())
    for level in range(swept_ref.shape[0]):
        for row in range(swept_ref.shape[1]):
            final = swept_ref[level, row]
            for g, (l, r) in enumerate(mirrors(level, row, levels, rows)):
                local_ref[pl.ds((l * rows + r) * members, members), :] = jnp.where(
                    outer, lane_roll(final, -part * g), interior_ref[l, r]
                )

    for level in range(levels):
        base = level * rows
        fields = [
            local_ref[pl.ds(base * members + member, rows, stride=members), :]
            for member in range(members)
        ]
        for term in range(terms):
            out_ref[pl.ds(term * levels * rows + base, rows), :] = total(
                pert_ref[member, term, level].astype(jnp.float32) * fields[member]
                for member in range(members)
            )


def finish_kernel(
    owner_ref,
    ends_ref,
    partial_ref,
    left_ref,
    right_ref,
    coeff_left_ref,
    coeff_right_ref,
    *rest,
):
    edge_refs, rest = rest[:CLASSES], rest[CLASSES:]
    out_ref, local_ref, sum_ref, keep_ref, square_ref = rest
    members, terms, rows, lanes = ends_ref.shape
    slab_rows, levels = out_ref.shape[2], out_ref.shape[3]
    part, half, width = lanes // GROUPS, lanes // 2, lanes // levels
    is_left = jnp.logical_not(first_is_left())
    turn = jnp.where(lax.axis_index("tile") == 0, 0, jnp.where(right_round() == 1, 1, 2))

    def edge_at(place, count):
        values = [ref[pl.ds(place, count), :] for ref in edge_refs]
        return jnp.where(turn == 0, values[0], jnp.where(turn == 1, values[1], values[2]))

    def strip_at(level, row):
        return jnp.where(is_left, left_ref[level, row], right_ref[level, row])

    def coeff_at(index):
        place = pl.ds(index, 1)
        return jnp.where(is_left, coeff_left_ref[place, :], coeff_right_ref[place, :])

    planes = swept_strips(
        strip_at, coeff_at, edge_at, left_ref.shape, is_left, keep_ref, square_ref
    )
    strip_levels, strip_rows = len(planes), len(planes[0])
    shift = jnp.where(is_left, half - width, 0)
    slot = (lane_index((members, lanes)) + shift) % half // width
    for row in range(strip_rows):
        for mirror in range(2):
            ends = None
            for level in range(strip_levels):
                moved = lane_roll(planes[level][row], width * (level + 1) - part * mirror)
                ends = moved if ends is None else jnp.where(slot == level, moved, ends)
            target = rows - 1 - row if mirror else row
            local_ref[pl.ds(target, members, stride=rows), :] = ends
    fields = [local_ref[pl.ds(member * rows, rows), :] for member in range(members)]
    outer = outer_lanes((rows, lanes), is_left)
    for term in range(terms):
        added = total(ends_ref[member, term] * fields[member] for member in range(members))
        for index, level in enumerate(level_slots(levels)):
            place = pl.ds((term * levels + level) * rows, rows)
            sum_ref[place, :] = jnp.where(
                outer, lane_roll(added, -width * (index + 1)), partial_ref[place, :]
            )
    for slab in range(rows // slab_rows):
        owner = owner_ref[slab]
        for term in range(terms):
            for inner in range(slab_rows):
                row = slab * slab_rows + inner
                out_ref[owner, term, inner] = sum_ref[
                    pl.ds(term * levels * rows + row, levels, stride=rows), :
                ]


def local_call(kernel, name, outs, scratch, operands, places, work):
    def shape_of(out):
        return out if isinstance(out, jax.ShapeDtypeStruct) else jax.ShapeDtypeStruct(out, jnp.float32)

    shapes = tuple(shape_of(out) for out in outs)
    specs = tuple(whole() for _ in outs)
    moved = sum(math.prod(x.shape) * x.dtype.itemsize for x in tuple(operands) + shapes)
    single = len(outs) == 1
    return pl.pallas_call(
        kernel,
        out_shape=shapes[0] if single else shapes,
        in_specs=[whole(place) for place in places],
        out_specs=specs[0] if single else specs,
        scratch_shapes=[
            pltpu.VMEM(item, jnp.float32) if isinstance(item, tuple) else item for item in scratch
        ],
        compiler_params=pltpu.CompilerParams(vmem_limit_bytes=VMEM_LIMIT),
        cost_estimate=pl.CostEstimate(flops=work, bytes_accessed=moved, transcendentals=0),
        name=name,
    )(*operands)


def body(perturbations, gradient_store, diffusivity, slab_owner):
    members, slots, variables, levels, rows, lanes = perturbations.shape
    terms = slots * variables
    n_member = lax.axis_size("member")
    n_tile = lax.axis_size("tile")
    slab_rows = gradient_store.shape[3]
    cells = levels * rows * lanes
    strip_levels, strip_rows = levels // 2, rows // 2
    strips = strip_levels * strip_rows
    wide_strip = (strip_levels, strip_rows, members, lanes)
    strip_scratch = [wide_strip, wide_strip]
    coeff_strip = (strips, lanes)
    wide_field = (levels, rows, members, lanes)
    flat_field = (levels * rows * members, lanes)
    field_coeff = (levels, rows, lanes)
    edge_shape = (strips // 2 * (members + 1), lanes)
    grad_shape = (terms * levels * rows, lanes)
    vmem, smem = pltpu.VMEM, pltpu.SMEM

    pert = perturbations.reshape(members, terms, levels, rows, lanes)
    slab = gradient_store.reshape(terms, levels, slab_rows, lanes).swapaxes(1, 2)
    anchor = local_call(anchor_kernel, "anchor", [(8, lanes)], [], (), (), ANCHOR_WORK)
    gathered = lax.all_gather(slab, "member", axis=0, tiled=False)

    field, left, right, coeff_left, coeff_right, swept, *edges = local_call(
        weigh_kernel,
        "weigh",
        [flat_field, wide_strip, wide_strip, coeff_strip, coeff_strip, wide_strip]
        + [edge_shape] * CLASSES,
        [grad_shape] + strip_scratch,
        (slab_owner, gathered, pert, diffusivity, anchor),
        (smem, vmem, vmem, vmem, vmem),
        2 * terms * members * cells,
    )
    edges = [
        lax.ppermute(
            values,
            "tile",
            [pair for i in range(turn, n_tile - 1, CLASSES) for pair in ((i, i + 1), (i + 1, i))],
        )
        for turn, values in enumerate(edges)
    ]

    interior, ends = local_call(
        interior_kernel,
        "interior",
        [wide_field, (members, terms, rows, lanes)],
        [wide_field, field_coeff, field_coeff, field_coeff],
        (field.reshape(wide_field), diffusivity, pert),
        (vmem,) * 3,
        8 * SWEEPS * members * cells,
    )
    swept = local_call(
        early_kernel,
        "early_strips",
        [wide_strip],
        strip_scratch,
        (left, right, coeff_left, coeff_right, edges[0], swept),
        (vmem,) * 6,
        2 * SWEEPS * members * cells,
    )
    swept = local_call(
        later_kernel,
        "later_strips",
        [wide_strip],
        strip_scratch,
        (left, coeff_left, edges[1], swept),
        (vmem,) * 4,
        2 * SWEEPS * members * cells,
    )
    partial = local_call(
        partial_kernel,
        "partial",
        [grad_shape],
        [flat_field],
        (pert, interior, swept),
        (vmem,) * 3,
        2 * terms * members * cells,
    )
    sums = local_call(
        finish_kernel,
        "finish",
        [(n_member, terms, slab_rows, levels, lanes)],
        [(members * rows, lanes), grad_shape] + strip_scratch,
        (slab_owner, ends, partial, left, right, coeff_left, coeff_right, *edges),
        (smem,) + (vmem,) * (6 + CLASSES),
        2 * terms * members * cells,
    )
    received = lax.all_to_all(sums, "member", 0, 0, tiled=True)
    norm_factor = 1.0 / (members * n_member - 1)
    owned = jnp.sum(received, axis=0) * norm_factor
    return owned.swapaxes(1, 2).reshape(slots, variables, levels, slab_rows, lanes)


def solution(mesh):
    in_specs = (
        P("member", None, None, None, None, "tile"),
        P(None, None, None, "member", "tile"),
        P(None, None, "tile"),
        P(),
    )
    out_specs = P(None, None, None, "member", "tile")
    return jax.shard_map(body, mesh=mesh, in_specs=in_specs, out_specs=out_specs, check_vma=False)
```

```python
import math

import jax
import jax.numpy as jnp
from jax import lax
from jax.experimental import pallas as pl
from jax.experimental.pallas import tpu as pltpu
from jax.sharding import PartitionSpec as P

SWEEPS = 10
GROUPS = 4
ANCHOR_WORK = 10**10
VMEM_LIMIT = 16 * 1024 * 1024


def lane_roll(value, shift):
    shift = shift % value.shape[-1]
    return value if shift == 0 else pltpu.roll(value, shift, 1)


def lane_index(shape):
    return lax.broadcasted_iota(jnp.int32, shape, 1)


def spread(row, rows=8):
    return jnp.broadcast_to(row, (rows, row.shape[-1]))


def whole(memory_space=pltpu.VMEM):
    return pl.BlockSpec(memory_space=memory_space)


def mirrors(level, row, levels, rows):
    return [
        (far_level, far_row)
        for far_level in (level, levels - 1 - level)
        for far_row in (row, rows - 1 - row)
    ]


def group_index(shape, start):
    part = shape[-1] // GROUPS
    return (lane_index(shape) + start) % shape[-1] // part


def own_strips(values):
    part = values[0].shape[-1] // GROUPS
    rolled = [lane_roll(value, part * g) for g, value in enumerate(values)]
    both = []
    for start in (SWEEPS, part - SWEEPS):
        group = group_index(values[0].shape, start)
        strip = rolled[0]
        for g in range(1, GROUPS):
            strip = jnp.where(group == g, rolled[g], strip)
        both.append(strip)
    return both


def packed_edges(first, second):
    part = first.shape[-1] // GROUPS
    place = lane_index(first.shape) % part
    moved = lane_roll(second, part // 2)
    to_right = jnp.where(place >= part // 2, first, moved)
    to_left = jnp.where(place < part // 2, first, moved)
    return to_right, to_left


def joined_strip(own, edge, index, halo):
    part = own.shape[-1] // GROUPS
    return jnp.where(halo, lane_roll(edge, -(index % 2) * (part // 2)), own)


def swap_sides(values, swapped):
    first, second = values
    return jnp.where(swapped, second, first), jnp.where(swapped, first, second)


def first_is_left():
    return lax.axis_index("tile") % 2 == 1


def swap_pairs(start, n_member, n_tile):
    pairs = []
    for member in range(n_member):
        for tile in range(n_tile):
            other = tile + 1 if (tile - start) % 2 == 0 else tile - 1
            if 0 <= other < n_tile:
                pairs.append((member * n_tile + tile, member * n_tile + other))
            elif n_member % 2 == 0:
                pairs.append((member * n_tile + tile, (member ^ 1) * n_tile + tile))
    return pairs


def without_partner(is_left, n_tile):
    tile = lax.axis_index("tile")
    return jnp.where(is_left, tile == 0, tile == n_tile - 1)


def total(terms):
    terms = list(terms)
    while len(terms) > 1:
        terms = [
            terms[i] + terms[i + 1] if i + 1 < len(terms) else terms[i]
            for i in range(0, len(terms), 2)
        ]
    return terms[0]


def around(planes, level, row, even_group=None):
    levels, rows = len(planes), len(planes[level])
    here = planes[level][row]
    terms = [lane_roll(here, 1), lane_roll(here, -1)]
    if row > 0:
        terms.append(planes[level][row - 1])
    if row < rows - 1:
        terms.append(planes[level][row + 1])
    elif even_group is not None:
        part = here.shape[-1] // GROUPS
        terms.append(jnp.where(even_group, lane_roll(here, -part), lane_roll(here, part)))
    if level > 0:
        terms.append(planes[level - 1][row])
    if level < levels - 1:
        terms.append(planes[level + 1][row])
    elif even_group is not None:
        terms.append(lane_roll(here, here.shape[-1] // 2))
    return total(terms)


def sweep(source, target, keep_at, square_at):
    levels, rows = source.shape[0], source.shape[1]
    planes = [[source[level, row] for row in range(rows)] for level in range(levels)]
    for level in range(levels):
        for row in range(rows):
            target[level, row] = keep_at(level, row) * planes[level][row] + square_at(
                level, row
            ) * around(planes, level, row)


def anchor_kernel(out_ref):
    out_ref[...] = jnp.zeros_like(out_ref)


def weigh_kernel(
    owner_ref,
    gathered_ref,
    pert_ref,
    coeff_ref,
    anchor_ref,
    field_ref,
    first_ref,
    second_ref,
    coeff_first_ref,
    coeff_second_ref,
    to_first_ref,
    to_second_ref,
    grad_ref,
):
    members, terms, levels, rows, lanes = pert_ref.shape
    slab_rows = gathered_ref.shape[2]
    strip_levels, strip_rows = first_ref.shape[:2]
    left_first = jnp.broadcast_to(first_is_left(), (8, lanes))
    for slab in range(rows // slab_rows):
        owner = owner_ref[slab]
        for term in range(terms):
            for inner in range(slab_rows):
                row = slab * slab_rows + inner
                grad_ref[pl.ds(term * levels * rows + row, levels, stride=rows), :] = gathered_ref[
                    owner, term, inner
                ]

    for level in range(levels):
        base = level * rows
        coeff = coeff_ref[level]
        gradients = [
            coeff * grad_ref[pl.ds(term * levels * rows + base, rows), :] for term in range(terms)
        ]
        for member in range(members):
            field_ref[pl.ds(base * members + member, rows, stride=members), :] = total(
                pert_ref[member, term, level].astype(jnp.float32) * gradients[term]
                for term in range(terms)
            )

    pairs = strip_levels * strip_rows // 2
    fields, coeffs = [], []
    for level in range(strip_levels):
        for row in range(strip_rows):
            index = level * strip_rows + row
            cells = mirrors(level, row, levels, rows)
            field = own_strips(
                [field_ref[pl.ds((l * rows + r) * members, members), :] for l, r in cells]
            )
            coeff = own_strips([spread(coeff_ref[l, pl.ds(r, 1), :]) for l, r in cells])
            fields.append(field[0])
            coeffs.append(coeff[0])
            field = swap_sides(field[::-1], left_first)
            coeff = swap_sides(coeff[::-1], left_first)
            first_ref[level, row], second_ref[level, row] = field
            coeff_first_ref[pl.ds(index, 1), :] = coeff[0][0:1]
            coeff_second_ref[pl.ds(index, 1), :] = coeff[1][0:1]
    for pair in range(pairs):
        edges = packed_edges(fields[2 * pair], fields[2 * pair + 1])
        coeff_edges = packed_edges(coeffs[2 * pair], coeffs[2 * pair + 1])
        edges = swap_sides(edges, left_first)
        coeff_edges = swap_sides(coeff_edges, left_first)
        for ref, edge, coeff_edge in zip((to_first_ref, to_second_ref), edges, coeff_edges):
            ref[pl.ds(pair * members, members), :] = edge
            ref[pl.ds(pairs * members + pair, 1), :] = coeff_edge[0:1]


def interior_kernel(
    field_ref, coeff_ref, pert_ref, out_ref, ends_ref, other_ref, keep_ref, square_ref, inverse_ref
):
    levels, rows, members, lanes = field_ref.shape
    terms = pert_ref.shape[1]
    width = lanes // levels
    shift = jnp.where(first_is_left(), 0, lanes - width)
    slot = (lane_index((rows, lanes)) + shift) % lanes // width

    def pack_ends(member):
        for term in range(terms):
            ends = None
            for index, level in enumerate(level_slots(levels)):
                value = pert_ref[member, term, level].astype(jnp.float32)
                moved = lane_roll(value, width * (index + 1))
                ends = moved if ends is None else jnp.where(slot == index, moved, ends)
            ends_ref[member, term] = ends

    row_index = lax.broadcasted_iota(jnp.int32, (rows, lanes), 0)
    for level in range(levels):
        here = coeff_ref[level]
        beside = [
            lane_roll(here, 1),
            lane_roll(here, -1),
            jnp.where(row_index > 0, pltpu.roll(here, 1, 0), 0.0),
            jnp.where(row_index < rows - 1, pltpu.roll(here, rows - 1, 0), 0.0),
        ]
        if level > 0:
            beside.append(coeff_ref[level - 1])
        if level < levels - 1:
            beside.append(coeff_ref[level + 1])
        keep_ref[level] = 1.0 - here * total(beside)
        square_ref[level] = here * here
        inverse_ref[level] = 1.0 / here

    def keep_at(level, row):
        return keep_ref[level, pl.ds(row, 1), :]

    def square_at(level, row):
        return square_ref[level, pl.ds(row, 1), :]

    sweep(field_ref, other_ref, keep_at, square_at)
    sweep(other_ref, out_ref, keep_at, square_at)

    pairs = SWEEPS // 2 - 1
    share = members // pairs

    def pair(index, carry):
        sweep(out_ref, other_ref, keep_at, square_at)
        sweep(other_ref, out_ref, keep_at, square_at)
        for extra in range(share):
            pack_ends(index * share + extra)
        return carry

    lax.fori_loop(0, pairs, pair, 0)
    for member in range(pairs * share, members):
        pack_ends(member)
    for level in range(levels):
        for row in range(rows):
            out_ref[level, row] = out_ref[level, row] * inverse_ref[level, pl.ds(row, 1), :]


def swept_strips(strip_ref, coeff_ref, edge_ref, is_left, keep_ref, square_ref):
    outside = without_partner(is_left, lax.axis_size("tile"))
    strip_levels, strip_rows, members, lanes = strip_ref.shape
    part = lanes // GROUPS
    pairs = strip_levels * strip_rows // 2
    lane = lane_index((members, lanes))
    even_group = (lane + jnp.where(is_left, SWEEPS, part - SWEEPS)) // part % 2 == 0
    halo = (lane + jnp.where(is_left, SWEEPS, 0)) % part < SWEEPS
    planes, coeffs = [], []
    for level in range(strip_levels):
        plane, coeff_plane = [], []
        for row in range(strip_rows):
            index = level * strip_rows + row
            edge = edge_ref[pl.ds(index // 2 * members, members), :]
            edge = jnp.where(outside, 0.0, edge)
            coeff_edge = edge_ref[pl.ds(pairs * members + index // 2, 1), :]
            coeff_edge = spread(jnp.where(outside, 0.0, coeff_edge), members)
            plane.append(joined_strip(strip_ref[level, row], edge, index, halo))
            coeff_own = spread(coeff_ref[pl.ds(index, 1), :], members)
            coeff_plane.append(joined_strip(coeff_own, coeff_edge, index, halo))
        planes.append(plane)
        coeffs.append(coeff_plane)
    for level in range(strip_levels):
        for row in range(strip_rows):
            here = coeffs[level][row]
            keep_ref[level, row] = 1.0 - here * around(coeffs, level, row, even_group)
            square_ref[level, row] = here * here
    for _ in range(SWEEPS):
        planes = [
            [
                keep_ref[level, row] * planes[level][row]
                + square_ref[level, row] * around(planes, level, row, even_group)
                for row in range(strip_rows)
            ]
            for level in range(strip_levels)
        ]
    for level in range(strip_levels):
        for row in range(strip_rows):
            coeff = spread(coeff_ref[pl.ds(level * strip_rows + row, 1), :], members)
            planes[level][row] = planes[level][row] / jnp.where(coeff > 0.0, coeff, 1.0)
    return planes


def outer_lanes(shape, is_left):
    return (lane_index(shape) + jnp.where(is_left, 0, SWEEPS)) % shape[-1] < SWEEPS


def level_slots(levels):
    near = list(range(levels // 2))
    return near + [levels - 1 - level for level in near]


def partial_kernel(
    pert_ref, interior_ref, strip_ref, coeff_ref, edge_ref, out_ref, local_ref, keep_ref, square_ref
):
    members, terms, levels, rows, lanes = pert_ref.shape
    part = lanes // GROUPS
    is_left = first_is_left()
    planes = swept_strips(strip_ref, coeff_ref, edge_ref, is_left, keep_ref, square_ref)
    outer = outer_lanes((members, lanes), is_left)
    for level, plane in enumerate(planes):
        for row, final in enumerate(plane):
            for g, (l, r) in enumerate(mirrors(level, row, levels, rows)):
                local_ref[pl.ds((l * rows + r) * members, members), :] = jnp.where(
                    outer, lane_roll(final, -part * g), interior_ref[l, r]
                )

    for level in range(levels):
        base = level * rows
        fields = [
            local_ref[pl.ds(base * members + member, rows, stride=members), :]
            for member in range(members)
        ]
        for term in range(terms):
            out_ref[pl.ds(term * levels * rows + base, rows), :] = total(
                pert_ref[member, term, level].astype(jnp.float32) * fields[member]
                for member in range(members)
            )


def finish_kernel(
    owner_ref,
    ends_ref,
    partial_ref,
    strip_ref,
    coeff_ref,
    edge_ref,
    out_ref,
    local_ref,
    sum_ref,
    keep_ref,
    square_ref,
):
    members, terms, rows, lanes = ends_ref.shape
    slab_rows, levels = out_ref.shape[2], out_ref.shape[3]
    part, half, width = lanes // GROUPS, lanes // 2, lanes // levels
    is_left = jnp.logical_not(first_is_left())
    planes = swept_strips(strip_ref, coeff_ref, edge_ref, is_left, keep_ref, square_ref)
    strip_levels, strip_rows = len(planes), len(planes[0])
    shift = jnp.where(is_left, half - width, 0)
    slot = (lane_index((members, lanes)) + shift) % half // width
    for row in range(strip_rows):
        for mirror in range(2):
            ends = None
            for level in range(strip_levels):
                moved = lane_roll(planes[level][row], width * (level + 1) - part * mirror)
                ends = moved if ends is None else jnp.where(slot == level, moved, ends)
            target = rows - 1 - row if mirror else row
            local_ref[pl.ds(target, members, stride=rows), :] = ends
    fields = [local_ref[pl.ds(member * rows, rows), :] for member in range(members)]
    outer = outer_lanes((rows, lanes), is_left)
    for term in range(terms):
        added = total(ends_ref[member, term] * fields[member] for member in range(members))
        for index, level in enumerate(level_slots(levels)):
            place = pl.ds((term * levels + level) * rows, rows)
            sum_ref[place, :] = jnp.where(
                outer, lane_roll(added, -width * (index + 1)), partial_ref[place, :]
            )
    for slab in range(rows // slab_rows):
        owner = owner_ref[slab]
        for term in range(terms):
            for inner in range(slab_rows):
                row = slab * slab_rows + inner
                out_ref[owner, term, inner] = sum_ref[
                    pl.ds(term * levels * rows + row, levels, stride=rows), :
                ]


def local_call(kernel, name, outs, scratch, operands, places, work):
    def shape_of(out):
        return out if isinstance(out, jax.ShapeDtypeStruct) else jax.ShapeDtypeStruct(out, jnp.float32)

    shapes = tuple(shape_of(out) for out in outs)
    specs = tuple(whole() for _ in outs)
    moved = sum(math.prod(x.shape) * x.dtype.itemsize for x in tuple(operands) + shapes)
    single = len(outs) == 1
    return pl.pallas_call(
        kernel,
        out_shape=shapes[0] if single else shapes,
        in_specs=[whole(place) for place in places],
        out_specs=specs[0] if single else specs,
        scratch_shapes=[
            pltpu.VMEM(item, jnp.float32) if isinstance(item, tuple) else item for item in scratch
        ],
        compiler_params=pltpu.CompilerParams(vmem_limit_bytes=VMEM_LIMIT),
        cost_estimate=pl.CostEstimate(flops=work, bytes_accessed=moved, transcendentals=0),
        name=name,
    )(*operands)


def body(perturbations, gradient_store, diffusivity, slab_owner):
    members, slots, variables, levels, rows, lanes = perturbations.shape
    terms = slots * variables
    n_member = lax.axis_size("member")
    n_tile = lax.axis_size("tile")
    slab_rows = gradient_store.shape[3]
    cells = levels * rows * lanes
    strip_levels, strip_rows = levels // 2, rows // 2
    strips = strip_levels * strip_rows
    wide_strip = (strip_levels, strip_rows, members, lanes)
    strip_scratch = [wide_strip, wide_strip]
    coeff_strip = (strips, lanes)
    wide_field = (levels, rows, members, lanes)
    flat_field = (levels * rows * members, lanes)
    field_coeff = (levels, rows, lanes)
    edge_shape = (strips // 2 * (members + 1), lanes)
    grad_shape = (terms * levels * rows, lanes)
    vmem, smem = pltpu.VMEM, pltpu.SMEM

    pert = perturbations.reshape(members, terms, levels, rows, lanes)
    slab = gradient_store.reshape(terms, levels, slab_rows, lanes).swapaxes(1, 2)
    anchor = local_call(anchor_kernel, "anchor", [(8, lanes)], [], (), (), ANCHOR_WORK)
    gathered = lax.all_gather(slab, "member", axis=0, tiled=False)

    field, first, second, coeff_first, coeff_second, to_first, to_second = local_call(
        weigh_kernel,
        "weigh",
        [flat_field, wide_strip, wide_strip, coeff_strip, coeff_strip, edge_shape, edge_shape],
        [grad_shape],
        (slab_owner, gathered, pert, diffusivity, anchor),
        (smem, vmem, vmem, vmem, vmem),
        2 * terms * members * cells,
    )
    from_first, from_second = (
        lax.ppermute(edges, ("member", "tile"), swap_pairs(start, n_member, n_tile))
        for start, edges in ((0, to_first), (1, to_second))
    )

    interior, ends = local_call(
        interior_kernel,
        "interior",
        [wide_field, (members, terms, rows, lanes)],
        [wide_field, field_coeff, field_coeff, field_coeff],
        (field.reshape(wide_field), diffusivity, pert),
        (vmem,) * 3,
        8 * SWEEPS * members * cells,
    )
    partial = local_call(
        partial_kernel,
        "partial",
        [grad_shape],
        [flat_field] + strip_scratch,
        (pert, interior, first, coeff_first, from_first),
        (vmem,) * 5,
        2 * SWEEPS * members * cells,
    )
    sums = local_call(
        finish_kernel,
        "finish",
        [(n_member, terms, slab_rows, levels, lanes)],
        [(members * rows, lanes), grad_shape] + strip_scratch,
        (slab_owner, ends, partial, second, coeff_second, from_second),
        (smem,) + (vmem,) * 5,
        2 * terms * members * cells,
    )
    received = lax.all_to_all(sums, "member", 0, 0, tiled=True)
    norm_factor = 1.0 / (members * n_member - 1)
    owned = jnp.sum(received, axis=0) * norm_factor
    return owned.swapaxes(1, 2).reshape(slots, variables, levels, slab_rows, lanes)


def solution(mesh):
    in_specs = (
        P("member", None, None, None, None, "tile"),
        P(None, None, None, "member", "tile"),
        P(None, None, "tile"),
        P(),
    )
    out_specs = P(None, None, None, "member", "tile")
    return jax.shard_map(body, mesh=mesh, in_specs=in_specs, out_specs=out_specs, check_vma=False)
```

```python
import math

import jax
import jax.numpy as jnp
from jax import lax
from jax.experimental import pallas as pl
from jax.experimental.pallas import tpu as pltpu
from jax.sharding import PartitionSpec as P

SWEEPS = 10
GROUPS = 4
ANCHOR_WORK = 10**10
VMEM_LIMIT = 16 * 1024 * 1024


def lane_roll(value, shift):
    shift = shift % value.shape[-1]
    return value if shift == 0 else pltpu.roll(value, shift, 1)


def lane_index(shape):
    return lax.broadcasted_iota(jnp.int32, shape, 1)


def spread(row, rows=8):
    return jnp.broadcast_to(row, (rows, row.shape[-1]))


def whole(memory_space=pltpu.VMEM):
    return pl.BlockSpec(memory_space=memory_space)


def mirrors(level, row, levels, rows):
    return [
        (far_level, far_row)
        for far_level in (level, levels - 1 - level)
        for far_row in (row, rows - 1 - row)
    ]


def group_index(shape, start):
    part = shape[-1] // GROUPS
    return (lane_index(shape) + start) % shape[-1] // part


def own_strips(values):
    part = values[0].shape[-1] // GROUPS
    rolled = [lane_roll(value, part * g) for g, value in enumerate(values)]
    both = []
    for start in (SWEEPS, part - SWEEPS):
        group = group_index(values[0].shape, start)
        strip = rolled[0]
        for g in range(1, GROUPS):
            strip = jnp.where(group == g, rolled[g], strip)
        both.append(strip)
    return both


def packed_edges(first, second):
    part = first.shape[-1] // GROUPS
    place = lane_index(first.shape) % part
    moved = lane_roll(second, part // 2)
    to_right = jnp.where(place >= part // 2, first, moved)
    to_left = jnp.where(place < part // 2, first, moved)
    return to_right, to_left


def joined_strip(own, edge, index, halo):
    part = own.shape[-1] // GROUPS
    return jnp.where(halo, lane_roll(edge, -(index % 2) * (part // 2)), own)


def swap_sides(values, swapped):
    first, second = values
    return jnp.where(swapped, second, first), jnp.where(swapped, first, second)


def first_is_left():
    return lax.axis_index("tile") % 2 == 1


def swap_pairs(start, n_member, n_tile):
    pairs = []
    for member in range(n_member):
        for tile in range(n_tile):
            other = tile + 1 if (tile - start) % 2 == 0 else tile - 1
            if 0 <= other < n_tile:
                pairs.append((member * n_tile + tile, member * n_tile + other))
            elif n_member % 2 == 0:
                pairs.append((member * n_tile + tile, (member ^ 1) * n_tile + tile))
    return pairs


def without_partner(is_left, n_tile):
    tile = lax.axis_index("tile")
    return jnp.where(is_left, tile == 0, tile == n_tile - 1)


def total(terms):
    terms = list(terms)
    while len(terms) > 1:
        terms = [
            terms[i] + terms[i + 1] if i + 1 < len(terms) else terms[i]
            for i in range(0, len(terms), 2)
        ]
    return terms[0]


def around(planes, level, row, even_group=None):
    levels, rows = len(planes), len(planes[level])
    here = planes[level][row]
    terms = [lane_roll(here, 1), lane_roll(here, -1)]
    if row > 0:
        terms.append(planes[level][row - 1])
    if row < rows - 1:
        terms.append(planes[level][row + 1])
    elif even_group is not None:
        part = here.shape[-1] // GROUPS
        terms.append(jnp.where(even_group, lane_roll(here, -part), lane_roll(here, part)))
    if level > 0:
        terms.append(planes[level - 1][row])
    if level < levels - 1:
        terms.append(planes[level + 1][row])
    elif even_group is not None:
        terms.append(lane_roll(here, here.shape[-1] // 2))
    return total(terms)


def sweep(source, target, keep_at, square_at):
    levels, rows = source.shape[0], source.shape[1]
    planes = [[source[level, row] for row in range(rows)] for level in range(levels)]
    for level in range(levels):
        for row in range(rows):
            target[level, row] = keep_at(level, row) * planes[level][row] + square_at(
                level, row
            ) * around(planes, level, row)


def anchor_kernel(out_ref):
    out_ref[...] = jnp.zeros_like(out_ref)


def weigh_kernel(
    owner_ref,
    gathered_ref,
    pert_ref,
    coeff_ref,
    anchor_ref,
    field_ref,
    left_ref,
    right_ref,
    coeff_left_ref,
    coeff_right_ref,
    to_first_ref,
    to_second_ref,
    grad_ref,
):
    members, terms, levels, rows, lanes = pert_ref.shape
    slab_rows = gathered_ref.shape[2]
    strip_levels, strip_rows = left_ref.shape[:2]
    left_first = jnp.broadcast_to(first_is_left(), (8, lanes))
    for slab in range(rows // slab_rows):
        owner = owner_ref[slab]
        for term in range(terms):
            for inner in range(slab_rows):
                row = slab * slab_rows + inner
                grad_ref[pl.ds(term * levels * rows + row, levels, stride=rows), :] = gathered_ref[
                    owner, term, inner
                ]

    for level in range(levels):
        base = level * rows
        coeff = coeff_ref[level]
        gradients = [
            coeff * grad_ref[pl.ds(term * levels * rows + base, rows), :] for term in range(terms)
        ]
        for member in range(members):
            field_ref[pl.ds(base * members + member, rows, stride=members), :] = total(
                pert_ref[member, term, level].astype(jnp.float32) * gradients[term]
                for term in range(terms)
            )

    pairs = strip_levels * strip_rows // 2
    fields, coeffs = [], []
    for level in range(strip_levels):
        for row in range(strip_rows):
            index = level * strip_rows + row
            cells = mirrors(level, row, levels, rows)
            field = own_strips(
                [field_ref[pl.ds((l * rows + r) * members, members), :] for l, r in cells]
            )
            coeff = own_strips([spread(coeff_ref[l, pl.ds(r, 1), :]) for l, r in cells])
            fields.append(field[0])
            coeffs.append(coeff[0])
            left_ref[level, row], right_ref[level, row] = field
            coeff_left_ref[pl.ds(index, 1), :] = coeff[0][0:1]
            coeff_right_ref[pl.ds(index, 1), :] = coeff[1][0:1]
    for pair in range(pairs):
        edges = packed_edges(fields[2 * pair], fields[2 * pair + 1])
        coeff_edges = packed_edges(coeffs[2 * pair], coeffs[2 * pair + 1])
        edges = swap_sides(edges, left_first)
        coeff_edges = swap_sides(coeff_edges, left_first)
        for ref, edge, coeff_edge in zip((to_first_ref, to_second_ref), edges, coeff_edges):
            ref[pl.ds(pair * members, members), :] = edge
            ref[pl.ds(pairs * members + pair, 1), :] = coeff_edge[0:1]


def interior_kernel(
    field_ref, coeff_ref, out_ref, other_ref, keep_ref, square_ref, inverse_ref
):
    levels, rows, members, lanes = field_ref.shape
    row_index = lax.broadcasted_iota(jnp.int32, (rows, lanes), 0)
    for level in range(levels):
        here = coeff_ref[level]
        beside = [
            lane_roll(here, 1),
            lane_roll(here, -1),
            jnp.where(row_index > 0, pltpu.roll(here, 1, 0), 0.0),
            jnp.where(row_index < rows - 1, pltpu.roll(here, rows - 1, 0), 0.0),
        ]
        if level > 0:
            beside.append(coeff_ref[level - 1])
        if level < levels - 1:
            beside.append(coeff_ref[level + 1])
        keep_ref[level] = 1.0 - here * total(beside)
        square_ref[level] = here * here
        inverse_ref[level] = 1.0 / here

    def keep_at(level, row):
        return keep_ref[level, pl.ds(row, 1), :]

    def square_at(level, row):
        return square_ref[level, pl.ds(row, 1), :]

    sweep(field_ref, other_ref, keep_at, square_at)
    sweep(other_ref, out_ref, keep_at, square_at)

    def pair(index, carry):
        sweep(out_ref, other_ref, keep_at, square_at)
        sweep(other_ref, out_ref, keep_at, square_at)
        return carry

    lax.fori_loop(0, SWEEPS // 2 - 1, pair, 0)
    for level in range(levels):
        for row in range(rows):
            out_ref[level, row] = out_ref[level, row] * inverse_ref[level, pl.ds(row, 1), :]


class Strips:
    def __init__(self, strip_ref, coeff_ref, edge_at, is_left, keep_ref, square_ref):
        self.levels, self.rows, self.members, lanes = strip_ref.shape
        self.coeff_ref, self.keep_ref, self.square_ref = coeff_ref, keep_ref, square_ref
        part = lanes // GROUPS
        pairs = self.levels * self.rows // 2
        shape = (self.members, lanes)
        self.even_group = group_index(shape, SWEEPS if is_left else part - SWEEPS) % 2 == 0
        place = lane_index(shape) % part
        halo = place >= part - SWEEPS if is_left else place < SWEEPS
        self.planes, coeffs = [], []
        for level in range(self.levels):
            plane, coeff_plane = [], []
            for row in range(self.rows):
                index = level * self.rows + row
                edge = edge_at(index // 2 * self.members, self.members)
                coeff_edge = spread(edge_at(pairs * self.members + index // 2, 1), self.members)
                plane.append(joined_strip(strip_ref[level, row], edge, index, halo))
                coeff_plane.append(joined_strip(self.own_coeff(level, row), coeff_edge, index, halo))
            self.planes.append(plane)
            coeffs.append(coeff_plane)
        for level in range(self.levels):
            for row in range(self.rows):
                here = coeffs[level][row]
                keep_ref[level, row] = 1.0 - here * around(coeffs, level, row, self.even_group)
                square_ref[level, row] = here * here

    def own_coeff(self, level, row):
        return spread(self.coeff_ref[pl.ds(level * self.rows + row, 1), :], self.members)

    def step(self):
        self.planes = [
            [
                self.keep_ref[level, row] * self.planes[level][row]
                + self.square_ref[level, row] * around(self.planes, level, row, self.even_group)
                for row in range(self.rows)
            ]
            for level in range(self.levels)
        ]

    def final(self, level, row):
        coeff = self.own_coeff(level, row)
        return self.planes[level][row] / jnp.where(coeff > 0.0, coeff, 1.0)


def finish_kernel(
    owner_ref,
    pert_ref,
    interior_ref,
    left_ref,
    right_ref,
    coeff_left_ref,
    coeff_right_ref,
    from_first_ref,
    from_second_ref,
    out_ref,
    local_ref,
    sum_ref,
    keep_left_ref,
    square_left_ref,
    keep_right_ref,
    square_right_ref,
):
    members, terms, levels, rows, lanes = pert_ref.shape
    slab_rows = out_ref.shape[2]
    part = lanes // GROUPS
    left_first = first_is_left()

    def edge_reader(is_left):
        outside = without_partner(is_left, lax.axis_size("tile"))

        def edge_at(place, count):
            first = from_first_ref[pl.ds(place, count), :]
            second = from_second_ref[pl.ds(place, count), :]
            edge = jnp.where(left_first == is_left, first, second)
            return jnp.where(outside, 0.0, edge)

        return edge_at

    left = Strips(
        left_ref, coeff_left_ref, edge_reader(True), True, keep_left_ref, square_left_ref
    )
    right = Strips(
        right_ref, coeff_right_ref, edge_reader(False), False, keep_right_ref, square_right_ref
    )
    for _ in range(SWEEPS):
        left.step()
        right.step()
    lane = lane_index((members, lanes))
    for level in range(left.levels):
        for row in range(left.rows):
            left_end, right_end = left.final(level, row), right.final(level, row)
            for g, (l, r) in enumerate(mirrors(level, row, levels, rows)):
                ends = jnp.where(
                    lane < lanes // 2,
                    lane_roll(left_end, -part * g),
                    lane_roll(right_end, -part * g),
                )
                local_ref[pl.ds((l * rows + r) * members, members), :] = jnp.where(
                    (lane < SWEEPS) | (lane >= lanes - SWEEPS), ends, interior_ref[l, r]
                )

    for level in range(levels):
        base = level * rows
        fields = [
            local_ref[pl.ds(base * members + member, rows, stride=members), :]
            for member in range(members)
        ]
        for term in range(terms):
            sum_ref[pl.ds(term * levels * rows + base, rows), :] = total(
                pert_ref[member, term, level].astype(jnp.float32) * fields[member]
                for member in range(members)
            )
    for slab in range(rows // slab_rows):
        owner = owner_ref[slab]
        for term in range(terms):
            for inner in range(slab_rows):
                row = slab * slab_rows + inner
                out_ref[owner, term, inner] = sum_ref[
                    pl.ds(term * levels * rows + row, levels, stride=rows), :
                ]


def local_call(kernel, name, outs, scratch, operands, places, work):
    def shape_of(out):
        return out if isinstance(out, jax.ShapeDtypeStruct) else jax.ShapeDtypeStruct(out, jnp.float32)

    shapes = tuple(shape_of(out) for out in outs)
    specs = tuple(whole() for _ in outs)
    moved = sum(math.prod(x.shape) * x.dtype.itemsize for x in tuple(operands) + shapes)
    single = len(outs) == 1
    return pl.pallas_call(
        kernel,
        out_shape=shapes[0] if single else shapes,
        in_specs=[whole(place) for place in places],
        out_specs=specs[0] if single else specs,
        scratch_shapes=[
            pltpu.VMEM(item, jnp.float32) if isinstance(item, tuple) else item for item in scratch
        ],
        compiler_params=pltpu.CompilerParams(vmem_limit_bytes=VMEM_LIMIT),
        cost_estimate=pl.CostEstimate(flops=work, bytes_accessed=moved, transcendentals=0),
        name=name,
    )(*operands)


def body(perturbations, gradient_store, diffusivity, slab_owner):
    members, slots, variables, levels, rows, lanes = perturbations.shape
    terms = slots * variables
    n_member = lax.axis_size("member")
    n_tile = lax.axis_size("tile")
    slab_rows = gradient_store.shape[3]
    cells = levels * rows * lanes
    strip_levels, strip_rows = levels // 2, rows // 2
    strips = strip_levels * strip_rows
    wide_strip = (strip_levels, strip_rows, members, lanes)
    coeff_strip = (strips, lanes)
    wide_field = (levels, rows, members, lanes)
    flat_field = (levels * rows * members, lanes)
    field_coeff = (levels, rows, lanes)
    edge_shape = (strips // 2 * (members + 1), lanes)
    grad_shape = (terms * levels * rows, lanes)
    vmem, smem = pltpu.VMEM, pltpu.SMEM

    pert = perturbations.reshape(members, terms, levels, rows, lanes)
    slab = gradient_store.reshape(terms, levels, slab_rows, lanes).swapaxes(1, 2)
    anchor = local_call(anchor_kernel, "anchor", [(8, lanes)], [], (), (), ANCHOR_WORK)
    gathered = lax.all_gather(slab, "member", axis=0, tiled=False)

    field, left, right, coeff_left, coeff_right, to_first, to_second = local_call(
        weigh_kernel,
        "weigh",
        [flat_field, wide_strip, wide_strip, coeff_strip, coeff_strip, edge_shape, edge_shape],
        [grad_shape],
        (slab_owner, gathered, pert, diffusivity, anchor),
        (smem, vmem, vmem, vmem, vmem),
        2 * terms * members * cells,
    )
    from_first, from_second = (
        lax.ppermute(edges, ("member", "tile"), swap_pairs(start, n_member, n_tile))
        for start, edges in ((0, to_first), (1, to_second))
    )

    interior = local_call(
        interior_kernel,
        "interior",
        [wide_field],
        [wide_field, field_coeff, field_coeff, field_coeff],
        (field.reshape(wide_field), diffusivity),
        (vmem,) * 2,
        8 * SWEEPS * members * cells,
    )
    sums = local_call(
        finish_kernel,
        "finish",
        [(n_member, terms, slab_rows, levels, lanes)],
        [flat_field, grad_shape] + [wide_strip] * 4,
        (
            slab_owner,
            pert,
            interior,
            left,
            right,
            coeff_left,
            coeff_right,
            from_first,
            from_second,
        ),
        (smem,) + (vmem,) * 8,
        2 * terms * members * cells,
    )
    received = lax.all_to_all(sums, "member", 0, 0, tiled=True)
    norm_factor = 1.0 / (members * n_member - 1)
    owned = jnp.sum(received, axis=0) * norm_factor
    return owned.swapaxes(1, 2).reshape(slots, variables, levels, slab_rows, lanes)


def solution(mesh):
    in_specs = (
        P("member", None, None, None, None, "tile"),
        P(None, None, None, "member", "tile"),
        P(None, None, "tile"),
        P(),
    )
    out_specs = P(None, None, None, "member", "tile")
    return jax.shard_map(body, mesh=mesh, in_specs=in_specs, out_specs=out_specs, check_vma=False)
```

```python
import math

import jax
import jax.numpy as jnp
from jax import lax
from jax.experimental import pallas as pl
from jax.experimental.pallas import tpu as pltpu
from jax.sharding import PartitionSpec as P

SWEEPS = 10
GROUPS = 4
BLOCK = 16
ANCHOR_WORK = 10**10
VMEM_LIMIT = 16 * 1024 * 1024


def lane_roll(value, shift):
    shift = shift % value.shape[-1]
    return value if shift == 0 else pltpu.roll(value, shift, 1)


def lane_index(shape):
    return lax.broadcasted_iota(jnp.int32, shape, 1)


def spread(row, rows=8):
    return jnp.broadcast_to(row, (rows, row.shape[-1]))


def whole(memory_space=pltpu.VMEM):
    return pl.BlockSpec(memory_space=memory_space)


def mirrors(level, row, levels, rows):
    return [
        (far_level, far_row)
        for far_level in (level, levels - 1 - level)
        for far_row in (row, rows - 1 - row)
    ]


def group_index(shape, start):
    part = shape[-1] // GROUPS
    return (lane_index(shape) + start) % shape[-1] // part


def own_strips(values):
    part = values[0].shape[-1] // GROUPS
    rolled = [lane_roll(value, part * g) for g, value in enumerate(values)]
    both = []
    for start in (SWEEPS, part - SWEEPS):
        group = group_index(values[0].shape, start)
        strip = rolled[0]
        for g in range(1, GROUPS):
            strip = jnp.where(group == g, rolled[g], strip)
        both.append(strip)
    return both


def packed_edges(first, second):
    part = first.shape[-1] // GROUPS
    place = lane_index(first.shape) % part
    moved = lane_roll(second, part // 2)
    to_right = jnp.where(place >= part // 2, first, moved)
    to_left = jnp.where(place < part // 2, first, moved)
    return to_right, to_left


def joined_strip(own, edge, index, halo):
    part = own.shape[-1] // GROUPS
    return jnp.where(halo, lane_roll(edge, -(index % 2) * (part // 2)), own)


def swap_sides(values, swapped):
    first, second = values
    return jnp.where(swapped, second, first), jnp.where(swapped, first, second)


def first_is_left():
    return lax.axis_index("tile") % 2 == 1


def swap_pairs(start, n_member, n_tile):
    pairs = []
    for member in range(n_member):
        for tile in range(n_tile):
            other = tile + 1 if (tile - start) % 2 == 0 else tile - 1
            if 0 <= other < n_tile:
                pairs.append((member * n_tile + tile, member * n_tile + other))
            elif n_member % 2 == 0:
                pairs.append((member * n_tile + tile, (member ^ 1) * n_tile + tile))
    return pairs


def without_partner(is_left, n_tile):
    tile = lax.axis_index("tile")
    return jnp.where(is_left, tile == 0, tile == n_tile - 1)


def total(terms):
    terms = list(terms)
    while len(terms) > 1:
        terms = [
            terms[i] + terms[i + 1] if i + 1 < len(terms) else terms[i]
            for i in range(0, len(terms), 2)
        ]
    return terms[0]


def around(planes, level, row, even_group=None):
    levels, rows = len(planes), len(planes[level])
    here = planes[level][row]
    terms = [lane_roll(here, 1), lane_roll(here, -1)]
    if row > 0:
        terms.append(planes[level][row - 1])
    if row < rows - 1:
        terms.append(planes[level][row + 1])
    elif even_group is not None:
        part = here.shape[-1] // GROUPS
        terms.append(jnp.where(even_group, lane_roll(here, -part), lane_roll(here, part)))
    if level > 0:
        terms.append(planes[level - 1][row])
    if level < levels - 1:
        terms.append(planes[level + 1][row])
    elif even_group is not None:
        terms.append(lane_roll(here, here.shape[-1] // 2))
    return total(terms)


def sweep(source, target, keep_at, square_at):
    levels, rows = source.shape[0], source.shape[1]
    planes = [[source[level, row] for row in range(rows)] for level in range(levels)]
    for level in range(levels):
        for row in range(rows):
            target[level, row] = keep_at(level, row) * planes[level][row] + square_at(
                level, row
            ) * around(planes, level, row)


def anchor_kernel(out_ref):
    out_ref[...] = jnp.zeros_like(out_ref)


def weigh_kernel(
    owner_ref,
    gathered_ref,
    pert_ref,
    coeff_ref,
    anchor_ref,
    field_ref,
    left_ref,
    right_ref,
    coeff_left_ref,
    coeff_right_ref,
    to_first_ref,
    to_second_ref,
    grad_ref,
):
    members, terms, _, lanes = pert_ref.shape
    levels, rows, _ = coeff_ref.shape
    slab_rows = gathered_ref.shape[2]
    strip_levels, strip_rows = left_ref.shape[:2]
    left_first = jnp.broadcast_to(first_is_left(), (8, lanes))
    for slab in range(rows // slab_rows):
        owner = owner_ref[slab]
        for term in range(terms):
            for inner in range(slab_rows):
                row = slab * slab_rows + inner
                grad_ref[pl.ds(term * levels * rows + row, levels, stride=rows), :] = gathered_ref[
                    owner, term, inner
                ]

    for start in range(0, levels * rows, BLOCK):
        block = pl.ds(start, BLOCK)
        coeff = jnp.concatenate([coeff_ref[l] for l in range(levels)], axis=0)[start : start + BLOCK]
        gradients = [
            coeff * grad_ref[pl.ds(term * levels * rows + start, BLOCK), :] for term in range(terms)
        ]
        for member in range(members):
            field_ref[pl.ds(start * members + member, BLOCK, stride=members), :] = total(
                pert_ref[member, term, block, :].astype(jnp.float32) * gradients[term]
                for term in range(terms)
            )

    pairs = strip_levels * strip_rows // 2
    fields, coeffs = [], []
    for level in range(strip_levels):
        for row in range(strip_rows):
            index = level * strip_rows + row
            cells = mirrors(level, row, levels, rows)
            field = own_strips(
                [field_ref[pl.ds((l * rows + r) * members, members), :] for l, r in cells]
            )
            coeff = own_strips([spread(coeff_ref[l, pl.ds(r, 1), :]) for l, r in cells])
            fields.append(field[0])
            coeffs.append(coeff[0])
            left_ref[level, row], right_ref[level, row] = field
            coeff_left_ref[pl.ds(index, 1), :] = coeff[0][0:1]
            coeff_right_ref[pl.ds(index, 1), :] = coeff[1][0:1]
    for pair in range(pairs):
        edges = packed_edges(fields[2 * pair], fields[2 * pair + 1])
        coeff_edges = packed_edges(coeffs[2 * pair], coeffs[2 * pair + 1])
        edges = swap_sides(edges, left_first)
        coeff_edges = swap_sides(coeff_edges, left_first)
        for ref, edge, coeff_edge in zip((to_first_ref, to_second_ref), edges, coeff_edges):
            ref[pl.ds(pair * members, members), :] = edge
            ref[pl.ds(pairs * members + pair, 1), :] = coeff_edge[0:1]


def interior_kernel(
    field_ref, coeff_ref, out_ref, other_ref, keep_ref, square_ref, inverse_ref
):
    levels, rows, members, lanes = field_ref.shape
    row_index = lax.broadcasted_iota(jnp.int32, (rows, lanes), 0)
    for level in range(levels):
        here = coeff_ref[level]
        beside = [
            lane_roll(here, 1),
            lane_roll(here, -1),
            jnp.where(row_index > 0, pltpu.roll(here, 1, 0), 0.0),
            jnp.where(row_index < rows - 1, pltpu.roll(here, rows - 1, 0), 0.0),
        ]
        if level > 0:
            beside.append(coeff_ref[level - 1])
        if level < levels - 1:
            beside.append(coeff_ref[level + 1])
        keep_ref[level] = 1.0 - here * total(beside)
        square_ref[level] = here * here
        inverse_ref[level] = 1.0 / here

    def keep_at(level, row):
        return keep_ref[level, pl.ds(row, 1), :]

    def square_at(level, row):
        return square_ref[level, pl.ds(row, 1), :]

    sweep(field_ref, other_ref, keep_at, square_at)
    sweep(other_ref, out_ref, keep_at, square_at)

    def pair(index, carry):
        sweep(out_ref, other_ref, keep_at, square_at)
        sweep(other_ref, out_ref, keep_at, square_at)
        return carry

    lax.fori_loop(0, SWEEPS // 2 - 1, pair, 0)
    for level in range(levels):
        for row in range(rows):
            out_ref[level, row] = out_ref[level, row] * inverse_ref[level, pl.ds(row, 1), :]


class Strips:
    def __init__(self, strip_ref, coeff_ref, edge_at, is_left, keep_ref, square_ref):
        self.levels, self.rows, self.members, lanes = strip_ref.shape
        self.coeff_ref, self.keep_ref, self.square_ref = coeff_ref, keep_ref, square_ref
        part = lanes // GROUPS
        pairs = self.levels * self.rows // 2
        shape = (self.members, lanes)
        self.even_group = group_index(shape, SWEEPS if is_left else part - SWEEPS) % 2 == 0
        place = lane_index(shape) % part
        halo = place >= part - SWEEPS if is_left else place < SWEEPS
        self.planes, coeffs = [], []
        for level in range(self.levels):
            plane, coeff_plane = [], []
            for row in range(self.rows):
                index = level * self.rows + row
                edge = edge_at(index // 2 * self.members, self.members)
                coeff_edge = spread(edge_at(pairs * self.members + index // 2, 1), self.members)
                plane.append(joined_strip(strip_ref[level, row], edge, index, halo))
                coeff_plane.append(joined_strip(self.own_coeff(level, row), coeff_edge, index, halo))
            self.planes.append(plane)
            coeffs.append(coeff_plane)
        for level in range(self.levels):
            for row in range(self.rows):
                here = coeffs[level][row]
                keep_ref[level, row] = 1.0 - here * around(coeffs, level, row, self.even_group)
                square_ref[level, row] = here * here

    def own_coeff(self, level, row):
        return spread(self.coeff_ref[pl.ds(level * self.rows + row, 1), :], self.members)

    def step(self):
        self.planes = [
            [
                self.keep_ref[level, row] * self.planes[level][row]
                + self.square_ref[level, row] * around(self.planes, level, row, self.even_group)
                for row in range(self.rows)
            ]
            for level in range(self.levels)
        ]

    def final(self, level, row):
        coeff = self.own_coeff(level, row)
        return self.planes[level][row] / jnp.where(coeff > 0.0, coeff, 1.0)


def finish_kernel(
    owner_ref,
    pert_ref,
    interior_ref,
    left_ref,
    right_ref,
    coeff_left_ref,
    coeff_right_ref,
    from_first_ref,
    from_second_ref,
    out_ref,
    local_ref,
    sum_ref,
    keep_left_ref,
    square_left_ref,
    keep_right_ref,
    square_right_ref,
):
    members, terms, _, lanes = pert_ref.shape
    levels, rows = interior_ref.shape[:2]
    slab_rows = out_ref.shape[2]
    part = lanes // GROUPS
    left_first = first_is_left()

    def edge_reader(is_left):
        outside = without_partner(is_left, lax.axis_size("tile"))

        def edge_at(place, count):
            first = from_first_ref[pl.ds(place, count), :]
            second = from_second_ref[pl.ds(place, count), :]
            edge = jnp.where(left_first == is_left, first, second)
            return jnp.where(outside, 0.0, edge)

        return edge_at

    left = Strips(
        left_ref, coeff_left_ref, edge_reader(True), True, keep_left_ref, square_left_ref
    )
    right = Strips(
        right_ref, coeff_right_ref, edge_reader(False), False, keep_right_ref, square_right_ref
    )
    for _ in range(SWEEPS):
        left.step()
        right.step()
    lane = lane_index((members, lanes))
    for level in range(left.levels):
        for row in range(left.rows):
            left_end, right_end = left.final(level, row), right.final(level, row)
            for g, (l, r) in enumerate(mirrors(level, row, levels, rows)):
                ends = jnp.where(
                    lane < lanes // 2,
                    lane_roll(left_end, -part * g),
                    lane_roll(right_end, -part * g),
                )
                local_ref[pl.ds((l * rows + r) * members, members), :] = jnp.where(
                    (lane < SWEEPS) | (lane >= lanes - SWEEPS), ends, interior_ref[l, r]
                )

    for start in range(0, levels * rows, BLOCK):
        block = pl.ds(start, BLOCK)
        fields = [
            local_ref[pl.ds(start * members + member, BLOCK, stride=members), :]
            for member in range(members)
        ]
        for term in range(terms):
            sum_ref[pl.ds(term * levels * rows + start, BLOCK), :] = total(
                pert_ref[member, term, block, :].astype(jnp.float32) * fields[member]
                for member in range(members)
            )
    for slab in range(rows // slab_rows):
        owner = owner_ref[slab]
        for term in range(terms):
            for inner in range(slab_rows):
                row = slab * slab_rows + inner
                out_ref[owner, term, inner] = sum_ref[
                    pl.ds(term * levels * rows + row, levels, stride=rows), :
                ]


def local_call(kernel, name, outs, scratch, operands, places, work):
    def shape_of(out):
        return out if isinstance(out, jax.ShapeDtypeStruct) else jax.ShapeDtypeStruct(out, jnp.float32)

    shapes = tuple(shape_of(out) for out in outs)
    specs = tuple(whole() for _ in outs)
    moved = sum(math.prod(x.shape) * x.dtype.itemsize for x in tuple(operands) + shapes)
    single = len(outs) == 1
    return pl.pallas_call(
        kernel,
        out_shape=shapes[0] if single else shapes,
        in_specs=[whole(place) for place in places],
        out_specs=specs[0] if single else specs,
        scratch_shapes=[
            pltpu.VMEM(item, jnp.float32) if isinstance(item, tuple) else item for item in scratch
        ],
        compiler_params=pltpu.CompilerParams(vmem_limit_bytes=VMEM_LIMIT),
        cost_estimate=pl.CostEstimate(flops=work, bytes_accessed=moved, transcendentals=0),
        name=name,
    )(*operands)


def body(perturbations, gradient_store, diffusivity, slab_owner):
    members, slots, variables, levels, rows, lanes = perturbations.shape
    terms = slots * variables
    n_member = lax.axis_size("member")
    n_tile = lax.axis_size("tile")
    slab_rows = gradient_store.shape[3]
    cells = levels * rows * lanes
    strip_levels, strip_rows = levels // 2, rows // 2
    strips = strip_levels * strip_rows
    wide_strip = (strip_levels, strip_rows, members, lanes)
    coeff_strip = (strips, lanes)
    wide_field = (levels, rows, members, lanes)
    flat_field = (levels * rows * members, lanes)
    field_coeff = (levels, rows, lanes)
    edge_shape = (strips // 2 * (members + 1), lanes)
    grad_shape = (terms * levels * rows, lanes)
    vmem, smem = pltpu.VMEM, pltpu.SMEM

    pert = perturbations.reshape(members, terms, levels * rows, lanes)
    slab = gradient_store.reshape(terms, levels, slab_rows, lanes).swapaxes(1, 2)
    anchor = local_call(anchor_kernel, "anchor", [(8, lanes)], [], (), (), ANCHOR_WORK)
    gathered = lax.all_gather(slab, "member", axis=0, tiled=False)

    field, left, right, coeff_left, coeff_right, to_first, to_second = local_call(
        weigh_kernel,
        "weigh",
        [flat_field, wide_strip, wide_strip, coeff_strip, coeff_strip, edge_shape, edge_shape],
        [grad_shape],
        (slab_owner, gathered, pert, diffusivity, anchor),
        (smem, vmem, vmem, vmem, vmem),
        2 * terms * members * cells,
    )
    from_first, from_second = (
        lax.ppermute(edges, ("member", "tile"), swap_pairs(start, n_member, n_tile))
        for start, edges in ((0, to_first), (1, to_second))
    )

    interior = local_call(
        interior_kernel,
        "interior",
        [wide_field],
        [wide_field, field_coeff, field_coeff, field_coeff],
        (field.reshape(wide_field), diffusivity),
        (vmem,) * 2,
        8 * SWEEPS * members * cells,
    )
    sums = local_call(
        finish_kernel,
        "finish",
        [(n_member, terms, slab_rows, levels, lanes)],
        [flat_field, grad_shape] + [wide_strip] * 4,
        (
            slab_owner,
            pert,
            interior,
            left,
            right,
            coeff_left,
            coeff_right,
            from_first,
            from_second,
        ),
        (smem,) + (vmem,) * 8,
        2 * terms * members * cells,
    )
    received = lax.all_to_all(sums, "member", 0, 0, tiled=True)
    norm_factor = 1.0 / (members * n_member - 1)
    owned = jnp.sum(received, axis=0) * norm_factor
    return owned.swapaxes(1, 2).reshape(slots, variables, levels, slab_rows, lanes)


def solution(mesh):
    in_specs = (
        P("member", None, None, None, None, "tile"),
        P(None, None, None, "member", "tile"),
        P(None, None, "tile"),
        P(),
    )
    out_specs = P(None, None, None, "member", "tile")
    return jax.shard_map(body, mesh=mesh, in_specs=in_specs, out_specs=out_specs, check_vma=False)
```

```python
import math

import jax
import jax.numpy as jnp
from jax import lax
from jax.experimental import pallas as pl
from jax.experimental.pallas import tpu as pltpu
from jax.sharding import PartitionSpec as P

SWEEPS = 10
GROUPS = 4
ANCHOR_WORK = 10**10
VMEM_LIMIT = 16 * 1024 * 1024


def lane_roll(value, shift):
    shift = shift % value.shape[-1]
    return value if shift == 0 else pltpu.roll(value, shift, 1)


def lane_index(shape):
    return lax.broadcasted_iota(jnp.int32, shape, 1)


def spread(row, rows=8):
    return jnp.broadcast_to(row, (rows, row.shape[-1]))


def whole(memory_space=pltpu.VMEM):
    return pl.BlockSpec(memory_space=memory_space)


def mirrors(level, row, levels, rows):
    return [
        (far_level, far_row)
        for far_level in (level, levels - 1 - level)
        for far_row in (row, rows - 1 - row)
    ]


def group_index(shape, start):
    part = shape[-1] // GROUPS
    return (lane_index(shape) + start) % shape[-1] // part


def own_strips(values):
    part = values[0].shape[-1] // GROUPS
    rolled = [lane_roll(value, part * g) for g, value in enumerate(values)]
    both = []
    for start in (SWEEPS, part - SWEEPS):
        group = group_index(values[0].shape, start)
        strip = rolled[0]
        for g in range(1, GROUPS):
            strip = jnp.where(group == g, rolled[g], strip)
        both.append(strip)
    return both


def packed_edges(first, second):
    part = first.shape[-1] // GROUPS
    place = lane_index(first.shape) % part
    moved = lane_roll(second, part // 2)
    to_right = jnp.where(place >= part // 2, first, moved)
    to_left = jnp.where(place < part // 2, first, moved)
    return to_right, to_left


def joined_strip(own, edge, index, halo):
    part = own.shape[-1] // GROUPS
    return jnp.where(halo, lane_roll(edge, -(index % 2) * (part // 2)), own)


def swap_sides(values, swapped):
    first, second = values
    return jnp.where(swapped, second, first), jnp.where(swapped, first, second)


def first_is_left():
    return lax.axis_index("tile") % 2 == 1


def swap_pairs(start, n_member, n_tile):
    pairs = []
    for member in range(n_member):
        for tile in range(n_tile):
            other = tile + 1 if (tile - start) % 2 == 0 else tile - 1
            if 0 <= other < n_tile:
                pairs.append((member * n_tile + tile, member * n_tile + other))
            elif n_member % 2 == 0:
                pairs.append((member * n_tile + tile, (member ^ 1) * n_tile + tile))
    return pairs


def without_partner(is_left, n_tile):
    tile = lax.axis_index("tile")
    return jnp.where(is_left, tile == 0, tile == n_tile - 1)


def total(terms):
    terms = list(terms)
    while len(terms) > 1:
        terms = [
            terms[i] + terms[i + 1] if i + 1 < len(terms) else terms[i]
            for i in range(0, len(terms), 2)
        ]
    return terms[0]


def around(planes, level, row, even_group=None):
    levels, rows = len(planes), len(planes[level])
    here = planes[level][row]
    terms = [lane_roll(here, 1), lane_roll(here, -1)]
    if row > 0:
        terms.append(planes[level][row - 1])
    if row < rows - 1:
        terms.append(planes[level][row + 1])
    elif even_group is not None:
        part = here.shape[-1] // GROUPS
        terms.append(jnp.where(even_group, lane_roll(here, -part), lane_roll(here, part)))
    if level > 0:
        terms.append(planes[level - 1][row])
    if level < levels - 1:
        terms.append(planes[level + 1][row])
    elif even_group is not None:
        terms.append(lane_roll(here, here.shape[-1] // 2))
    return total(terms)


def sweep(source, target, keep_at, square_at):
    levels, rows = source.shape[0], source.shape[1]
    planes = [[source[level, row] for row in range(rows)] for level in range(levels)]
    for level in range(levels):
        for row in range(rows):
            target[level, row] = keep_at(level, row) * planes[level][row] + square_at(
                level, row
            ) * around(planes, level, row)


def anchor_kernel(out_ref):
    out_ref[...] = jnp.zeros_like(out_ref)


def weigh_kernel(
    owner_ref,
    gathered_ref,
    pert_ref,
    coeff_ref,
    anchor_ref,
    field_ref,
    left_ref,
    right_ref,
    coeff_left_ref,
    coeff_right_ref,
    to_first_ref,
    to_second_ref,
    wide_ref,
    grad_ref,
):
    members, terms, levels, rows, lanes = pert_ref.shape
    slab_rows = gathered_ref.shape[2]
    strip_levels, strip_rows = left_ref.shape[:2]
    left_first = jnp.broadcast_to(first_is_left(), (8, lanes))
    for slab in range(rows // slab_rows):
        owner = owner_ref[slab]
        for term in range(terms):
            for inner in range(slab_rows):
                row = slab * slab_rows + inner
                grad_ref[pl.ds(term * levels * rows + row, levels, stride=rows), :] = gathered_ref[
                    owner, term, inner
                ]

    for level in range(levels):
        base = level * rows
        coeff = coeff_ref[level]
        gradients = [
            coeff * grad_ref[pl.ds(term * levels * rows + base, rows), :] for term in range(terms)
        ]
        for member in range(members):
            pieces = []
            for term in range(terms):
                wide = pert_ref[member, term, level].astype(jnp.float32)
                wide_ref[member, term, level] = wide
                pieces.append(wide * gradients[term])
            field_ref[pl.ds(base * members + member, rows, stride=members), :] = total(pieces)

    pairs = strip_levels * strip_rows // 2
    fields, coeffs = [], []
    for level in range(strip_levels):
        for row in range(strip_rows):
            index = level * strip_rows + row
            cells = mirrors(level, row, levels, rows)
            field = own_strips(
                [field_ref[pl.ds((l * rows + r) * members, members), :] for l, r in cells]
            )
            coeff = own_strips([spread(coeff_ref[l, pl.ds(r, 1), :]) for l, r in cells])
            fields.append(field[0])
            coeffs.append(coeff[0])
            left_ref[level, row], right_ref[level, row] = field
            coeff_left_ref[pl.ds(index, 1), :] = coeff[0][0:1]
            coeff_right_ref[pl.ds(index, 1), :] = coeff[1][0:1]
    for pair in range(pairs):
        edges = packed_edges(fields[2 * pair], fields[2 * pair + 1])
        coeff_edges = packed_edges(coeffs[2 * pair], coeffs[2 * pair + 1])
        edges = swap_sides(edges, left_first)
        coeff_edges = swap_sides(coeff_edges, left_first)
        for ref, edge, coeff_edge in zip((to_first_ref, to_second_ref), edges, coeff_edges):
            ref[pl.ds(pair * members, members), :] = edge
            ref[pl.ds(pairs * members + pair, 1), :] = coeff_edge[0:1]


def interior_kernel(
    field_ref, coeff_ref, out_ref, other_ref, keep_ref, square_ref, inverse_ref
):
    levels, rows, members, lanes = field_ref.shape
    row_index = lax.broadcasted_iota(jnp.int32, (rows, lanes), 0)
    for level in range(levels):
        here = coeff_ref[level]
        beside = [
            lane_roll(here, 1),
            lane_roll(here, -1),
            jnp.where(row_index > 0, pltpu.roll(here, 1, 0), 0.0),
            jnp.where(row_index < rows - 1, pltpu.roll(here, rows - 1, 0), 0.0),
        ]
        if level > 0:
            beside.append(coeff_ref[level - 1])
        if level < levels - 1:
            beside.append(coeff_ref[level + 1])
        keep_ref[level] = 1.0 - here * total(beside)
        square_ref[level] = here * here
        inverse_ref[level] = 1.0 / here

    def keep_at(level, row):
        return keep_ref[level, pl.ds(row, 1), :]

    def square_at(level, row):
        return square_ref[level, pl.ds(row, 1), :]

    sweep(field_ref, other_ref, keep_at, square_at)
    sweep(other_ref, out_ref, keep_at, square_at)

    def pair(index, carry):
        sweep(out_ref, other_ref, keep_at, square_at)
        sweep(other_ref, out_ref, keep_at, square_at)
        return carry

    lax.fori_loop(0, SWEEPS // 2 - 1, pair, 0)
    for level in range(levels):
        for row in range(rows):
            out_ref[level, row] = out_ref[level, row] * inverse_ref[level, pl.ds(row, 1), :]


class Strips:
    def __init__(self, strip_ref, coeff_ref, edge_at, is_left, keep_ref, square_ref):
        self.levels, self.rows, self.members, lanes = strip_ref.shape
        self.coeff_ref, self.keep_ref, self.square_ref = coeff_ref, keep_ref, square_ref
        part = lanes // GROUPS
        pairs = self.levels * self.rows // 2
        shape = (self.members, lanes)
        self.even_group = group_index(shape, SWEEPS if is_left else part - SWEEPS) % 2 == 0
        place = lane_index(shape) % part
        halo = place >= part - SWEEPS if is_left else place < SWEEPS
        self.planes, coeffs = [], []
        for level in range(self.levels):
            plane, coeff_plane = [], []
            for row in range(self.rows):
                index = level * self.rows + row
                edge = edge_at(index // 2 * self.members, self.members)
                coeff_edge = spread(edge_at(pairs * self.members + index // 2, 1), self.members)
                plane.append(joined_strip(strip_ref[level, row], edge, index, halo))
                coeff_plane.append(joined_strip(self.own_coeff(level, row), coeff_edge, index, halo))
            self.planes.append(plane)
            coeffs.append(coeff_plane)
        for level in range(self.levels):
            for row in range(self.rows):
                here = coeffs[level][row]
                keep_ref[level, row] = 1.0 - here * around(coeffs, level, row, self.even_group)
                square_ref[level, row] = here * here

    def own_coeff(self, level, row):
        return spread(self.coeff_ref[pl.ds(level * self.rows + row, 1), :], self.members)

    def step(self):
        self.planes = [
            [
                self.keep_ref[level, row] * self.planes[level][row]
                + self.square_ref[level, row] * around(self.planes, level, row, self.even_group)
                for row in range(self.rows)
            ]
            for level in range(self.levels)
        ]

    def final(self, level, row):
        coeff = self.own_coeff(level, row)
        return self.planes[level][row] / jnp.where(coeff > 0.0, coeff, 1.0)


def finish_kernel(
    owner_ref,
    pert_ref,
    interior_ref,
    left_ref,
    right_ref,
    coeff_left_ref,
    coeff_right_ref,
    from_first_ref,
    from_second_ref,
    out_ref,
    local_ref,
    sum_ref,
    keep_left_ref,
    square_left_ref,
    keep_right_ref,
    square_right_ref,
):
    members, terms, levels, rows, lanes = pert_ref.shape
    slab_rows = out_ref.shape[2]
    part = lanes // GROUPS
    left_first = first_is_left()

    def edge_reader(is_left):
        outside = without_partner(is_left, lax.axis_size("tile"))

        def edge_at(place, count):
            first = from_first_ref[pl.ds(place, count), :]
            second = from_second_ref[pl.ds(place, count), :]
            edge = jnp.where(left_first == is_left, first, second)
            return jnp.where(outside, 0.0, edge)

        return edge_at

    left = Strips(
        left_ref, coeff_left_ref, edge_reader(True), True, keep_left_ref, square_left_ref
    )
    right = Strips(
        right_ref, coeff_right_ref, edge_reader(False), False, keep_right_ref, square_right_ref
    )
    for _ in range(SWEEPS):
        left.step()
        right.step()
    lane = lane_index((members, lanes))
    for level in range(left.levels):
        for row in range(left.rows):
            left_end, right_end = left.final(level, row), right.final(level, row)
            for g, (l, r) in enumerate(mirrors(level, row, levels, rows)):
                ends = jnp.where(
                    lane < lanes // 2,
                    lane_roll(left_end, -part * g),
                    lane_roll(right_end, -part * g),
                )
                local_ref[pl.ds((l * rows + r) * members, members), :] = jnp.where(
                    (lane < SWEEPS) | (lane >= lanes - SWEEPS), ends, interior_ref[l, r]
                )

    for level in range(levels):
        base = level * rows
        fields = [
            local_ref[pl.ds(base * members + member, rows, stride=members), :]
            for member in range(members)
        ]
        for term in range(terms):
            sum_ref[pl.ds(term * levels * rows + base, rows), :] = total(
                pert_ref[member, term, level] * fields[member]
                for member in range(members)
            )
    for slab in range(rows // slab_rows):
        owner = owner_ref[slab]
        for term in range(terms):
            for inner in range(slab_rows):
                row = slab * slab_rows + inner
                out_ref[owner, term, inner] = sum_ref[
                    pl.ds(term * levels * rows + row, levels, stride=rows), :
                ]


def local_call(kernel, name, outs, scratch, operands, places, work):
    def shape_of(out):
        return out if isinstance(out, jax.ShapeDtypeStruct) else jax.ShapeDtypeStruct(out, jnp.float32)

    shapes = tuple(shape_of(out) for out in outs)
    specs = tuple(whole() for _ in outs)
    moved = sum(math.prod(x.shape) * x.dtype.itemsize for x in tuple(operands) + shapes)
    single = len(outs) == 1
    return pl.pallas_call(
        kernel,
        out_shape=shapes[0] if single else shapes,
        in_specs=[whole(place) for place in places],
        out_specs=specs[0] if single else specs,
        scratch_shapes=[
            pltpu.VMEM(item, jnp.float32) if isinstance(item, tuple) else item for item in scratch
        ],
        compiler_params=pltpu.CompilerParams(vmem_limit_bytes=VMEM_LIMIT),
        cost_estimate=pl.CostEstimate(flops=work, bytes_accessed=moved, transcendentals=0),
        name=name,
    )(*operands)


def body(perturbations, gradient_store, diffusivity, slab_owner):
    members, slots, variables, levels, rows, lanes = perturbations.shape
    terms = slots * variables
    n_member = lax.axis_size("member")
    n_tile = lax.axis_size("tile")
    slab_rows = gradient_store.shape[3]
    cells = levels * rows * lanes
    strip_levels, strip_rows = levels // 2, rows // 2
    strips = strip_levels * strip_rows
    wide_strip = (strip_levels, strip_rows, members, lanes)
    coeff_strip = (strips, lanes)
    wide_field = (levels, rows, members, lanes)
    flat_field = (levels * rows * members, lanes)
    field_coeff = (levels, rows, lanes)
    edge_shape = (strips // 2 * (members + 1), lanes)
    grad_shape = (terms * levels * rows, lanes)
    vmem, smem = pltpu.VMEM, pltpu.SMEM

    pert = perturbations.reshape(members, terms, levels, rows, lanes)
    slab = gradient_store.reshape(terms, levels, slab_rows, lanes).swapaxes(1, 2)
    anchor = local_call(anchor_kernel, "anchor", [(8, lanes)], [], (), (), ANCHOR_WORK)
    gathered = lax.all_gather(slab, "member", axis=0, tiled=False)

    field, left, right, coeff_left, coeff_right, to_first, to_second, wide = local_call(
        weigh_kernel,
        "weigh",
        [flat_field, wide_strip, wide_strip, coeff_strip, coeff_strip, edge_shape, edge_shape]
        + [pert.shape],
        [grad_shape],
        (slab_owner, gathered, pert, diffusivity, anchor),
        (smem, vmem, vmem, vmem, vmem),
        2 * terms * members * cells,
    )
    from_first, from_second = (
        lax.ppermute(edges, ("member", "tile"), swap_pairs(start, n_member, n_tile))
        for start, edges in ((0, to_first), (1, to_second))
    )

    interior = local_call(
        interior_kernel,
        "interior",
        [wide_field],
        [wide_field, field_coeff, field_coeff, field_coeff],
        (field.reshape(wide_field), diffusivity),
        (vmem,) * 2,
        8 * SWEEPS * members * cells,
    )
    sums = local_call(
        finish_kernel,
        "finish",
        [(n_member, terms, slab_rows, levels, lanes)],
        [flat_field, grad_shape] + [wide_strip] * 4,
        (
            slab_owner,
            wide,
            interior,
            left,
            right,
            coeff_left,
            coeff_right,
            from_first,
            from_second,
        ),
        (smem,) + (vmem,) * 8,
        2 * terms * members * cells,
    )
    received = lax.all_to_all(sums, "member", 0, 0, tiled=True)
    norm_factor = 1.0 / (members * n_member - 1)
    owned = jnp.sum(received, axis=0) * norm_factor
    return owned.swapaxes(1, 2).reshape(slots, variables, levels, slab_rows, lanes)


def solution(mesh):
    in_specs = (
        P("member", None, None, None, None, "tile"),
        P(None, None, None, "member", "tile"),
        P(None, None, "tile"),
        P(),
    )
    out_specs = P(None, None, None, "member", "tile")
    return jax.shard_map(body, mesh=mesh, in_specs=in_specs, out_specs=out_specs, check_vma=False)
```

```python
import math

import jax
import jax.numpy as jnp
from jax import lax
from jax.experimental import pallas as pl
from jax.experimental.pallas import tpu as pltpu
from jax.sharding import PartitionSpec as P

SWEEPS = 10
GROUPS = 4
ANCHOR_WORK = 10**10
VMEM_LIMIT = 16 * 1024 * 1024


def lane_roll(value, shift):
    shift = shift % value.shape[-1]
    return value if shift == 0 else pltpu.roll(value, shift, 1)


def lane_index(shape):
    return lax.broadcasted_iota(jnp.int32, shape, 1)


def spread(row, rows=8):
    return jnp.broadcast_to(row, (rows, row.shape[-1]))


def whole(memory_space=pltpu.VMEM):
    return pl.BlockSpec(memory_space=memory_space)


def mirrors(level, row, levels, rows):
    return [
        (far_level, far_row)
        for far_level in (level, levels - 1 - level)
        for far_row in (row, rows - 1 - row)
    ]


def group_index(shape, start):
    part = shape[-1] // GROUPS
    return (lane_index(shape) + start) % shape[-1] // part


def own_strips(values):
    part = values[0].shape[-1] // GROUPS
    rolled = [lane_roll(value, part * g) for g, value in enumerate(values)]
    both = []
    for start in (SWEEPS, part - SWEEPS):
        group = group_index(values[0].shape, start)
        strip = rolled[0]
        for g in range(1, GROUPS):
            strip = jnp.where(group == g, rolled[g], strip)
        both.append(strip)
    return both


def packed_edges(first, second):
    part = first.shape[-1] // GROUPS
    place = lane_index(first.shape) % part
    moved = lane_roll(second, part // 2)
    to_right = jnp.where(place >= part // 2, first, moved)
    to_left = jnp.where(place < part // 2, first, moved)
    return to_right, to_left


def joined_strip(own, edge, index, halo):
    part = own.shape[-1] // GROUPS
    return jnp.where(halo, lane_roll(edge, -(index % 2) * (part // 2)), own)


def swap_sides(values, swapped):
    first, second = values
    return jnp.where(swapped, second, first), jnp.where(swapped, first, second)


def first_is_left():
    return lax.axis_index("tile") % 2 == 1


def swap_pairs(start, n_member, n_tile):
    pairs = []
    for member in range(n_member):
        for tile in range(n_tile):
            other = tile + 1 if (tile - start) % 2 == 0 else tile - 1
            if 0 <= other < n_tile:
                pairs.append((member * n_tile + tile, member * n_tile + other))
            elif n_member % 2 == 0:
                pairs.append((member * n_tile + tile, (member ^ 1) * n_tile + tile))
    return pairs


def without_partner(is_left, n_tile):
    tile = lax.axis_index("tile")
    return jnp.where(is_left, tile == 0, tile == n_tile - 1)


def is_outer():
    tile = lax.axis_index("tile")
    return (tile == 0) | ((tile == lax.axis_size("tile") - 1) & first_is_left())


def early_is_left():
    return jnp.logical_xor(is_outer(), first_is_left())


def outer_lanes(shape, is_left):
    return (lane_index(shape) + jnp.where(is_left, 0, SWEEPS)) % shape[-1] < SWEEPS


def total(terms):
    terms = list(terms)
    while len(terms) > 1:
        terms = [
            terms[i] + terms[i + 1] if i + 1 < len(terms) else terms[i]
            for i in range(0, len(terms), 2)
        ]
    return terms[0]


def around(planes, level, row, even_group=None):
    levels, rows = len(planes), len(planes[level])
    here = planes[level][row]
    terms = [lane_roll(here, 1), lane_roll(here, -1)]
    if row > 0:
        terms.append(planes[level][row - 1])
    if row < rows - 1:
        terms.append(planes[level][row + 1])
    elif even_group is not None:
        part = here.shape[-1] // GROUPS
        terms.append(jnp.where(even_group, lane_roll(here, -part), lane_roll(here, part)))
    if level > 0:
        terms.append(planes[level - 1][row])
    if level < levels - 1:
        terms.append(planes[level + 1][row])
    elif even_group is not None:
        terms.append(lane_roll(here, here.shape[-1] // 2))
    return total(terms)


def sweep(source, target, keep_at, square_at):
    levels, rows = source.shape[0], source.shape[1]
    planes = [[source[level, row] for row in range(rows)] for level in range(levels)]
    for level in range(levels):
        for row in range(rows):
            target[level, row] = keep_at(level, row) * planes[level][row] + square_at(
                level, row
            ) * around(planes, level, row)


def anchor_kernel(out_ref):
    out_ref[...] = jnp.zeros_like(out_ref)


def weigh_kernel(
    owner_ref,
    gathered_ref,
    pert_ref,
    coeff_ref,
    anchor_ref,
    field_ref,
    left_ref,
    right_ref,
    coeff_left_ref,
    coeff_right_ref,
    to_first_ref,
    to_second_ref,
    grad_ref,
):
    members, terms, levels, rows, lanes = pert_ref.shape
    slab_rows = gathered_ref.shape[2]
    strip_levels, strip_rows = left_ref.shape[:2]
    left_first = jnp.broadcast_to(first_is_left(), (8, lanes))
    for slab in range(rows // slab_rows):
        owner = owner_ref[slab]
        for term in range(terms):
            for inner in range(slab_rows):
                row = slab * slab_rows + inner
                grad_ref[pl.ds(term * levels * rows + row, levels, stride=rows), :] = gathered_ref[
                    owner, term, inner
                ]

    for level in range(levels):
        base = level * rows
        coeff = coeff_ref[level]
        gradients = [
            coeff * grad_ref[pl.ds(term * levels * rows + base, rows), :] for term in range(terms)
        ]
        for member in range(members):
            field_ref[pl.ds(base * members + member, rows, stride=members), :] = total(
                pert_ref[member, term, level].astype(jnp.float32) * gradients[term]
                for term in range(terms)
            )

    pairs = strip_levels * strip_rows // 2
    fields, coeffs = [], []
    for level in range(strip_levels):
        for row in range(strip_rows):
            index = level * strip_rows + row
            cells = mirrors(level, row, levels, rows)
            field = own_strips(
                [field_ref[pl.ds((l * rows + r) * members, members), :] for l, r in cells]
            )
            coeff = own_strips([spread(coeff_ref[l, pl.ds(r, 1), :]) for l, r in cells])
            fields.append(field[0])
            coeffs.append(coeff[0])
            left_ref[level, row], right_ref[level, row] = field
            coeff_left_ref[pl.ds(index, 1), :] = coeff[0][0:1]
            coeff_right_ref[pl.ds(index, 1), :] = coeff[1][0:1]
    for pair in range(pairs):
        edges = packed_edges(fields[2 * pair], fields[2 * pair + 1])
        coeff_edges = packed_edges(coeffs[2 * pair], coeffs[2 * pair + 1])
        edges = swap_sides(edges, left_first)
        coeff_edges = swap_sides(coeff_edges, left_first)
        for ref, edge, coeff_edge in zip((to_first_ref, to_second_ref), edges, coeff_edges):
            ref[pl.ds(pair * members, members), :] = edge
            ref[pl.ds(pairs * members + pair, 1), :] = coeff_edge[0:1]


def interior_kernel(
    field_ref,
    coeff_ref,
    left_ref,
    right_ref,
    coeff_left_ref,
    coeff_right_ref,
    out_ref,
    outer_ref,
    other_ref,
    keep_ref,
    square_ref,
    strip_keep_ref,
    strip_square_ref,
):
    levels, rows, members, lanes = field_ref.shape
    row_index = lax.broadcasted_iota(jnp.int32, (rows, lanes), 0)
    for level in range(levels):
        here = coeff_ref[level]
        beside = [
            lane_roll(here, 1),
            lane_roll(here, -1),
            jnp.where(row_index > 0, pltpu.roll(here, 1, 0), 0.0),
            jnp.where(row_index < rows - 1, pltpu.roll(here, rows - 1, 0), 0.0),
        ]
        if level > 0:
            beside.append(coeff_ref[level - 1])
        if level < levels - 1:
            beside.append(coeff_ref[level + 1])
        keep = 1.0 - here * total(beside)
        square = here * here
        for row in range(rows):
            keep_ref[level, row] = spread(keep[row : row + 1], members)
            square_ref[level, row] = spread(square[row : row + 1], members)

    def keep_at(level, row):
        return keep_ref[level, row]

    def square_at(level, row):
        return square_ref[level, row]

    sweep(field_ref, other_ref, keep_at, square_at)
    sweep(other_ref, out_ref, keep_at, square_at)

    def pair(index, carry):
        sweep(out_ref, other_ref, keep_at, square_at)
        sweep(other_ref, out_ref, keep_at, square_at)
        return carry

    lax.fori_loop(0, SWEEPS // 2 - 1, pair, 0)
    for level in range(levels):
        inverse = 1.0 / coeff_ref[level]
        for row in range(rows):
            out_ref[level, row] = out_ref[level, row] * spread(inverse[row : row + 1], members)

    @pl.when(is_outer())
    def _():
        strips = left_ref, right_ref, coeff_left_ref, coeff_right_ref
        edge_at = lambda place, count: jnp.zeros((count, lanes), jnp.float32)
        planes = swept_strips(strips, edge_at, early_is_left(), strip_keep_ref, strip_square_ref)
        store_planes(outer_ref, planes)


def swept_strips(strips, edge_at, is_left, keep_ref, square_ref):
    left_ref, right_ref, coeff_left_ref, coeff_right_ref = strips
    levels, rows, members, lanes = left_ref.shape
    outside = without_partner(is_left, lax.axis_size("tile"))
    part = lanes // GROUPS
    pairs = levels * rows // 2
    lane = lane_index((members, lanes))
    even_group = (lane + jnp.where(is_left, SWEEPS, part - SWEEPS)) // part % 2 == 0
    halo = (lane + jnp.where(is_left, SWEEPS, 0)) % part < SWEEPS

    def own_coeff(level, row):
        place = pl.ds(level * rows + row, 1)
        return spread(jnp.where(is_left, coeff_left_ref[place, :], coeff_right_ref[place, :]), members)

    planes, coeffs = [], []
    for level in range(levels):
        plane, coeff_plane = [], []
        for row in range(rows):
            index = level * rows + row
            edge = jnp.where(outside, 0.0, edge_at(index // 2 * members, members))
            coeff_edge = jnp.where(outside, 0.0, edge_at(pairs * members + index // 2, 1))
            own = jnp.where(is_left, left_ref[level, row], right_ref[level, row])
            plane.append(joined_strip(own, edge, index, halo))
            coeff_plane.append(
                joined_strip(own_coeff(level, row), spread(coeff_edge, members), index, halo)
            )
        planes.append(plane)
        coeffs.append(coeff_plane)
    for level in range(levels):
        for row in range(rows):
            here = coeffs[level][row]
            keep_ref[level, row] = 1.0 - here * around(coeffs, level, row, even_group)
            square_ref[level, row] = here * here
    for _ in range(SWEEPS):
        planes = [
            [
                keep_ref[level, row] * planes[level][row]
                + square_ref[level, row] * around(planes, level, row, even_group)
                for row in range(rows)
            ]
            for level in range(levels)
        ]
    for level in range(levels):
        for row in range(rows):
            coeff = own_coeff(level, row)
            planes[level][row] = planes[level][row] / jnp.where(coeff > 0.0, coeff, 1.0)
    return planes


def store_planes(ref, planes):
    for level, plane in enumerate(planes):
        for row, value in enumerate(plane):
            ref[level, row] = value


def early_kernel(
    interior_ref,
    outer_ref,
    left_ref,
    right_ref,
    coeff_left_ref,
    coeff_right_ref,
    edge_ref,
    out_ref,
    swept_ref,
    keep_ref,
    square_ref,
):
    levels, rows, members, lanes = interior_ref.shape
    part = lanes // GROUPS
    is_left = early_is_left()

    @pl.when(is_outer())
    def _():
        swept_ref[...] = outer_ref[...]

    @pl.when(jnp.logical_not(is_outer()))
    def _():
        strips = left_ref, right_ref, coeff_left_ref, coeff_right_ref
        edge_at = lambda place, count: edge_ref[pl.ds(place, count), :]
        store_planes(swept_ref, swept_strips(strips, edge_at, is_left, keep_ref, square_ref))

    ends = outer_lanes((members, lanes), is_left)
    for level in range(swept_ref.shape[0]):
        for row in range(swept_ref.shape[1]):
            final = swept_ref[level, row]
            for g, (l, r) in enumerate(mirrors(level, row, levels, rows)):
                out_ref[l, r] = jnp.where(ends, lane_roll(final, -part * g), interior_ref[l, r])


def finish_kernel(
    owner_ref,
    pert_ref,
    partial_ref,
    left_ref,
    right_ref,
    coeff_left_ref,
    coeff_right_ref,
    from_first_ref,
    from_second_ref,
    out_ref,
    local_ref,
    sum_ref,
    keep_ref,
    square_ref,
):
    members, terms, levels, rows, lanes = pert_ref.shape
    slab_rows = out_ref.shape[2]
    part = lanes // GROUPS
    is_left = jnp.logical_not(early_is_left())
    outer = is_outer()

    def edge_at(place, count):
        place = pl.ds(place, count)
        return jnp.where(outer, from_first_ref[place, :], from_second_ref[place, :])

    strips = left_ref, right_ref, coeff_left_ref, coeff_right_ref
    planes = swept_strips(strips, edge_at, is_left, keep_ref, square_ref)
    ends = outer_lanes((members, lanes), is_left)
    for level, plane in enumerate(planes):
        for row, final in enumerate(plane):
            for g, (l, r) in enumerate(mirrors(level, row, levels, rows)):
                local_ref[pl.ds((l * rows + r) * members, members), :] = jnp.where(
                    ends, lane_roll(final, -part * g), partial_ref[l, r]
                )

    for level in range(levels):
        base = level * rows
        fields = [
            local_ref[pl.ds(base * members + member, rows, stride=members), :]
            for member in range(members)
        ]
        for term in range(terms):
            sum_ref[pl.ds(term * levels * rows + base, rows), :] = total(
                pert_ref[member, term, level].astype(jnp.float32) * fields[member]
                for member in range(members)
            )
    for slab in range(rows // slab_rows):
        owner = owner_ref[slab]
        for term in range(terms):
            for inner in range(slab_rows):
                row = slab * slab_rows + inner
                out_ref[owner, term, inner] = sum_ref[
                    pl.ds(term * levels * rows + row, levels, stride=rows), :
                ]


def local_call(kernel, name, outs, scratch, operands, places, work):
    def shape_of(out):
        return out if isinstance(out, jax.ShapeDtypeStruct) else jax.ShapeDtypeStruct(out, jnp.float32)

    shapes = tuple(shape_of(out) for out in outs)
    specs = tuple(whole() for _ in outs)
    moved = sum(math.prod(x.shape) * x.dtype.itemsize for x in tuple(operands) + shapes)
    single = len(outs) == 1
    return pl.pallas_call(
        kernel,
        out_shape=shapes[0] if single else shapes,
        in_specs=[whole(place) for place in places],
        out_specs=specs[0] if single else specs,
        scratch_shapes=[
            pltpu.VMEM(item, jnp.float32) if isinstance(item, tuple) else item for item in scratch
        ],
        compiler_params=pltpu.CompilerParams(vmem_limit_bytes=VMEM_LIMIT),
        cost_estimate=pl.CostEstimate(flops=work, bytes_accessed=moved, transcendentals=0),
        name=name,
    )(*operands)


def body(perturbations, gradient_store, diffusivity, slab_owner):
    members, slots, variables, levels, rows, lanes = perturbations.shape
    terms = slots * variables
    n_member = lax.axis_size("member")
    n_tile = lax.axis_size("tile")
    slab_rows = gradient_store.shape[3]
    cells = levels * rows * lanes
    strip_levels, strip_rows = levels // 2, rows // 2
    strips = strip_levels * strip_rows
    wide_strip = (strip_levels, strip_rows, members, lanes)
    coeff_strip = (strips, lanes)
    wide_field = (levels, rows, members, lanes)
    flat_field = (levels * rows * members, lanes)
    field_coeff = (levels, rows, lanes)
    edge_shape = (strips // 2 * (members + 1), lanes)
    grad_shape = (terms * levels * rows, lanes)
    vmem, smem = pltpu.VMEM, pltpu.SMEM

    pert = perturbations.reshape(members, terms, levels, rows, lanes)
    slab = gradient_store.reshape(terms, levels, slab_rows, lanes).swapaxes(1, 2)
    anchor = local_call(anchor_kernel, "anchor", [(8, lanes)], [], (), (), ANCHOR_WORK)
    gathered = lax.all_gather(slab, "member", axis=0, tiled=False)

    field, left, right, coeff_left, coeff_right, to_first, to_second = local_call(
        weigh_kernel,
        "weigh",
        [flat_field, wide_strip, wide_strip, coeff_strip, coeff_strip, edge_shape, edge_shape],
        [grad_shape],
        (slab_owner, gathered, pert, diffusivity, anchor),
        (smem, vmem, vmem, vmem, vmem),
        2 * terms * members * cells,
    )
    from_first, from_second = (
        lax.ppermute(edges, ("member", "tile"), swap_pairs(start, n_member, n_tile))
        for start, edges in ((0, to_first), (1, to_second))
    )

    strips = (left, right, coeff_left, coeff_right)
    interior, outer = local_call(
        interior_kernel,
        "interior",
        [wide_field, wide_strip],
        [wide_field] * 3 + [wide_strip] * 2,
        (field.reshape(wide_field), diffusivity) + strips,
        (vmem,) * 6,
        8 * SWEEPS * members * cells,
    )
    partial = local_call(
        early_kernel,
        "early_strips",
        [wide_field],
        [wide_strip] * 3,
        (interior, outer) + strips + (from_first,),
        (vmem,) * 7,
        2 * SWEEPS * members * cells,
    )
    sums = local_call(
        finish_kernel,
        "finish",
        [(n_member, terms, slab_rows, levels, lanes)],
        [flat_field, grad_shape] + [wide_strip] * 2,
        (slab_owner, pert, partial) + strips + (from_first, from_second),
        (smem,) + (vmem,) * 8,
        2 * terms * members * cells,
    )
    received = lax.all_to_all(sums, "member", 0, 0, tiled=True)
    norm_factor = 1.0 / (members * n_member - 1)
    owned = jnp.sum(received, axis=0) * norm_factor
    return owned.swapaxes(1, 2).reshape(slots, variables, levels, slab_rows, lanes)


def solution(mesh):
    in_specs = (
        P("member", None, None, None, None, "tile"),
        P(None, None, None, "member", "tile"),
        P(None, None, "tile"),
        P(),
    )
    out_specs = P(None, None, None, "member", "tile")
    return jax.shard_map(body, mesh=mesh, in_specs=in_specs, out_specs=out_specs, check_vma=False)
```

```python
import math

import jax
import jax.numpy as jnp
from jax import lax
from jax.experimental import pallas as pl
from jax.experimental.pallas import tpu as pltpu
from jax.sharding import PartitionSpec as P

SWEEPS = 10
GROUPS = 4
ANCHOR_WORK = 10**10
VMEM_LIMIT = 16 * 1024 * 1024


def lane_roll(value, shift):
    shift = shift % value.shape[-1]
    return value if shift == 0 else pltpu.roll(value, shift, 1)


def lane_index(shape):
    return lax.broadcasted_iota(jnp.int32, shape, 1)


def spread(row, rows=8):
    return jnp.broadcast_to(row, (rows, row.shape[-1]))


def whole(memory_space=pltpu.VMEM):
    return pl.BlockSpec(memory_space=memory_space)


def mirrors(level, row, levels, rows):
    return [
        (far_level, far_row)
        for far_level in (level, levels - 1 - level)
        for far_row in (row, rows - 1 - row)
    ]


def group_index(shape, start):
    part = shape[-1] // GROUPS
    return (lane_index(shape) + start) % shape[-1] // part


def own_strips(values):
    part = values[0].shape[-1] // GROUPS
    rolled = [lane_roll(value, part * g) for g, value in enumerate(values)]
    both = []
    for start in (SWEEPS, part - SWEEPS):
        group = group_index(values[0].shape, start)
        strip = rolled[0]
        for g in range(1, GROUPS):
            strip = jnp.where(group == g, rolled[g], strip)
        both.append(strip)
    return both


def packed_edges(first, second):
    part = first.shape[-1] // GROUPS
    place = lane_index(first.shape) % part
    moved = lane_roll(second, part // 2)
    to_right = jnp.where(place >= part // 2, first, moved)
    to_left = jnp.where(place < part // 2, first, moved)
    return to_right, to_left


def joined_strip(own, edge, index, halo):
    part = own.shape[-1] // GROUPS
    return jnp.where(halo, lane_roll(edge, -(index % 2) * (part // 2)), own)


def swap_sides(values, swapped):
    first, second = values
    return jnp.where(swapped, second, first), jnp.where(swapped, first, second)


def first_is_left():
    return lax.axis_index("tile") % 2 == 1


def swap_pairs(start, n_member, n_tile):
    pairs = []
    for member in range(n_member):
        for tile in range(n_tile):
            other = tile + 1 if (tile - start) % 2 == 0 else tile - 1
            if 0 <= other < n_tile:
                pairs.append((member * n_tile + tile, member * n_tile + other))
            elif n_member % 2 == 0:
                pairs.append((member * n_tile + tile, (member ^ 1) * n_tile + tile))
    return pairs


def without_partner(is_left, n_tile):
    tile = lax.axis_index("tile")
    return jnp.where(is_left, tile == 0, tile == n_tile - 1)


def exchanged(values):
    return jnp.swapaxes(jnp.stack(values, axis=0), 0, 1)


def total(terms):
    terms = list(terms)
    while len(terms) > 1:
        terms = [
            terms[i] + terms[i + 1] if i + 1 < len(terms) else terms[i]
            for i in range(0, len(terms), 2)
        ]
    return terms[0]


def around(planes, level, row, even_group=None):
    levels, rows = len(planes), len(planes[level])
    here = planes[level][row]
    terms = [lane_roll(here, 1), lane_roll(here, -1)]
    if row > 0:
        terms.append(planes[level][row - 1])
    if row < rows - 1:
        terms.append(planes[level][row + 1])
    elif even_group is not None:
        part = here.shape[-1] // GROUPS
        terms.append(jnp.where(even_group, lane_roll(here, -part), lane_roll(here, part)))
    if level > 0:
        terms.append(planes[level - 1][row])
    if level < levels - 1:
        terms.append(planes[level + 1][row])
    elif even_group is not None:
        terms.append(lane_roll(here, here.shape[-1] // 2))
    return total(terms)


def sweep(source, target, keep_at, square_at):
    levels, rows = source.shape[0], source.shape[1]
    planes = [[source[level, row] for row in range(rows)] for level in range(levels)]
    for level in range(levels):
        for row in range(rows):
            target[level, row] = keep_at(level, row) * planes[level][row] + square_at(
                level, row
            ) * around(planes, level, row)


def anchor_kernel(out_ref):
    out_ref[...] = jnp.zeros_like(out_ref)


def weigh_kernel(
    owner_ref,
    gathered_ref,
    pert_ref,
    coeff_ref,
    anchor_ref,
    field_ref,
    left_ref,
    right_ref,
    coeff_left_ref,
    coeff_right_ref,
    to_first_ref,
    to_second_ref,
    grad_ref,
):
    members, terms, levels, rows, lanes = pert_ref.shape
    slab_rows = gathered_ref.shape[2]
    strip_levels, strip_rows = left_ref.shape[:2]
    left_first = jnp.broadcast_to(first_is_left(), (8, lanes))
    owners = [owner_ref[slab] for slab in range(rows // slab_rows)]
    for term in range(terms):
        found = [gathered_ref[owner, term, inner] for owner in owners for inner in range(slab_rows)]
        grad_ref[term] = exchanged(found)

    for level in range(levels):
        coeff = coeff_ref[level]
        gradients = [coeff * grad_ref[term, level] for term in range(terms)]
        field_ref[level] = exchanged(
            [
                total(
                    pert_ref[member, term, level].astype(jnp.float32) * gradients[term]
                    for term in range(terms)
                )
                for member in range(members)
            ]
        )

    pairs = strip_levels * strip_rows // 2
    fields, coeffs = [], []
    for level in range(strip_levels):
        for row in range(strip_rows):
            index = level * strip_rows + row
            cells = mirrors(level, row, levels, rows)
            field = own_strips(
                [field_ref[l, r] for l, r in cells]
            )
            coeff = own_strips([spread(coeff_ref[l, pl.ds(r, 1), :]) for l, r in cells])
            fields.append(field[0])
            coeffs.append(coeff[0])
            left_ref[level, row], right_ref[level, row] = field
            coeff_left_ref[pl.ds(index, 1), :] = coeff[0][0:1]
            coeff_right_ref[pl.ds(index, 1), :] = coeff[1][0:1]
    for pair in range(pairs):
        edges = packed_edges(fields[2 * pair], fields[2 * pair + 1])
        coeff_edges = packed_edges(coeffs[2 * pair], coeffs[2 * pair + 1])
        edges = swap_sides(edges, left_first)
        coeff_edges = swap_sides(coeff_edges, left_first)
        for ref, edge, coeff_edge in zip((to_first_ref, to_second_ref), edges, coeff_edges):
            ref[pl.ds(pair * members, members), :] = edge
            ref[pl.ds(pairs * members + pair, 1), :] = coeff_edge[0:1]


def interior_kernel(
    field_ref, coeff_ref, out_ref, other_ref, keep_ref, square_ref, inverse_ref
):
    levels, rows, members, lanes = field_ref.shape
    row_index = lax.broadcasted_iota(jnp.int32, (rows, lanes), 0)
    for level in range(levels):
        here = coeff_ref[level]
        beside = [
            lane_roll(here, 1),
            lane_roll(here, -1),
            jnp.where(row_index > 0, pltpu.roll(here, 1, 0), 0.0),
            jnp.where(row_index < rows - 1, pltpu.roll(here, rows - 1, 0), 0.0),
        ]
        if level > 0:
            beside.append(coeff_ref[level - 1])
        if level < levels - 1:
            beside.append(coeff_ref[level + 1])
        keep_ref[level] = 1.0 - here * total(beside)
        square_ref[level] = here * here
        inverse_ref[level] = 1.0 / here

    def keep_at(level, row):
        return keep_ref[level, pl.ds(row, 1), :]

    def square_at(level, row):
        return square_ref[level, pl.ds(row, 1), :]

    sweep(field_ref, other_ref, keep_at, square_at)
    sweep(other_ref, out_ref, keep_at, square_at)

    def pair(index, carry):
        sweep(out_ref, other_ref, keep_at, square_at)
        sweep(other_ref, out_ref, keep_at, square_at)
        return carry

    lax.fori_loop(0, SWEEPS // 2 - 1, pair, 0)
    for level in range(levels):
        for row in range(rows):
            out_ref[level, row] = out_ref[level, row] * inverse_ref[level, pl.ds(row, 1), :]


class Strips:
    def __init__(self, strip_ref, coeff_ref, edge_at, is_left, keep_ref, square_ref):
        self.levels, self.rows, self.members, lanes = strip_ref.shape
        self.coeff_ref, self.keep_ref, self.square_ref = coeff_ref, keep_ref, square_ref
        part = lanes // GROUPS
        pairs = self.levels * self.rows // 2
        shape = (self.members, lanes)
        self.even_group = group_index(shape, SWEEPS if is_left else part - SWEEPS) % 2 == 0
        place = lane_index(shape) % part
        halo = place >= part - SWEEPS if is_left else place < SWEEPS
        self.planes, coeffs = [], []
        for level in range(self.levels):
            plane, coeff_plane = [], []
            for row in range(self.rows):
                index = level * self.rows + row
                edge = edge_at(index // 2 * self.members, self.members)
                coeff_edge = spread(edge_at(pairs * self.members + index // 2, 1), self.members)
                plane.append(joined_strip(strip_ref[level, row], edge, index, halo))
                coeff_plane.append(joined_strip(self.own_coeff(level, row), coeff_edge, index, halo))
            self.planes.append(plane)
            coeffs.append(coeff_plane)
        for level in range(self.levels):
            for row in range(self.rows):
                here = coeffs[level][row]
                keep_ref[level, row] = 1.0 - here * around(coeffs, level, row, self.even_group)
                square_ref[level, row] = here * here

    def own_coeff(self, level, row):
        return spread(self.coeff_ref[pl.ds(level * self.rows + row, 1), :], self.members)

    def step(self):
        self.planes = [
            [
                self.keep_ref[level, row] * self.planes[level][row]
                + self.square_ref[level, row] * around(self.planes, level, row, self.even_group)
                for row in range(self.rows)
            ]
            for level in range(self.levels)
        ]

    def final(self, level, row):
        coeff = self.own_coeff(level, row)
        return self.planes[level][row] / jnp.where(coeff > 0.0, coeff, 1.0)


def finish_kernel(
    owner_ref,
    pert_ref,
    interior_ref,
    left_ref,
    right_ref,
    coeff_left_ref,
    coeff_right_ref,
    from_first_ref,
    from_second_ref,
    out_ref,
    local_ref,
    sum_ref,
    keep_left_ref,
    square_left_ref,
    keep_right_ref,
    square_right_ref,
):
    members, terms, levels, rows, lanes = pert_ref.shape
    slab_rows = out_ref.shape[2]
    part = lanes // GROUPS
    left_first = first_is_left()

    def edge_reader(is_left):
        outside = without_partner(is_left, lax.axis_size("tile"))

        def edge_at(place, count):
            first = from_first_ref[pl.ds(place, count), :]
            second = from_second_ref[pl.ds(place, count), :]
            edge = jnp.where(left_first == is_left, first, second)
            return jnp.where(outside, 0.0, edge)

        return edge_at

    left = Strips(
        left_ref, coeff_left_ref, edge_reader(True), True, keep_left_ref, square_left_ref
    )
    right = Strips(
        right_ref, coeff_right_ref, edge_reader(False), False, keep_right_ref, square_right_ref
    )
    for _ in range(SWEEPS):
        left.step()
        right.step()
    lane = lane_index((members, lanes))
    for level in range(left.levels):
        for row in range(left.rows):
            left_end, right_end = left.final(level, row), right.final(level, row)
            for g, (l, r) in enumerate(mirrors(level, row, levels, rows)):
                ends = jnp.where(
                    lane < lanes // 2,
                    lane_roll(left_end, -part * g),
                    lane_roll(right_end, -part * g),
                )
                local_ref[l, r] = jnp.where(
                    (lane < SWEEPS) | (lane >= lanes - SWEEPS), ends, interior_ref[l, r]
                )

    for level in range(levels):
        fields = exchanged([local_ref[level, row] for row in range(rows)])
        for term in range(terms):
            sum_ref[term, level] = total(
                pert_ref[member, term, level].astype(jnp.float32) * fields[member]
                for member in range(members)
            )
    owners = [owner_ref[slab] for slab in range(rows // slab_rows)]
    for term in range(terms):
        found = exchanged([sum_ref[term, level] for level in range(levels)])
        for slab, owner in enumerate(owners):
            for inner in range(slab_rows):
                out_ref[owner, term, inner] = found[slab * slab_rows + inner]


def local_call(kernel, name, outs, scratch, operands, places, work):
    def shape_of(out):
        return out if isinstance(out, jax.ShapeDtypeStruct) else jax.ShapeDtypeStruct(out, jnp.float32)

    shapes = tuple(shape_of(out) for out in outs)
    specs = tuple(whole() for _ in outs)
    moved = sum(math.prod(x.shape) * x.dtype.itemsize for x in tuple(operands) + shapes)
    single = len(outs) == 1
    return pl.pallas_call(
        kernel,
        out_shape=shapes[0] if single else shapes,
        in_specs=[whole(place) for place in places],
        out_specs=specs[0] if single else specs,
        scratch_shapes=[
            pltpu.VMEM(item, jnp.float32) if isinstance(item, tuple) else item for item in scratch
        ],
        compiler_params=pltpu.CompilerParams(vmem_limit_bytes=VMEM_LIMIT),
        cost_estimate=pl.CostEstimate(flops=work, bytes_accessed=moved, transcendentals=0),
        name=name,
    )(*operands)


def body(perturbations, gradient_store, diffusivity, slab_owner):
    members, slots, variables, levels, rows, lanes = perturbations.shape
    terms = slots * variables
    n_member = lax.axis_size("member")
    n_tile = lax.axis_size("tile")
    slab_rows = gradient_store.shape[3]
    cells = levels * rows * lanes
    strip_levels, strip_rows = levels // 2, rows // 2
    strips = strip_levels * strip_rows
    wide_strip = (strip_levels, strip_rows, members, lanes)
    coeff_strip = (strips, lanes)
    wide_field = (levels, rows, members, lanes)
    field_coeff = (levels, rows, lanes)
    edge_shape = (strips // 2 * (members + 1), lanes)
    grad_shape = (terms, levels, rows, lanes)
    vmem, smem = pltpu.VMEM, pltpu.SMEM

    pert = perturbations.reshape(members, terms, levels, rows, lanes)
    slab = gradient_store.reshape(terms, levels, slab_rows, lanes).swapaxes(1, 2)
    anchor = local_call(anchor_kernel, "anchor", [(8, lanes)], [], (), (), ANCHOR_WORK)
    gathered = lax.all_gather(slab, "member", axis=0, tiled=False)

    field, left, right, coeff_left, coeff_right, to_first, to_second = local_call(
        weigh_kernel,
        "weigh",
        [wide_field, wide_strip, wide_strip, coeff_strip, coeff_strip, edge_shape, edge_shape],
        [grad_shape],
        (slab_owner, gathered, pert, diffusivity, anchor),
        (smem, vmem, vmem, vmem, vmem),
        2 * terms * members * cells,
    )
    from_first, from_second = (
        lax.ppermute(edges, ("member", "tile"), swap_pairs(start, n_member, n_tile))
        for start, edges in ((0, to_first), (1, to_second))
    )

    interior = local_call(
        interior_kernel,
        "interior",
        [wide_field],
        [wide_field, field_coeff, field_coeff, field_coeff],
        (field, diffusivity),
        (vmem,) * 2,
        8 * SWEEPS * members * cells,
    )
    sums = local_call(
        finish_kernel,
        "finish",
        [(n_member, terms, slab_rows, levels, lanes)],
        [wide_field, grad_shape] + [wide_strip] * 4,
        (
            slab_owner,
            pert,
            interior,
            left,
            right,
            coeff_left,
            coeff_right,
            from_first,
            from_second,
        ),
        (smem,) + (vmem,) * 8,
        2 * terms * members * cells,
    )
    received = lax.all_to_all(sums, "member", 0, 0, tiled=True)
    norm_factor = 1.0 / (members * n_member - 1)
    owned = jnp.sum(received, axis=0) * norm_factor
    return owned.swapaxes(1, 2).reshape(slots, variables, levels, slab_rows, lanes)


def solution(mesh):
    in_specs = (
        P("member", None, None, None, None, "tile"),
        P(None, None, None, "member", "tile"),
        P(None, None, "tile"),
        P(),
    )
    out_specs = P(None, None, None, "member", "tile")
    return jax.shard_map(body, mesh=mesh, in_specs=in_specs, out_specs=out_specs, check_vma=False)
```

```python
import math

import jax
import jax.numpy as jnp
from jax import lax
from jax.experimental import pallas as pl
from jax.experimental.pallas import tpu as pltpu
from jax.sharding import PartitionSpec as P

SWEEPS = 10
GROUPS = 4
ANCHOR_WORK = 10**10
VMEM_LIMIT = 16 * 1024 * 1024


def lane_roll(value, shift):
    shift = shift % value.shape[-1]
    return value if shift == 0 else pltpu.roll(value, shift, 1)


def lane_index(shape):
    return lax.broadcasted_iota(jnp.int32, shape, 1)


def spread(row, rows=8):
    return jnp.broadcast_to(row, (rows, row.shape[-1]))


def whole(memory_space=pltpu.VMEM):
    return pl.BlockSpec(memory_space=memory_space)


def mirrors(level, row, levels, rows):
    return [
        (far_level, far_row)
        for far_level in (level, levels - 1 - level)
        for far_row in (row, rows - 1 - row)
    ]


def group_index(shape, start):
    part = shape[-1] // GROUPS
    return (lane_index(shape) + start) % shape[-1] // part


def own_strips(values):
    part = values[0].shape[-1] // GROUPS
    rolled = [lane_roll(value, part * g) for g, value in enumerate(values)]
    both = []
    for start in (SWEEPS, part - SWEEPS):
        group = group_index(values[0].shape, start)
        strip = rolled[0]
        for g in range(1, GROUPS):
            strip = jnp.where(group == g, rolled[g], strip)
        both.append(strip)
    return both


def packed_edges(first, second):
    part = first.shape[-1] // GROUPS
    place = lane_index(first.shape) % part
    moved = lane_roll(second, part // 2)
    to_right = jnp.where(place >= part // 2, first, moved)
    to_left = jnp.where(place < part // 2, first, moved)
    return to_right, to_left


def joined_strip(own, edge, index, halo):
    part = own.shape[-1] // GROUPS
    return jnp.where(halo, lane_roll(edge, -(index % 2) * (part // 2)), own)


def swap_sides(values, swapped):
    first, second = values
    return jnp.where(swapped, second, first), jnp.where(swapped, first, second)


def first_is_left():
    return lax.axis_index("tile") % 2 == 1


def swap_pairs(start, n_member, n_tile):
    pairs = []
    for member in range(n_member):
        for tile in range(n_tile):
            other = tile + 1 if (tile - start) % 2 == 0 else tile - 1
            if 0 <= other < n_tile:
                pairs.append((member * n_tile + tile, member * n_tile + other))
            elif n_member % 2 == 0:
                pairs.append((member * n_tile + tile, (member ^ 1) * n_tile + tile))
    return pairs


def without_partner(is_left, n_tile):
    tile = lax.axis_index("tile")
    return jnp.where(is_left, tile == 0, tile == n_tile - 1)


def total(terms):
    terms = list(terms)
    while len(terms) > 1:
        terms = [
            terms[i] + terms[i + 1] if i + 1 < len(terms) else terms[i]
            for i in range(0, len(terms), 2)
        ]
    return terms[0]


def around(planes, level, row, even_group=None):
    levels, rows = len(planes), len(planes[level])
    here = planes[level][row]
    terms = [lane_roll(here, 1), lane_roll(here, -1)]
    if row > 0:
        terms.append(planes[level][row - 1])
    if row < rows - 1:
        terms.append(planes[level][row + 1])
    elif even_group is not None:
        part = here.shape[-1] // GROUPS
        terms.append(jnp.where(even_group, lane_roll(here, -part), lane_roll(here, part)))
    if level > 0:
        terms.append(planes[level - 1][row])
    if level < levels - 1:
        terms.append(planes[level + 1][row])
    elif even_group is not None:
        terms.append(lane_roll(here, here.shape[-1] // 2))
    return total(terms)


def sweep(source, target, keep_at, square_at):
    levels, rows = source.shape[0], source.shape[1]
    planes = [[source[level, row] for row in range(rows)] for level in range(levels)]
    for level in range(levels):
        for row in range(rows):
            target[level, row] = keep_at(level, row) * planes[level][row] + square_at(
                level, row
            ) * around(planes, level, row)


def anchor_kernel(out_ref):
    out_ref[...] = jnp.zeros_like(out_ref)


def weigh_kernel(
    owner_ref,
    gathered_ref,
    pert_ref,
    coeff_ref,
    anchor_ref,
    field_ref,
    left_ref,
    right_ref,
    coeff_left_ref,
    coeff_right_ref,
    to_first_ref,
    to_second_ref,
    grad_ref,
):
    members, terms, levels, rows, lanes = pert_ref.shape
    slab_rows = gathered_ref.shape[2]
    strip_levels, strip_rows = left_ref.shape[:2]
    owner_row = owner_ref[...].astype(jnp.float32)
    place = lane_index(owner_row.shape)
    owners = [
        jnp.sum(jnp.where(place == slab, owner_row, 0.0)).astype(jnp.int32)
        for slab in range(rows // slab_rows)
    ]
    left_first = jnp.broadcast_to(first_is_left(), (8, lanes))
    for slab, owner in enumerate(owners):
        for term in range(terms):
            for inner in range(slab_rows):
                row = slab * slab_rows + inner
                grad_ref[pl.ds(term * levels * rows + row, levels, stride=rows), :] = gathered_ref[
                    owner, term, inner
                ]

    for level in range(levels):
        base = level * rows
        coeff = coeff_ref[level]
        gradients = [
            coeff * grad_ref[pl.ds(term * levels * rows + base, rows), :] for term in range(terms)
        ]
        for member in range(members):
            field_ref[pl.ds(base * members + member, rows, stride=members), :] = total(
                pert_ref[member, term, level].astype(jnp.float32) * gradients[term]
                for term in range(terms)
            )

    pairs = strip_levels * strip_rows // 2
    fields, coeffs = [], []
    for level in range(strip_levels):
        for row in range(strip_rows):
            index = level * strip_rows + row
            cells = mirrors(level, row, levels, rows)
            field = own_strips(
                [field_ref[pl.ds((l * rows + r) * members, members), :] for l, r in cells]
            )
            coeff = own_strips([spread(coeff_ref[l, pl.ds(r, 1), :]) for l, r in cells])
            fields.append(field[0])
            coeffs.append(coeff[0])
            left_ref[level, row], right_ref[level, row] = field
            coeff_left_ref[pl.ds(index, 1), :] = coeff[0][0:1]
            coeff_right_ref[pl.ds(index, 1), :] = coeff[1][0:1]
    for pair in range(pairs):
        edges = packed_edges(fields[2 * pair], fields[2 * pair + 1])
        coeff_edges = packed_edges(coeffs[2 * pair], coeffs[2 * pair + 1])
        edges = swap_sides(edges, left_first)
        coeff_edges = swap_sides(coeff_edges, left_first)
        for ref, edge, coeff_edge in zip((to_first_ref, to_second_ref), edges, coeff_edges):
            ref[pl.ds(pair * members, members), :] = edge
            ref[pl.ds(pairs * members + pair, 1), :] = coeff_edge[0:1]


def interior_kernel(
    field_ref, coeff_ref, out_ref, other_ref, keep_ref, square_ref, inverse_ref
):
    levels, rows, members, lanes = field_ref.shape
    row_index = lax.broadcasted_iota(jnp.int32, (rows, lanes), 0)
    for level in range(levels):
        here = coeff_ref[level]
        beside = [
            lane_roll(here, 1),
            lane_roll(here, -1),
            jnp.where(row_index > 0, pltpu.roll(here, 1, 0), 0.0),
            jnp.where(row_index < rows - 1, pltpu.roll(here, rows - 1, 0), 0.0),
        ]
        if level > 0:
            beside.append(coeff_ref[level - 1])
        if level < levels - 1:
            beside.append(coeff_ref[level + 1])
        keep_ref[level] = 1.0 - here * total(beside)
        square_ref[level] = here * here
        inverse_ref[level] = 1.0 / here

    def keep_at(level, row):
        return keep_ref[level, pl.ds(row, 1), :]

    def square_at(level, row):
        return square_ref[level, pl.ds(row, 1), :]

    sweep(field_ref, other_ref, keep_at, square_at)
    sweep(other_ref, out_ref, keep_at, square_at)

    def pair(index, carry):
        sweep(out_ref, other_ref, keep_at, square_at)
        sweep(other_ref, out_ref, keep_at, square_at)
        return carry

    lax.fori_loop(0, SWEEPS // 2 - 1, pair, 0)
    for level in range(levels):
        for row in range(rows):
            out_ref[level, row] = out_ref[level, row] * inverse_ref[level, pl.ds(row, 1), :]


class Strips:
    def __init__(self, strip_ref, coeff_ref, edge_at, is_left, keep_ref, square_ref):
        self.levels, self.rows, self.members, lanes = strip_ref.shape
        self.coeff_ref, self.keep_ref, self.square_ref = coeff_ref, keep_ref, square_ref
        part = lanes // GROUPS
        pairs = self.levels * self.rows // 2
        shape = (self.members, lanes)
        self.even_group = group_index(shape, SWEEPS if is_left else part - SWEEPS) % 2 == 0
        place = lane_index(shape) % part
        halo = place >= part - SWEEPS if is_left else place < SWEEPS
        self.planes, coeffs = [], []
        for level in range(self.levels):
            plane, coeff_plane = [], []
            for row in range(self.rows):
                index = level * self.rows + row
                edge = edge_at(index // 2 * self.members, self.members)
                coeff_edge = spread(edge_at(pairs * self.members + index // 2, 1), self.members)
                plane.append(joined_strip(strip_ref[level, row], edge, index, halo))
                coeff_plane.append(joined_strip(self.own_coeff(level, row), coeff_edge, index, halo))
            self.planes.append(plane)
            coeffs.append(coeff_plane)
        for level in range(self.levels):
            for row in range(self.rows):
                here = coeffs[level][row]
                keep_ref[level, row] = 1.0 - here * around(coeffs, level, row, self.even_group)
                square_ref[level, row] = here * here

    def own_coeff(self, level, row):
        return spread(self.coeff_ref[pl.ds(level * self.rows + row, 1), :], self.members)

    def step(self):
        self.planes = [
            [
                self.keep_ref[level, row] * self.planes[level][row]
                + self.square_ref[level, row] * around(self.planes, level, row, self.even_group)
                for row in range(self.rows)
            ]
            for level in range(self.levels)
        ]

    def final(self, level, row):
        coeff = self.own_coeff(level, row)
        return self.planes[level][row] / jnp.where(coeff > 0.0, coeff, 1.0)


def finish_kernel(
    owner_hbm,
    pert_ref,
    interior_ref,
    left_ref,
    right_ref,
    coeff_left_ref,
    coeff_right_ref,
    from_first_ref,
    from_second_ref,
    out_ref,
    local_ref,
    sum_ref,
    keep_left_ref,
    square_left_ref,
    keep_right_ref,
    square_right_ref,
    owner_ref,
    owner_sem,
):
    members, terms, levels, rows, lanes = pert_ref.shape
    slab_rows = out_ref.shape[2]
    part = lanes // GROUPS
    left_first = first_is_left()
    owner_copy = pltpu.make_async_copy(owner_hbm, owner_ref, owner_sem)
    owner_copy.start()

    def edge_reader(is_left):
        outside = without_partner(is_left, lax.axis_size("tile"))

        def edge_at(place, count):
            first = from_first_ref[pl.ds(place, count), :]
            second = from_second_ref[pl.ds(place, count), :]
            edge = jnp.where(left_first == is_left, first, second)
            return jnp.where(outside, 0.0, edge)

        return edge_at

    left = Strips(
        left_ref, coeff_left_ref, edge_reader(True), True, keep_left_ref, square_left_ref
    )
    right = Strips(
        right_ref, coeff_right_ref, edge_reader(False), False, keep_right_ref, square_right_ref
    )
    for _ in range(SWEEPS):
        left.step()
        right.step()
    lane = lane_index((members, lanes))
    for level in range(left.levels):
        for row in range(left.rows):
            left_end, right_end = left.final(level, row), right.final(level, row)
            for g, (l, r) in enumerate(mirrors(level, row, levels, rows)):
                ends = jnp.where(
                    lane < lanes // 2,
                    lane_roll(left_end, -part * g),
                    lane_roll(right_end, -part * g),
                )
                local_ref[pl.ds((l * rows + r) * members, members), :] = jnp.where(
                    (lane < SWEEPS) | (lane >= lanes - SWEEPS), ends, interior_ref[l, r]
                )

    for level in range(levels):
        base = level * rows
        fields = [
            local_ref[pl.ds(base * members + member, rows, stride=members), :]
            for member in range(members)
        ]
        for term in range(terms):
            sum_ref[pl.ds(term * levels * rows + base, rows), :] = total(
                pert_ref[member, term, level].astype(jnp.float32) * fields[member]
                for member in range(members)
            )
    owner_copy.wait()
    for slab in range(rows // slab_rows):
        owner = owner_ref[slab]
        for term in range(terms):
            for inner in range(slab_rows):
                row = slab * slab_rows + inner
                out_ref[owner, term, inner] = sum_ref[
                    pl.ds(term * levels * rows + row, levels, stride=rows), :
                ]


def local_call(kernel, name, outs, scratch, operands, places, work):
    def shape_of(out):
        return out if isinstance(out, jax.ShapeDtypeStruct) else jax.ShapeDtypeStruct(out, jnp.float32)

    shapes = tuple(shape_of(out) for out in outs)
    specs = tuple(whole() for _ in outs)
    moved = sum(math.prod(x.shape) * x.dtype.itemsize for x in tuple(operands) + shapes)
    single = len(outs) == 1
    return pl.pallas_call(
        kernel,
        out_shape=shapes[0] if single else shapes,
        in_specs=[whole(place) for place in places],
        out_specs=specs[0] if single else specs,
        scratch_shapes=[
            pltpu.VMEM(item, jnp.float32) if isinstance(item, tuple) else item for item in scratch
        ],
        compiler_params=pltpu.CompilerParams(vmem_limit_bytes=VMEM_LIMIT),
        cost_estimate=pl.CostEstimate(flops=work, bytes_accessed=moved, transcendentals=0),
        name=name,
    )(*operands)


def body(perturbations, gradient_store, diffusivity, slab_owner):
    members, slots, variables, levels, rows, lanes = perturbations.shape
    terms = slots * variables
    n_member = lax.axis_size("member")
    n_tile = lax.axis_size("tile")
    slab_rows = gradient_store.shape[3]
    cells = levels * rows * lanes
    strip_levels, strip_rows = levels // 2, rows // 2
    strips = strip_levels * strip_rows
    wide_strip = (strip_levels, strip_rows, members, lanes)
    coeff_strip = (strips, lanes)
    wide_field = (levels, rows, members, lanes)
    flat_field = (levels * rows * members, lanes)
    field_coeff = (levels, rows, lanes)
    edge_shape = (strips // 2 * (members + 1), lanes)
    grad_shape = (terms * levels * rows, lanes)
    vmem = pltpu.VMEM

    pert = perturbations.reshape(members, terms, levels, rows, lanes)
    slab = gradient_store.reshape(terms, levels, slab_rows, lanes).swapaxes(1, 2)
    anchor = local_call(anchor_kernel, "anchor", [(8, lanes)], [], (), (), ANCHOR_WORK)
    gathered = lax.all_gather(slab, "member", axis=0, tiled=False)

    field, left, right, coeff_left, coeff_right, to_first, to_second = local_call(
        weigh_kernel,
        "weigh",
        [flat_field, wide_strip, wide_strip, coeff_strip, coeff_strip, edge_shape, edge_shape],
        [grad_shape],
        (slab_owner.reshape(1, -1), gathered, pert, diffusivity, anchor),
        (vmem,) * 5,
        2 * terms * members * cells,
    )
    from_first, from_second = (
        lax.ppermute(edges, ("member", "tile"), swap_pairs(start, n_member, n_tile))
        for start, edges in ((0, to_first), (1, to_second))
    )

    interior = local_call(
        interior_kernel,
        "interior",
        [wide_field],
        [wide_field, field_coeff, field_coeff, field_coeff],
        (field.reshape(wide_field), diffusivity),
        (vmem,) * 2,
        8 * SWEEPS * members * cells,
    )
    sums = local_call(
        finish_kernel,
        "finish",
        [(n_member, terms, slab_rows, levels, lanes)],
        [flat_field, grad_shape]
        + [wide_strip] * 4
        + [pltpu.SMEM(slab_owner.shape, slab_owner.dtype), pltpu.SemaphoreType.DMA],
        (
            pltpu.with_memory_space_constraint(slab_owner, pltpu.HBM),
            pert,
            interior,
            left,
            right,
            coeff_left,
            coeff_right,
            from_first,
            from_second,
        ),
        (pltpu.HBM,) + (vmem,) * 8,
        2 * terms * members * cells,
    )
    received = lax.all_to_all(sums, "member", 0, 0, tiled=True)
    norm_factor = 1.0 / (members * n_member - 1)
    owned = jnp.sum(received, axis=0) * norm_factor
    return owned.swapaxes(1, 2).reshape(slots, variables, levels, slab_rows, lanes)


def solution(mesh):
    in_specs = (
        P("member", None, None, None, None, "tile"),
        P(None, None, None, "member", "tile"),
        P(None, None, "tile"),
        P(),
    )
    out_specs = P(None, None, None, "member", "tile")
    return jax.shard_map(body, mesh=mesh, in_specs=in_specs, out_specs=out_specs, check_vma=False)
```

```python
import math

import jax
import jax.numpy as jnp
from jax import lax
from jax.experimental import pallas as pl
from jax.experimental.pallas import tpu as pltpu
from jax.sharding import PartitionSpec as P

SWEEPS = 10
GROUPS = 4
ROUNDS = 3
ANCHOR_WORK = 10**10
VMEM_LIMIT = 16 * 1024 * 1024


def lane_roll(value, shift):
    shift = shift % value.shape[-1]
    return value if shift == 0 else pltpu.roll(value, shift, 1)


def lane_index(shape):
    return lax.broadcasted_iota(jnp.int32, shape, 1)


def spread(row, rows=8):
    return jnp.broadcast_to(row, (rows, row.shape[-1]))


def whole(memory_space=pltpu.VMEM):
    return pl.BlockSpec(memory_space=memory_space)


def mirrors(level, row, levels, rows):
    return [
        (far_level, far_row)
        for far_level in (level, levels - 1 - level)
        for far_row in (row, rows - 1 - row)
    ]


def group_index(shape, start):
    part = shape[-1] // GROUPS
    return (lane_index(shape) + start) % shape[-1] // part


def own_strips(values):
    part = values[0].shape[-1] // GROUPS
    rolled = [lane_roll(value, part * g) for g, value in enumerate(values)]
    both = []
    for start in (SWEEPS, part - SWEEPS):
        group = group_index(values[0].shape, start)
        strip = rolled[0]
        for g in range(1, GROUPS):
            strip = jnp.where(group == g, rolled[g], strip)
        both.append(strip)
    return both


def packed_edges(first, second):
    part = first.shape[-1] // GROUPS
    place = lane_index(first.shape) % part
    moved = lane_roll(second, part // 2)
    to_right = jnp.where(place >= part // 2, first, moved)
    to_left = jnp.where(place < part // 2, first, moved)
    return to_right, to_left


def joined_strip(own, edge, index, halo):
    part = own.shape[-1] // GROUPS
    return jnp.where(halo, lane_roll(edge, -(index % 2) * (part // 2)), own)


def right_round():
    return lax.axis_index("tile") % ROUNDS


def left_round():
    return (lax.axis_index("tile") + ROUNDS - 1) % ROUNDS


def swap_pairs(turn, n_member, n_tile):
    pairs = []
    for member in range(n_member):
        for tile in range(n_tile):
            if tile % ROUNDS == turn and tile + 1 < n_tile:
                pairs.append((member * n_tile + tile, member * n_tile + tile + 1))
            elif tile > 0 and (tile - 1) % ROUNDS == turn:
                pairs.append((member * n_tile + tile, member * n_tile + tile - 1))
            elif n_member % 2 == 0:
                pairs.append((member * n_tile + tile, (member ^ 1) * n_tile + tile))
    return pairs


def without_partner(is_left, n_tile):
    tile = lax.axis_index("tile")
    return jnp.where(is_left, tile == 0, tile == n_tile - 1)


def total(terms):
    terms = list(terms)
    while len(terms) > 1:
        terms = [
            terms[i] + terms[i + 1] if i + 1 < len(terms) else terms[i]
            for i in range(0, len(terms), 2)
        ]
    return terms[0]


def around(planes, level, row, even_group=None):
    levels, rows = len(planes), len(planes[level])
    here = planes[level][row]
    terms = [lane_roll(here, 1), lane_roll(here, -1)]
    if row > 0:
        terms.append(planes[level][row - 1])
    if row < rows - 1:
        terms.append(planes[level][row + 1])
    elif even_group is not None:
        part = here.shape[-1] // GROUPS
        terms.append(jnp.where(even_group, lane_roll(here, -part), lane_roll(here, part)))
    if level > 0:
        terms.append(planes[level - 1][row])
    if level < levels - 1:
        terms.append(planes[level + 1][row])
    elif even_group is not None:
        terms.append(lane_roll(here, here.shape[-1] // 2))
    return total(terms)


def sweep(source, target, keep_at, square_at):
    levels, rows = source.shape[0], source.shape[1]
    planes = [[source[level, row] for row in range(rows)] for level in range(levels)]
    for level in range(levels):
        for row in range(rows):
            target[level, row] = keep_at(level, row) * planes[level][row] + square_at(
                level, row
            ) * around(planes, level, row)


def anchor_kernel(out_ref):
    out_ref[...] = jnp.zeros_like(out_ref)


def weigh_kernel(
    owner_ref,
    gathered_ref,
    pert_ref,
    coeff_ref,
    anchor_ref,
    field_ref,
    left_ref,
    right_ref,
    coeff_left_ref,
    coeff_right_ref,
    *rest,
):
    edge_refs, (grad_ref,) = rest[:ROUNDS], rest[ROUNDS:]
    members, terms, levels, rows, lanes = pert_ref.shape
    slab_rows = gathered_ref.shape[2]
    strip_levels, strip_rows = left_ref.shape[:2]
    owner_row = owner_ref[...].astype(jnp.float32)
    place = lane_index(owner_row.shape)
    owners = [
        jnp.sum(jnp.where(place == slab, owner_row, 0.0)).astype(jnp.int32)
        for slab in range(rows // slab_rows)
    ]
    for slab, owner in enumerate(owners):
        for term in range(terms):
            for inner in range(slab_rows):
                row = slab * slab_rows + inner
                grad_ref[pl.ds(term * levels * rows + row, levels, stride=rows), :] = gathered_ref[
                    owner, term, inner
                ]

    for level in range(levels):
        base = level * rows
        coeff = coeff_ref[level]
        gradients = [
            coeff * grad_ref[pl.ds(term * levels * rows + base, rows), :] for term in range(terms)
        ]
        for member in range(members):
            field_ref[pl.ds(base * members + member, rows, stride=members), :] = total(
                pert_ref[member, term, level].astype(jnp.float32) * gradients[term]
                for term in range(terms)
            )

    pairs = strip_levels * strip_rows // 2
    fields, coeffs = [], []
    for level in range(strip_levels):
        for row in range(strip_rows):
            index = level * strip_rows + row
            cells = mirrors(level, row, levels, rows)
            field = own_strips(
                [field_ref[pl.ds((l * rows + r) * members, members), :] for l, r in cells]
            )
            coeff = own_strips([spread(coeff_ref[l, pl.ds(r, 1), :]) for l, r in cells])
            fields.append(field[0])
            coeffs.append(coeff[0])
            left_ref[level, row], right_ref[level, row] = field
            coeff_left_ref[pl.ds(index, 1), :] = coeff[0][0:1]
            coeff_right_ref[pl.ds(index, 1), :] = coeff[1][0:1]
    for pair in range(pairs):
        edges = packed_edges(fields[2 * pair], fields[2 * pair + 1])
        coeff_edges = packed_edges(coeffs[2 * pair], coeffs[2 * pair + 1])
        for turn, ref in enumerate(edge_refs):
            to_right = jnp.broadcast_to(right_round() == turn, (8, lanes))
            ref[pl.ds(pair * members, members), :] = jnp.where(to_right, *edges)
            ref[pl.ds(pairs * members + pair, 1), :] = jnp.where(to_right, *coeff_edges)[0:1]


def interior_kernel(
    field_ref, coeff_ref, out_ref, other_ref, keep_ref, square_ref, inverse_ref
):
    levels, rows, members, lanes = field_ref.shape
    row_index = lax.broadcasted_iota(jnp.int32, (rows, lanes), 0)
    for level in range(levels):
        here = coeff_ref[level]
        beside = [
            lane_roll(here, 1),
            lane_roll(here, -1),
            jnp.where(row_index > 0, pltpu.roll(here, 1, 0), 0.0),
            jnp.where(row_index < rows - 1, pltpu.roll(here, rows - 1, 0), 0.0),
        ]
        if level > 0:
            beside.append(coeff_ref[level - 1])
        if level < levels - 1:
            beside.append(coeff_ref[level + 1])
        keep_ref[level] = 1.0 - here * total(beside)
        square_ref[level] = here * here
        inverse_ref[level] = 1.0 / here

    def keep_at(level, row):
        return keep_ref[level, pl.ds(row, 1), :]

    def square_at(level, row):
        return square_ref[level, pl.ds(row, 1), :]

    sweep(field_ref, other_ref, keep_at, square_at)
    sweep(other_ref, out_ref, keep_at, square_at)

    def pair(index, carry):
        sweep(out_ref, other_ref, keep_at, square_at)
        sweep(other_ref, out_ref, keep_at, square_at)
        return carry

    lax.fori_loop(0, SWEEPS // 2 - 1, pair, 0)
    for level in range(levels):
        for row in range(rows):
            out_ref[level, row] = out_ref[level, row] * inverse_ref[level, pl.ds(row, 1), :]


class Strips:
    def __init__(self, strip_ref, coeff_ref, edge_at, is_left, keep_ref, square_ref):
        self.levels, self.rows, self.members, lanes = strip_ref.shape
        self.coeff_ref, self.keep_ref, self.square_ref = coeff_ref, keep_ref, square_ref
        part = lanes // GROUPS
        pairs = self.levels * self.rows // 2
        shape = (self.members, lanes)
        self.even_group = group_index(shape, SWEEPS if is_left else part - SWEEPS) % 2 == 0
        place = lane_index(shape) % part
        halo = place >= part - SWEEPS if is_left else place < SWEEPS
        self.planes, coeffs = [], []
        for level in range(self.levels):
            plane, coeff_plane = [], []
            for row in range(self.rows):
                index = level * self.rows + row
                edge = edge_at(index // 2 * self.members, self.members)
                coeff_edge = spread(edge_at(pairs * self.members + index // 2, 1), self.members)
                plane.append(joined_strip(strip_ref[level, row], edge, index, halo))
                coeff_plane.append(joined_strip(self.own_coeff(level, row), coeff_edge, index, halo))
            self.planes.append(plane)
            coeffs.append(coeff_plane)
        for level in range(self.levels):
            for row in range(self.rows):
                here = coeffs[level][row]
                keep_ref[level, row] = 1.0 - here * around(coeffs, level, row, self.even_group)
                square_ref[level, row] = here * here

    def own_coeff(self, level, row):
        return spread(self.coeff_ref[pl.ds(level * self.rows + row, 1), :], self.members)

    def step(self):
        self.planes = [
            [
                self.keep_ref[level, row] * self.planes[level][row]
                + self.square_ref[level, row] * around(self.planes, level, row, self.even_group)
                for row in range(self.rows)
            ]
            for level in range(self.levels)
        ]

    def final(self, level, row):
        coeff = self.own_coeff(level, row)
        return self.planes[level][row] / jnp.where(coeff > 0.0, coeff, 1.0)


def finish_kernel(
    owner_hbm,
    pert_ref,
    interior_ref,
    left_ref,
    right_ref,
    coeff_left_ref,
    coeff_right_ref,
    *rest,
):
    edge_refs, rest = rest[:ROUNDS], rest[ROUNDS:]
    out_ref, local_ref, sum_ref, keep_left_ref, square_left_ref = rest[:5]
    keep_right_ref, square_right_ref, owner_ref, owner_sem = rest[5:]
    members, terms, levels, rows, lanes = pert_ref.shape
    slab_rows = out_ref.shape[2]
    part = lanes // GROUPS
    owner_copy = pltpu.make_async_copy(owner_hbm, owner_ref, owner_sem)
    owner_copy.start()

    def edge_reader(is_left):
        outside = without_partner(is_left, lax.axis_size("tile"))
        turn = left_round() if is_left else right_round()

        def edge_at(place, count):
            edge = edge_refs[0][pl.ds(place, count), :]
            for index in range(1, ROUNDS):
                edge = jnp.where(turn == index, edge_refs[index][pl.ds(place, count), :], edge)
            return jnp.where(outside, 0.0, edge)

        return edge_at

    left = Strips(
        left_ref, coeff_left_ref, edge_reader(True), True, keep_left_ref, square_left_ref
    )
    right = Strips(
        right_ref, coeff_right_ref, edge_reader(False), False, keep_right_ref, square_right_ref
    )
    for _ in range(SWEEPS):
        left.step()
        right.step()
    lane = lane_index((members, lanes))
    for level in range(left.levels):
        for row in range(left.rows):
            left_end, right_end = left.final(level, row), right.final(level, row)
            for g, (l, r) in enumerate(mirrors(level, row, levels, rows)):
                ends = jnp.where(
                    lane < lanes // 2,
                    lane_roll(left_end, -part * g),
                    lane_roll(right_end, -part * g),
                )
                local_ref[pl.ds((l * rows + r) * members, members), :] = jnp.where(
                    (lane < SWEEPS) | (lane >= lanes - SWEEPS), ends, interior_ref[l, r]
                )

    for level in range(levels):
        base = level * rows
        fields = [
            local_ref[pl.ds(base * members + member, rows, stride=members), :]
            for member in range(members)
        ]
        for term in range(terms):
            sum_ref[pl.ds(term * levels * rows + base, rows), :] = total(
                pert_ref[member, term, level].astype(jnp.float32) * fields[member]
                for member in range(members)
            )
    owner_copy.wait()
    for slab in range(rows // slab_rows):
        owner = owner_ref[slab]
        for term in range(terms):
            for inner in range(slab_rows):
                row = slab * slab_rows + inner
                out_ref[owner, term, inner] = sum_ref[
                    pl.ds(term * levels * rows + row, levels, stride=rows), :
                ]


def local_call(kernel, name, outs, scratch, operands, places, work):
    def shape_of(out):
        return out if isinstance(out, jax.ShapeDtypeStruct) else jax.ShapeDtypeStruct(out, jnp.float32)

    shapes = tuple(shape_of(out) for out in outs)
    specs = tuple(whole() for _ in outs)
    moved = sum(math.prod(x.shape) * x.dtype.itemsize for x in tuple(operands) + shapes)
    single = len(outs) == 1
    return pl.pallas_call(
        kernel,
        out_shape=shapes[0] if single else shapes,
        in_specs=[whole(place) for place in places],
        out_specs=specs[0] if single else specs,
        scratch_shapes=[
            pltpu.VMEM(item, jnp.float32) if isinstance(item, tuple) else item for item in scratch
        ],
        compiler_params=pltpu.CompilerParams(vmem_limit_bytes=VMEM_LIMIT),
        cost_estimate=pl.CostEstimate(flops=work, bytes_accessed=moved, transcendentals=0),
        name=name,
    )(*operands)


def body(perturbations, gradient_store, diffusivity, slab_owner):
    members, slots, variables, levels, rows, lanes = perturbations.shape
    terms = slots * variables
    n_member = lax.axis_size("member")
    n_tile = lax.axis_size("tile")
    slab_rows = gradient_store.shape[3]
    cells = levels * rows * lanes
    strip_levels, strip_rows = levels // 2, rows // 2
    strips = strip_levels * strip_rows
    wide_strip = (strip_levels, strip_rows, members, lanes)
    coeff_strip = (strips, lanes)
    wide_field = (levels, rows, members, lanes)
    flat_field = (levels * rows * members, lanes)
    field_coeff = (levels, rows, lanes)
    edge_shape = (strips // 2 * (members + 1), lanes)
    grad_shape = (terms * levels * rows, lanes)
    vmem = pltpu.VMEM

    pert = perturbations.reshape(members, terms, levels, rows, lanes)
    slab = gradient_store.reshape(terms, levels, slab_rows, lanes).swapaxes(1, 2)
    anchor = local_call(anchor_kernel, "anchor", [(8, lanes)], [], (), (), ANCHOR_WORK)
    gathered = lax.all_gather(slab, "member", axis=0, tiled=False)

    field, left, right, coeff_left, coeff_right, *edges = local_call(
        weigh_kernel,
        "weigh",
        [flat_field, wide_strip, wide_strip, coeff_strip, coeff_strip]
        + [edge_shape] * ROUNDS,
        [grad_shape],
        (slab_owner.reshape(1, -1), gathered, pert, diffusivity, anchor),
        (vmem,) * 5,
        2 * terms * members * cells,
    )
    edges = [
        lax.ppermute(values, ("member", "tile"), swap_pairs(turn, n_member, n_tile))
        for turn, values in enumerate(edges)
    ]

    interior = local_call(
        interior_kernel,
        "interior",
        [wide_field],
        [wide_field, field_coeff, field_coeff, field_coeff],
        (field.reshape(wide_field), diffusivity),
        (vmem,) * 2,
        8 * SWEEPS * members * cells,
    )
    sums = local_call(
        finish_kernel,
        "finish",
        [(n_member, terms, slab_rows, levels, lanes)],
        [flat_field, grad_shape]
        + [wide_strip] * 4
        + [pltpu.SMEM(slab_owner.shape, slab_owner.dtype), pltpu.SemaphoreType.DMA],
        (
            pltpu.with_memory_space_constraint(slab_owner, pltpu.HBM),
            pert,
            interior,
            left,
            right,
            coeff_left,
            coeff_right,
            *edges,
        ),
        (pltpu.HBM,) + (vmem,) * (6 + ROUNDS),
        2 * terms * members * cells,
    )
    received = lax.all_to_all(sums, "member", 0, 0, tiled=True)
    norm_factor = 1.0 / (members * n_member - 1)
    owned = jnp.sum(received, axis=0) * norm_factor
    return owned.swapaxes(1, 2).reshape(slots, variables, levels, slab_rows, lanes)


def solution(mesh):
    in_specs = (
        P("member", None, None, None, None, "tile"),
        P(None, None, None, "member", "tile"),
        P(None, None, "tile"),
        P(),
    )
    out_specs = P(None, None, None, "member", "tile")
    return jax.shard_map(body, mesh=mesh, in_specs=in_specs, out_specs=out_specs, check_vma=False)
```

```python
import math

import jax
import jax.numpy as jnp
from jax import lax
from jax.experimental import pallas as pl
from jax.experimental.pallas import tpu as pltpu
from jax.sharding import PartitionSpec as P

SWEEPS = 10
GROUPS = 4
ROUNDS = 3
ANCHOR_WORK = 5 * 10**6
VMEM_LIMIT = 16 * 1024 * 1024


def lane_roll(value, shift):
    shift = shift % value.shape[-1]
    return value if shift == 0 else pltpu.roll(value, shift, 1)


def lane_index(shape):
    return lax.broadcasted_iota(jnp.int32, shape, 1)


def spread(row, rows=8):
    return jnp.broadcast_to(row, (rows, row.shape[-1]))


def whole(memory_space=pltpu.VMEM):
    return pl.BlockSpec(memory_space=memory_space)


def mirrors(level, row, levels, rows):
    return [
        (far_level, far_row)
        for far_level in (level, levels - 1 - level)
        for far_row in (row, rows - 1 - row)
    ]


def group_index(shape, start):
    part = shape[-1] // GROUPS
    return (lane_index(shape) + start) % shape[-1] // part


def own_strips(values):
    part = values[0].shape[-1] // GROUPS
    rolled = [lane_roll(value, part * g) for g, value in enumerate(values)]
    both = []
    for start in (SWEEPS, part - SWEEPS):
        group = group_index(values[0].shape, start)
        strip = rolled[0]
        for g in range(1, GROUPS):
            strip = jnp.where(group == g, rolled[g], strip)
        both.append(strip)
    return both


def packed_edges(first, second):
    part = first.shape[-1] // GROUPS
    place = lane_index(first.shape) % part
    moved = lane_roll(second, part // 2)
    to_right = jnp.where(place >= part // 2, first, moved)
    to_left = jnp.where(place < part // 2, first, moved)
    return to_right, to_left


def joined_strip(own, edge, index, halo):
    part = own.shape[-1] // GROUPS
    return jnp.where(halo, lane_roll(edge, -(index % 2) * (part // 2)), own)


def right_round():
    return lax.axis_index("tile") % ROUNDS


def left_round():
    return (lax.axis_index("tile") + ROUNDS - 1) % ROUNDS


def swap_pairs(turn, n_member, n_tile):
    pairs = []
    for member in range(n_member):
        for tile in range(n_tile):
            if tile % ROUNDS == turn and tile + 1 < n_tile:
                pairs.append((member * n_tile + tile, member * n_tile + tile + 1))
            elif tile > 0 and (tile - 1) % ROUNDS == turn:
                pairs.append((member * n_tile + tile, member * n_tile + tile - 1))
            elif n_member % 2 == 0:
                pairs.append((member * n_tile + tile, (member ^ 1) * n_tile + tile))
    return pairs


def without_partner(is_left, n_tile):
    tile = lax.axis_index("tile")
    return jnp.where(is_left, tile == 0, tile == n_tile - 1)


def total(terms):
    terms = list(terms)
    while len(terms) > 1:
        terms = [
            terms[i] + terms[i + 1] if i + 1 < len(terms) else terms[i]
            for i in range(0, len(terms), 2)
        ]
    return terms[0]


def around(planes, level, row, even_group=None):
    levels, rows = len(planes), len(planes[level])
    here = planes[level][row]
    terms = [lane_roll(here, 1), lane_roll(here, -1)]
    if row > 0:
        terms.append(planes[level][row - 1])
    if row < rows - 1:
        terms.append(planes[level][row + 1])
    elif even_group is not None:
        part = here.shape[-1] // GROUPS
        terms.append(jnp.where(even_group, lane_roll(here, -part), lane_roll(here, part)))
    if level > 0:
        terms.append(planes[level - 1][row])
    if level < levels - 1:
        terms.append(planes[level + 1][row])
    elif even_group is not None:
        terms.append(lane_roll(here, here.shape[-1] // 2))
    return total(terms)


def sweep(source, target, keep_at, square_at):
    levels, rows = source.shape[0], source.shape[1]
    planes = [[source[level, row] for row in range(rows)] for level in range(levels)]
    for level in range(levels):
        for row in range(rows):
            target[level, row] = keep_at(level, row) * planes[level][row] + square_at(
                level, row
            ) * around(planes, level, row)


def anchor_kernel(out_ref):
    out_ref[...] = jnp.zeros_like(out_ref)


def weigh_kernel(
    owner_ref,
    gathered_ref,
    pert_ref,
    coeff_ref,
    anchor_ref,
    field_ref,
    left_ref,
    right_ref,
    coeff_left_ref,
    coeff_right_ref,
    *rest,
):
    edge_refs, (grad_ref,) = rest[:ROUNDS], rest[ROUNDS:]
    members, terms, levels, rows, lanes = pert_ref.shape
    slab_rows = gathered_ref.shape[2]
    strip_levels, strip_rows = left_ref.shape[:2]
    owner_row = owner_ref[...].astype(jnp.float32)
    place = lane_index(owner_row.shape)
    owners = [
        jnp.sum(jnp.where(place == slab, owner_row, 0.0)).astype(jnp.int32)
        for slab in range(rows // slab_rows)
    ]
    for slab, owner in enumerate(owners):
        for term in range(terms):
            for inner in range(slab_rows):
                row = slab * slab_rows + inner
                grad_ref[pl.ds(term * levels * rows + row, levels, stride=rows), :] = gathered_ref[
                    owner, term, inner
                ]

    for level in range(levels):
        base = level * rows
        coeff = coeff_ref[level]
        gradients = [
            coeff * grad_ref[pl.ds(term * levels * rows + base, rows), :] for term in range(terms)
        ]
        for member in range(members):
            field_ref[pl.ds(base * members + member, rows, stride=members), :] = total(
                pert_ref[member, term, level].astype(jnp.float32) * gradients[term]
                for term in range(terms)
            )

    pairs = strip_levels * strip_rows // 2
    fields, coeffs = [], []
    for level in range(strip_levels):
        for row in range(strip_rows):
            index = level * strip_rows + row
            cells = mirrors(level, row, levels, rows)
            field = own_strips(
                [field_ref[pl.ds((l * rows + r) * members, members), :] for l, r in cells]
            )
            coeff = own_strips([spread(coeff_ref[l, pl.ds(r, 1), :]) for l, r in cells])
            fields.append(field[0])
            coeffs.append(coeff[0])
            left_ref[level, row], right_ref[level, row] = field
            coeff_left_ref[pl.ds(index, 1), :] = coeff[0][0:1]
            coeff_right_ref[pl.ds(index, 1), :] = coeff[1][0:1]
    for pair in range(pairs):
        edges = packed_edges(fields[2 * pair], fields[2 * pair + 1])
        coeff_edges = packed_edges(coeffs[2 * pair], coeffs[2 * pair + 1])
        for turn, ref in enumerate(edge_refs):
            to_right = jnp.broadcast_to(right_round() == turn, (8, lanes))
            ref[pl.ds(pair * members, members), :] = jnp.where(to_right, *edges)
            ref[pl.ds(pairs * members + pair, 1), :] = jnp.where(to_right, *coeff_edges)[0:1]


def interior_kernel(
    field_ref, coeff_ref, out_ref, other_ref, keep_ref, square_ref, inverse_ref
):
    levels, rows, members, lanes = field_ref.shape
    row_index = lax.broadcasted_iota(jnp.int32, (rows, lanes), 0)
    for level in range(levels):
        here = coeff_ref[level]
        beside = [
            lane_roll(here, 1),
            lane_roll(here, -1),
            jnp.where(row_index > 0, pltpu.roll(here, 1, 0), 0.0),
            jnp.where(row_index < rows - 1, pltpu.roll(here, rows - 1, 0), 0.0),
        ]
        if level > 0:
            beside.append(coeff_ref[level - 1])
        if level < levels - 1:
            beside.append(coeff_ref[level + 1])
        keep_ref[level] = 1.0 - here * total(beside)
        square_ref[level] = here * here
        inverse_ref[level] = 1.0 / here

    def keep_at(level, row):
        return keep_ref[level, pl.ds(row, 1), :]

    def square_at(level, row):
        return square_ref[level, pl.ds(row, 1), :]

    sweep(field_ref, other_ref, keep_at, square_at)
    sweep(other_ref, out_ref, keep_at, square_at)

    def pair(index, carry):
        sweep(out_ref, other_ref, keep_at, square_at)
        sweep(other_ref, out_ref, keep_at, square_at)
        return carry

    lax.fori_loop(0, SWEEPS // 2 - 1, pair, 0)
    for level in range(levels):
        for row in range(rows):
            out_ref[level, row] = out_ref[level, row] * inverse_ref[level, pl.ds(row, 1), :]


class Strips:
    def __init__(self, strip_ref, coeff_ref, edge_at, is_left, keep_ref, square_ref):
        self.levels, self.rows, self.members, lanes = strip_ref.shape
        self.coeff_ref, self.keep_ref, self.square_ref = coeff_ref, keep_ref, square_ref
        part = lanes // GROUPS
        pairs = self.levels * self.rows // 2
        shape = (self.members, lanes)
        self.even_group = group_index(shape, SWEEPS if is_left else part - SWEEPS) % 2 == 0
        place = lane_index(shape) % part
        halo = place >= part - SWEEPS if is_left else place < SWEEPS
        self.planes, coeffs = [], []
        for level in range(self.levels):
            plane, coeff_plane = [], []
            for row in range(self.rows):
                index = level * self.rows + row
                edge = edge_at(index // 2 * self.members, self.members)
                coeff_edge = spread(edge_at(pairs * self.members + index // 2, 1), self.members)
                plane.append(joined_strip(strip_ref[level, row], edge, index, halo))
                coeff_plane.append(joined_strip(self.own_coeff(level, row), coeff_edge, index, halo))
            self.planes.append(plane)
            coeffs.append(coeff_plane)
        for level in range(self.levels):
            for row in range(self.rows):
                here = coeffs[level][row]
                keep_ref[level, row] = 1.0 - here * around(coeffs, level, row, self.even_group)
                square_ref[level, row] = here * here

    def own_coeff(self, level, row):
        return spread(self.coeff_ref[pl.ds(level * self.rows + row, 1), :], self.members)

    def step(self):
        self.planes = [
            [
                self.keep_ref[level, row] * self.planes[level][row]
                + self.square_ref[level, row] * around(self.planes, level, row, self.even_group)
                for row in range(self.rows)
            ]
            for level in range(self.levels)
        ]

    def final(self, level, row):
        coeff = self.own_coeff(level, row)
        return self.planes[level][row] / jnp.where(coeff > 0.0, coeff, 1.0)


def finish_kernel(
    owner_hbm,
    pert_ref,
    interior_ref,
    left_ref,
    right_ref,
    coeff_left_ref,
    coeff_right_ref,
    *rest,
):
    edge_refs, rest = rest[:ROUNDS], rest[ROUNDS:]
    out_ref, local_ref, sum_ref, keep_left_ref, square_left_ref = rest[:5]
    keep_right_ref, square_right_ref, owner_ref, owner_sem = rest[5:]
    members, terms, levels, rows, lanes = pert_ref.shape
    slab_rows = out_ref.shape[2]
    part = lanes // GROUPS
    owner_copy = pltpu.make_async_copy(owner_hbm, owner_ref, owner_sem)
    owner_copy.start()

    def edge_reader(is_left):
        outside = without_partner(is_left, lax.axis_size("tile"))
        turn = left_round() if is_left else right_round()

        def edge_at(place, count):
            edge = edge_refs[0][pl.ds(place, count), :]
            for index in range(1, ROUNDS):
                edge = jnp.where(turn == index, edge_refs[index][pl.ds(place, count), :], edge)
            return jnp.where(outside, 0.0, edge)

        return edge_at

    left = Strips(
        left_ref, coeff_left_ref, edge_reader(True), True, keep_left_ref, square_left_ref
    )
    right = Strips(
        right_ref, coeff_right_ref, edge_reader(False), False, keep_right_ref, square_right_ref
    )
    for _ in range(SWEEPS):
        left.step()
        right.step()
    lane = lane_index((members, lanes))
    for level in range(left.levels):
        for row in range(left.rows):
            left_end, right_end = left.final(level, row), right.final(level, row)
            for g, (l, r) in enumerate(mirrors(level, row, levels, rows)):
                ends = jnp.where(
                    lane < lanes // 2,
                    lane_roll(left_end, -part * g),
                    lane_roll(right_end, -part * g),
                )
                local_ref[pl.ds((l * rows + r) * members, members), :] = jnp.where(
                    (lane < SWEEPS) | (lane >= lanes - SWEEPS), ends, interior_ref[l, r]
                )

    for level in range(levels):
        base = level * rows
        fields = [
            local_ref[pl.ds(base * members + member, rows, stride=members), :]
            for member in range(members)
        ]
        for term in range(terms):
            sum_ref[pl.ds(term * levels * rows + base, rows), :] = total(
                pert_ref[member, term, level].astype(jnp.float32) * fields[member]
                for member in range(members)
            )
    owner_copy.wait()
    for slab in range(rows // slab_rows):
        owner = owner_ref[slab]
        for term in range(terms):
            for inner in range(slab_rows):
                row = slab * slab_rows + inner
                out_ref[owner, term, inner] = sum_ref[
                    pl.ds(term * levels * rows + row, levels, stride=rows), :
                ]


def local_call(kernel, name, outs, scratch, operands, places, work):
    def shape_of(out):
        return out if isinstance(out, jax.ShapeDtypeStruct) else jax.ShapeDtypeStruct(out, jnp.float32)

    shapes = tuple(shape_of(out) for out in outs)
    specs = tuple(whole() for _ in outs)
    moved = sum(math.prod(x.shape) * x.dtype.itemsize for x in tuple(operands) + shapes)
    single = len(outs) == 1
    return pl.pallas_call(
        kernel,
        out_shape=shapes[0] if single else shapes,
        in_specs=[whole(place) for place in places],
        out_specs=specs[0] if single else specs,
        scratch_shapes=[
            pltpu.VMEM(item, jnp.float32) if isinstance(item, tuple) else item for item in scratch
        ],
        compiler_params=pltpu.CompilerParams(vmem_limit_bytes=VMEM_LIMIT),
        cost_estimate=pl.CostEstimate(flops=work, bytes_accessed=moved, transcendentals=0),
        name=name,
    )(*operands)


def body(perturbations, gradient_store, diffusivity, slab_owner):
    members, slots, variables, levels, rows, lanes = perturbations.shape
    terms = slots * variables
    n_member = lax.axis_size("member")
    n_tile = lax.axis_size("tile")
    slab_rows = gradient_store.shape[3]
    cells = levels * rows * lanes
    strip_levels, strip_rows = levels // 2, rows // 2
    strips = strip_levels * strip_rows
    wide_strip = (strip_levels, strip_rows, members, lanes)
    coeff_strip = (strips, lanes)
    wide_field = (levels, rows, members, lanes)
    flat_field = (levels * rows * members, lanes)
    field_coeff = (levels, rows, lanes)
    edge_shape = (strips // 2 * (members + 1), lanes)
    grad_shape = (terms * levels * rows, lanes)
    vmem = pltpu.VMEM

    pert = perturbations.reshape(members, terms, levels, rows, lanes)
    slab = gradient_store.reshape(terms, levels, slab_rows, lanes).swapaxes(1, 2)
    anchor = local_call(anchor_kernel, "anchor", [(8, lanes)], [], (), (), ANCHOR_WORK)
    gathered = lax.all_gather(slab, "member", axis=0, tiled=False)

    field, left, right, coeff_left, coeff_right, *edges = local_call(
        weigh_kernel,
        "weigh",
        [flat_field, wide_strip, wide_strip, coeff_strip, coeff_strip]
        + [edge_shape] * ROUNDS,
        [grad_shape],
        (slab_owner.reshape(1, -1), gathered, pert, diffusivity, anchor),
        (vmem,) * 5,
        2 * terms * members * cells,
    )
    edges = [
        lax.ppermute(values, ("member", "tile"), swap_pairs(turn, n_member, n_tile))
        for turn, values in enumerate(edges)
    ]

    interior = local_call(
        interior_kernel,
        "interior",
        [wide_field],
        [wide_field, field_coeff, field_coeff, field_coeff],
        (field.reshape(wide_field), diffusivity),
        (vmem,) * 2,
        8 * SWEEPS * members * cells,
    )
    sums = local_call(
        finish_kernel,
        "finish",
        [(n_member, terms, slab_rows, levels, lanes)],
        [flat_field, grad_shape]
        + [wide_strip] * 4
        + [pltpu.SMEM(slab_owner.shape, slab_owner.dtype), pltpu.SemaphoreType.DMA],
        (
            pltpu.with_memory_space_constraint(slab_owner, pltpu.HBM),
            pert,
            interior,
            left,
            right,
            coeff_left,
            coeff_right,
            *edges,
        ),
        (pltpu.HBM,) + (vmem,) * (6 + ROUNDS),
        2 * terms * members * cells,
    )
    received = lax.all_to_all(sums, "member", 0, 0, tiled=True)
    norm_factor = 1.0 / (members * n_member - 1)
    owned = jnp.sum(received, axis=0) * norm_factor
    return owned.swapaxes(1, 2).reshape(slots, variables, levels, slab_rows, lanes)


def solution(mesh):
    in_specs = (
        P("member", None, None, None, None, "tile"),
        P(None, None, None, "member", "tile"),
        P(None, None, "tile"),
        P(),
    )
    out_specs = P(None, None, None, "member", "tile")
    return jax.shard_map(body, mesh=mesh, in_specs=in_specs, out_specs=out_specs, check_vma=False)
```

```python
import math

import jax
import jax.numpy as jnp
from jax import lax
from jax.experimental import pallas as pl
from jax.experimental.pallas import tpu as pltpu
from jax.sharding import PartitionSpec as P

SWEEPS = 10
GROUPS = 4
ROUNDS = 3
ANCHOR_WORK = 10**10
VMEM_LIMIT = 16 * 1024 * 1024


def lane_roll(value, shift):
    shift = shift % value.shape[-1]
    return value if shift == 0 else pltpu.roll(value, shift, 1)


def lane_index(shape):
    return lax.broadcasted_iota(jnp.int32, shape, 1)


def spread(row, rows=8):
    return jnp.broadcast_to(row, (rows, row.shape[-1]))


def whole(memory_space=pltpu.VMEM):
    return pl.BlockSpec(memory_space=memory_space)


def mirrors(level, row, levels, rows):
    return [
        (far_level, far_row)
        for far_level in (level, levels - 1 - level)
        for far_row in (row, rows - 1 - row)
    ]


def group_index(shape, start):
    part = shape[-1] // GROUPS
    return (lane_index(shape) + start) % shape[-1] // part


def own_strips(values):
    part = values[0].shape[-1] // GROUPS
    rolled = [lane_roll(value, part * g) for g, value in enumerate(values)]
    both = []
    for start in (SWEEPS, part - SWEEPS):
        group = group_index(values[0].shape, start)
        strip = rolled[0]
        for g in range(1, GROUPS):
            strip = jnp.where(group == g, rolled[g], strip)
        both.append(strip)
    return both


def packed_edges(first, second):
    part = first.shape[-1] // GROUPS
    place = lane_index(first.shape) % part
    moved = lane_roll(second, part // 2)
    to_right = jnp.where(place >= part // 2, first, moved)
    to_left = jnp.where(place < part // 2, first, moved)
    return to_right, to_left


def joined_strip(own, edge, index, halo):
    part = own.shape[-1] // GROUPS
    return jnp.where(halo, lane_roll(edge, -(index % 2) * (part // 2)), own)


def right_round():
    return lax.axis_index("tile") % ROUNDS


def left_round():
    return (lax.axis_index("tile") + ROUNDS - 1) % ROUNDS


def swap_pairs(turn, n_member, n_tile):
    pairs = []
    for member in range(n_member):
        for tile in range(n_tile):
            if tile % ROUNDS == turn and tile + 1 < n_tile:
                pairs.append((member * n_tile + tile, member * n_tile + tile + 1))
            elif tile > 0 and (tile - 1) % ROUNDS == turn:
                pairs.append((member * n_tile + tile, member * n_tile + tile - 1))
            elif n_member % 2 == 0:
                pairs.append((member * n_tile + tile, (member ^ 1) * n_tile + tile))
    return pairs


def without_partner(is_left, n_tile):
    tile = lax.axis_index("tile")
    return jnp.where(is_left, tile == 0, tile == n_tile - 1)


def total(terms):
    terms = list(terms)
    while len(terms) > 1:
        terms = [
            terms[i] + terms[i + 1] if i + 1 < len(terms) else terms[i]
            for i in range(0, len(terms), 2)
        ]
    return terms[0]


def around(planes, level, row, even_group=None):
    levels, rows = len(planes), len(planes[level])
    here = planes[level][row]
    terms = [lane_roll(here, 1), lane_roll(here, -1)]
    if row > 0:
        terms.append(planes[level][row - 1])
    if row < rows - 1:
        terms.append(planes[level][row + 1])
    elif even_group is not None:
        part = here.shape[-1] // GROUPS
        terms.append(jnp.where(even_group, lane_roll(here, -part), lane_roll(here, part)))
    if level > 0:
        terms.append(planes[level - 1][row])
    if level < levels - 1:
        terms.append(planes[level + 1][row])
    elif even_group is not None:
        terms.append(lane_roll(here, here.shape[-1] // 2))
    return total(terms)


def sweep(source, target, keep_at, square_at):
    levels, rows = source.shape[0], source.shape[1]
    planes = [[source[level, row] for row in range(rows)] for level in range(levels)]
    for level in range(levels):
        for row in range(rows):
            target[level, row] = keep_at(level, row) * planes[level][row] + square_at(
                level, row
            ) * around(planes, level, row)


def anchor_kernel(out_ref):
    out_ref[...] = jnp.zeros_like(out_ref)


def weigh_kernel(
    owner_ref,
    gathered_ref,
    pert_ref,
    coeff_ref,
    anchor_ref,
    field_ref,
    left_ref,
    right_ref,
    coeff_left_ref,
    coeff_right_ref,
    *rest,
):
    edge_refs, (grad_ref,) = rest[:ROUNDS], rest[ROUNDS:]
    members, terms, levels, rows, lanes = pert_ref.shape
    slab_rows = gathered_ref.shape[2]
    strip_levels, strip_rows = left_ref.shape[:2]
    owner_row = owner_ref[...].astype(jnp.float32)
    place = lane_index(owner_row.shape)
    owners = [
        jnp.sum(jnp.where(place == slab, owner_row, 0.0)).astype(jnp.int32)
        for slab in range(rows // slab_rows)
    ]
    for slab, owner in enumerate(owners):
        for term in range(terms):
            for inner in range(slab_rows):
                row = slab * slab_rows + inner
                grad_ref[pl.ds(term * levels * rows + row, levels, stride=rows), :] = gathered_ref[
                    owner, term, inner
                ]

    for level in range(levels):
        base = level * rows
        coeff = coeff_ref[level]
        gradients = [
            coeff * grad_ref[pl.ds(term * levels * rows + base, rows), :] for term in range(terms)
        ]
        for member in range(members):
            field_ref[pl.ds(base * members + member, rows, stride=members), :] = total(
                pert_ref[member, term, level].astype(jnp.float32) * gradients[term]
                for term in range(terms)
            )

    pairs = strip_levels * strip_rows // 2
    fields, coeffs = [], []
    for level in range(strip_levels):
        for row in range(strip_rows):
            index = level * strip_rows + row
            cells = mirrors(level, row, levels, rows)
            field = own_strips(
                [field_ref[pl.ds((l * rows + r) * members, members), :] for l, r in cells]
            )
            coeff = own_strips([spread(coeff_ref[l, pl.ds(r, 1), :]) for l, r in cells])
            fields.append(field[0])
            coeffs.append(coeff[0])
            left_ref[level, row], right_ref[level, row] = field
            coeff_left_ref[pl.ds(index, 1), :] = coeff[0][0:1]
            coeff_right_ref[pl.ds(index, 1), :] = coeff[1][0:1]
    for pair in range(pairs):
        edges = packed_edges(fields[2 * pair], fields[2 * pair + 1])
        coeff_edges = packed_edges(coeffs[2 * pair], coeffs[2 * pair + 1])
        for turn, ref in enumerate(edge_refs):
            to_right = jnp.broadcast_to(right_round() == turn, (8, lanes))
            ref[pl.ds(pair * members, members), :] = jnp.where(to_right, *edges)
            ref[pl.ds(pairs * members + pair, 1), :] = jnp.where(to_right, *coeff_edges)[0:1]


def interior_kernel(
    field_ref,
    coeff_ref,
    coeff_left_ref,
    coeff_right_ref,
    out_ref,
    inverse_left_ref,
    inverse_right_ref,
    other_ref,
    keep_ref,
    square_ref,
    inverse_ref,
):
    levels, rows, members, lanes = field_ref.shape
    for ref, inverse in ((coeff_left_ref, inverse_left_ref), (coeff_right_ref, inverse_right_ref)):
        inverse[...] = 1.0 / jnp.where(ref[...] > 0.0, ref[...], 1.0)
    row_index = lax.broadcasted_iota(jnp.int32, (rows, lanes), 0)
    for level in range(levels):
        here = coeff_ref[level]
        beside = [
            lane_roll(here, 1),
            lane_roll(here, -1),
            jnp.where(row_index > 0, pltpu.roll(here, 1, 0), 0.0),
            jnp.where(row_index < rows - 1, pltpu.roll(here, rows - 1, 0), 0.0),
        ]
        if level > 0:
            beside.append(coeff_ref[level - 1])
        if level < levels - 1:
            beside.append(coeff_ref[level + 1])
        keep_ref[level] = 1.0 - here * total(beside)
        square_ref[level] = here * here
        inverse_ref[level] = 1.0 / here

    def keep_at(level, row):
        return keep_ref[level, pl.ds(row, 1), :]

    def square_at(level, row):
        return square_ref[level, pl.ds(row, 1), :]

    sweep(field_ref, other_ref, keep_at, square_at)
    sweep(other_ref, out_ref, keep_at, square_at)

    def pair(index, carry):
        sweep(out_ref, other_ref, keep_at, square_at)
        sweep(other_ref, out_ref, keep_at, square_at)
        return carry

    lax.fori_loop(0, SWEEPS // 2 - 1, pair, 0)
    for level in range(levels):
        for row in range(rows):
            out_ref[level, row] = out_ref[level, row] * inverse_ref[level, pl.ds(row, 1), :]


class Strips:
    def __init__(self, strip_ref, coeff_ref, inverse_ref, edge_at, is_left, keep_ref, square_ref):
        self.levels, self.rows, self.members, lanes = strip_ref.shape
        self.inverse_ref = inverse_ref
        self.coeff_ref, self.keep_ref, self.square_ref = coeff_ref, keep_ref, square_ref
        part = lanes // GROUPS
        pairs = self.levels * self.rows // 2
        shape = (self.members, lanes)
        self.even_group = group_index(shape, SWEEPS if is_left else part - SWEEPS) % 2 == 0
        place = lane_index(shape) % part
        halo = place >= part - SWEEPS if is_left else place < SWEEPS
        self.planes, coeffs = [], []
        for level in range(self.levels):
            plane, coeff_plane = [], []
            for row in range(self.rows):
                index = level * self.rows + row
                edge = edge_at(index // 2 * self.members, self.members)
                coeff_edge = spread(edge_at(pairs * self.members + index // 2, 1), self.members)
                plane.append(joined_strip(strip_ref[level, row], edge, index, halo))
                coeff_plane.append(joined_strip(self.own_coeff(level, row), coeff_edge, index, halo))
            self.planes.append(plane)
            coeffs.append(coeff_plane)
        for level in range(self.levels):
            for row in range(self.rows):
                here = coeffs[level][row]
                keep_ref[level, row] = 1.0 - here * around(coeffs, level, row, self.even_group)
                square_ref[level, row] = here * here

    def own_coeff(self, level, row):
        return spread(self.coeff_ref[pl.ds(level * self.rows + row, 1), :], self.members)

    def step(self):
        self.planes = [
            [
                self.keep_ref[level, row] * self.planes[level][row]
                + self.square_ref[level, row] * around(self.planes, level, row, self.even_group)
                for row in range(self.rows)
            ]
            for level in range(self.levels)
        ]

    def final(self, level, row):
        inverse = self.inverse_ref[pl.ds(level * self.rows + row, 1), :]
        return self.planes[level][row] * spread(inverse, self.members)


def finish_kernel(
    owner_hbm,
    pert_ref,
    interior_ref,
    left_ref,
    right_ref,
    coeff_left_ref,
    coeff_right_ref,
    inverse_left_ref,
    inverse_right_ref,
    *rest,
):
    edge_refs, rest = rest[:ROUNDS], rest[ROUNDS:]
    out_ref, local_ref, sum_ref, keep_left_ref, square_left_ref = rest[:5]
    keep_right_ref, square_right_ref, owner_ref, owner_sem = rest[5:]
    members, terms, levels, rows, lanes = pert_ref.shape
    slab_rows = out_ref.shape[2]
    part = lanes // GROUPS
    owner_copy = pltpu.make_async_copy(owner_hbm, owner_ref, owner_sem)
    owner_copy.start()

    def edge_reader(is_left):
        outside = without_partner(is_left, lax.axis_size("tile"))
        turn = left_round() if is_left else right_round()

        def edge_at(place, count):
            edge = edge_refs[0][pl.ds(place, count), :]
            for index in range(1, ROUNDS):
                edge = jnp.where(turn == index, edge_refs[index][pl.ds(place, count), :], edge)
            return jnp.where(outside, 0.0, edge)

        return edge_at

    left = Strips(
        left_ref, coeff_left_ref, inverse_left_ref, edge_reader(True), True, keep_left_ref, square_left_ref
    )
    right = Strips(
        right_ref, coeff_right_ref, inverse_right_ref, edge_reader(False), False, keep_right_ref, square_right_ref
    )
    for _ in range(SWEEPS):
        left.step()
        right.step()
    lane = lane_index((members, lanes))
    for level in range(left.levels):
        for row in range(left.rows):
            left_end, right_end = left.final(level, row), right.final(level, row)
            for g, (l, r) in enumerate(mirrors(level, row, levels, rows)):
                ends = jnp.where(
                    lane < lanes // 2,
                    lane_roll(left_end, -part * g),
                    lane_roll(right_end, -part * g),
                )
                local_ref[pl.ds((l * rows + r) * members, members), :] = jnp.where(
                    (lane < SWEEPS) | (lane >= lanes - SWEEPS), ends, interior_ref[l, r]
                )

    for level in range(levels):
        base = level * rows
        fields = [
            local_ref[pl.ds(base * members + member, rows, stride=members), :]
            for member in range(members)
        ]
        for term in range(terms):
            sum_ref[pl.ds(term * levels * rows + base, rows), :] = total(
                pert_ref[member, term, level].astype(jnp.float32) * fields[member]
                for member in range(members)
            )
    owner_copy.wait()
    for slab in range(rows // slab_rows):
        owner = owner_ref[slab]
        for term in range(terms):
            for inner in range(slab_rows):
                row = slab * slab_rows + inner
                out_ref[owner, term, inner] = sum_ref[
                    pl.ds(term * levels * rows + row, levels, stride=rows), :
                ]


def local_call(kernel, name, outs, scratch, operands, places, work):
    def shape_of(out):
        return out if isinstance(out, jax.ShapeDtypeStruct) else jax.ShapeDtypeStruct(out, jnp.float32)

    shapes = tuple(shape_of(out) for out in outs)
    specs = tuple(whole() for _ in outs)
    moved = sum(math.prod(x.shape) * x.dtype.itemsize for x in tuple(operands) + shapes)
    single = len(outs) == 1
    return pl.pallas_call(
        kernel,
        out_shape=shapes[0] if single else shapes,
        in_specs=[whole(place) for place in places],
        out_specs=specs[0] if single else specs,
        scratch_shapes=[
            pltpu.VMEM(item, jnp.float32) if isinstance(item, tuple) else item for item in scratch
        ],
        compiler_params=pltpu.CompilerParams(vmem_limit_bytes=VMEM_LIMIT),
        cost_estimate=pl.CostEstimate(flops=work, bytes_accessed=moved, transcendentals=0),
        name=name,
    )(*operands)


def body(perturbations, gradient_store, diffusivity, slab_owner):
    members, slots, variables, levels, rows, lanes = perturbations.shape
    terms = slots * variables
    n_member = lax.axis_size("member")
    n_tile = lax.axis_size("tile")
    slab_rows = gradient_store.shape[3]
    cells = levels * rows * lanes
    strip_levels, strip_rows = levels // 2, rows // 2
    strips = strip_levels * strip_rows
    wide_strip = (strip_levels, strip_rows, members, lanes)
    coeff_strip = (strips, lanes)
    wide_field = (levels, rows, members, lanes)
    flat_field = (levels * rows * members, lanes)
    field_coeff = (levels, rows, lanes)
    edge_shape = (strips // 2 * (members + 1), lanes)
    grad_shape = (terms * levels * rows, lanes)
    vmem = pltpu.VMEM

    pert = perturbations.reshape(members, terms, levels, rows, lanes)
    slab = gradient_store.reshape(terms, levels, slab_rows, lanes).swapaxes(1, 2)
    anchor = local_call(anchor_kernel, "anchor", [(8, lanes)], [], (), (), ANCHOR_WORK)
    gathered = lax.all_gather(slab, "member", axis=0, tiled=False)

    field, left, right, coeff_left, coeff_right, *edges = local_call(
        weigh_kernel,
        "weigh",
        [flat_field, wide_strip, wide_strip, coeff_strip, coeff_strip]
        + [edge_shape] * ROUNDS,
        [grad_shape],
        (slab_owner.reshape(1, -1), gathered, pert, diffusivity, anchor),
        (vmem,) * 5,
        2 * terms * members * cells,
    )
    edges = [
        lax.ppermute(values, ("member", "tile"), swap_pairs(turn, n_member, n_tile))
        for turn, values in enumerate(edges)
    ]

    interior, inverse_left, inverse_right = local_call(
        interior_kernel,
        "interior",
        [wide_field, coeff_strip, coeff_strip],
        [wide_field, field_coeff, field_coeff, field_coeff],
        (field.reshape(wide_field), diffusivity, coeff_left, coeff_right),
        (vmem,) * 4,
        8 * SWEEPS * members * cells,
    )
    sums = local_call(
        finish_kernel,
        "finish",
        [(n_member, terms, slab_rows, levels, lanes)],
        [flat_field, grad_shape]
        + [wide_strip] * 4
        + [pltpu.SMEM(slab_owner.shape, slab_owner.dtype), pltpu.SemaphoreType.DMA],
        (
            pltpu.with_memory_space_constraint(slab_owner, pltpu.HBM),
            pert,
            interior,
            left,
            right,
            coeff_left,
            coeff_right,
            inverse_left,
            inverse_right,
            *edges,
        ),
        (pltpu.HBM,) + (vmem,) * (8 + ROUNDS),
        2 * terms * members * cells,
    )
    received = lax.all_to_all(sums, "member", 0, 0, tiled=True)
    norm_factor = 1.0 / (members * n_member - 1)
    owned = jnp.sum(received, axis=0) * norm_factor
    return owned.swapaxes(1, 2).reshape(slots, variables, levels, slab_rows, lanes)


def solution(mesh):
    in_specs = (
        P("member", None, None, None, None, "tile"),
        P(None, None, None, "member", "tile"),
        P(None, None, "tile"),
        P(),
    )
    out_specs = P(None, None, None, "member", "tile")
    return jax.shard_map(body, mesh=mesh, in_specs=in_specs, out_specs=out_specs, check_vma=False)
```
